128 devices in a mesh: section: 4 (over x), dp: 32 (over y, z, core).
Axes of the slice: x: 4, y: 4, z: 4, core: 2. Of those that a mesh axis runs over, the one named last changes fastest.
Arguments:
- bottom_stack_feed: bfloat16 [64, 64, 1024], P('dp'), may hold values from -6 to 6
- loss_sensitivity: bfloat16 [64, 64, 1024], P('dp'), may hold values from -6 to 6
- resumes_segment: int32 [64], P('dp'), may hold values 0 or 1
- mixing_coefficients: float32 [4, 9, 1024], P('section'), may hold values from -0.9 to 1.45, as said below
- fading_log: float32 [4, 1024], P('section'), may hold values from -6 to -3
- feature_boost: float32 [4, 1024], P('section'), may hold values from -1 to 1
- attention_maps: bfloat16 [4, 3, 1024, 1024], P('section'), may hold values from -0.1875 to 0.1875
- emission_coefficients: bfloat16 [4, 1024, 1024], P('section'), may hold values from -0.75 to 0.75
- feature_addressing: bfloat16 [4, 1024, 4096], P('section'), may hold values from -0.1875 to 0.1875
- feature_payload: bfloat16 [4, 4096, 1024], P('section'), may hold values from -0.09375 to 0.09375
- feature_receptance: bfloat16 [4, 1024, 1024], P('section'), may hold values from -0.1875 to 0.1875
- dividend_memory: float32 [4, 64, 1024], P('section', 'dp'), may hold values from -6 to 6
- divisor_memory: float32 [4, 64, 1024], P('section', 'dp'), may hold values from 0.5 to 4
- memory_power_shift: float32 [4, 64, 1024], P('section', 'dp'), may hold values from -1 to 1
- prior_normed_lines: bfloat16 [4, 2, 64, 1024], P('section', None, 'dp'), may hold values from -6 to 6
Outputs:
- layer_outputs: bfloat16 [4, 64, 64, 1024], P('section', 'dp')
- input_grads: bfloat16 [4, 64, 64, 1024], P('section', 'dp')
- vector_grads: float32 [4, 9, 1024], P('section', None, 'dp')
- decay_grads: float32 [4, 1024], P('section', 'dp')
- bonus_grads: float32 [4, 1024], P('section', 'dp')
- projection_grads: float32 [4, 3, 1024, 1024], P('section', None, 'dp')
- out_weight_grads: float32 [4, 1024, 1024], P('section', 'dp')
- ffn_key_grads: float32 [4, 1024, 4096], P('section', 'dp')
- ffn_value_grads: float32 [4, 4096, 1024], P('section', 'dp')
- ffn_gate_grads: float32 [4, 1024, 1024], P('section', 'dp')
- state_num_grads: float32 [4, 64, 1024], P('section', 'dp')
- state_den_grads: float32 [4, 64, 1024], P('section', 'dp')
- state_max_grads: float32 [4, 64, 1024], P('section', 'dp')
- earlier_row_grads: float32 [4, 2, 64, 1024], P('section', None, 'dp')
The draws below stay inside these ranges and needn't reach their ends.
Inputs may be any that keep to these rules, and one draw needn't show every extreme that they name: `resumes_segment`: 1 where a sequence continues an earlier segment whose states and last normed rows are given, 0 where it starts afresh. `mixing_coefficients`: rows 0 and 5 are gains near 1, rows 1 and 6 biases, rows 2, 3, 4, 7 and 8 mixing weights within 0.05 to 0.95.
All inputs are finite; a program needn't handle non-finite values. No bound on the sum of `resumes_segment` on one device may be relied on, other than what follows from the above.
Results may differ from the reference program's by a relative error of at most 0.038.
Values may be sent and summed in bfloat16 or wider, within the bound.
No kernel may reach another device: no remote copies, remote signals or barrier semaphores. Data moves between devices by JAX's collectives and lax.ppermute only.
A program may use at most 256 MiB of HBM per device.

```python
import math
import jax
import jax.numpy as jnp
from jax import lax

HIDDEN_SIZE = 1024
FF = 4096
LEN = 64
DEPTH_TOTAL = 4
SEQS = 64


def draw_mixing_coefficients(key, part):
    key = jax.random.fold_in(key, 11)
    normal_key, spread_key = jax.random.split(key, 2)
    normal = jnp.clip(jax.random.normal(normal_key, (DEPTH_TOTAL, 9, HIDDEN_SIZE), jnp.float32), -3.0, 3.0)
    spread = jax.random.uniform(spread_key, (DEPTH_TOTAL, 9, HIDDEN_SIZE), jnp.float32, 0.05, 0.95)
    row_index = lax.broadcasted_iota(jnp.int32, (DEPTH_TOTAL, 9, HIDDEN_SIZE), 1)
    gains = (row_index == 0) | (row_index == 5)
    offsets = (row_index == 1) | (row_index == 6)
    return jnp.where(gains, 1.0 + 0.15 * normal, jnp.where(offsets, 0.3 * normal, spread))


def set_ends(entries, key, smallest, top_value):
    shape = entries.shape
    place = [jax.random.randint(jax.random.fold_in(key, axis), (), 0, shape[axis]) for axis in range(len(shape))]
    entries = entries.at[tuple(place)].set(smallest)
    longest = shape.index(max(shape))
    place[longest] = (place[longest] + 1) % shape[longest]
    return entries.at[tuple(place)].set(top_value)


def shard_levels(stream_key, dims, cuts, least, top_value):
    def one(position, parts):
        steps = jax.random.uniform(jax.random.fold_in(jax.random.fold_in(stream_key, 6), position), (parts,), jnp.float32, least / len(cuts), top_value / len(cuts))
        return jnp.repeat(jnp.exp(steps), dims[position] // parts).reshape((-1,) + (1,) * (len(dims) - position - 1))

    loudness = one(*cuts[0])
    for cut in cuts[1:]:
        loudness = loudness * one(*cut)
    return loudness


def gaussian(own_key, dims, width, bound, shards=(), kind=jnp.bfloat16):
    array = jax.random.normal(own_key, dims, jnp.float32) * width
    if len(shards) > 0:
        array = shard_levels(own_key, dims, shards, -0.22, 0.18) * array
    return jnp.clip(array, min=-bound, max=bound).astype(kind)


def setup_inputs(seed: int = 0) -> dict:
    seeds = jax.random.split(jax.random.key(seed), 16)
    return {
        "bottom_stack_feed": gaussian(seeds[0], (SEQS, LEN, HIDDEN_SIZE), 1.0, 6.0, ((0, 32),)),
        "loss_sensitivity": gaussian(seeds[1], (SEQS, LEN, HIDDEN_SIZE), 1.0, 6.0, ((0, 32),)),
        "resumes_segment": set_ends((jax.random.randint(seeds[2], (SEQS,), 0, 4) < 3).astype(jnp.int32), jax.random.fold_in(seeds[2], 1), 0, 1),
        "mixing_coefficients": draw_mixing_coefficients(jax.random.fold_in(seeds[15], 71), 0),
        "fading_log": jnp.clip(-6.0 + 3.0 * jax.random.uniform(seeds[4], (DEPTH_TOTAL, HIDDEN_SIZE), jnp.float32) ** shard_levels(seeds[4], (DEPTH_TOTAL, HIDDEN_SIZE), ((0, 4),), -0.2, 0.2), -6.0, -3.0),
        "feature_boost": jnp.clip(jax.random.uniform(seeds[5], (DEPTH_TOTAL, HIDDEN_SIZE), jnp.float32, -1.0, 1.0) * shard_levels(seeds[5], (DEPTH_TOTAL, HIDDEN_SIZE), ((0, 4),), -0.4, 0.0), -1.0, 1.0),
        "attention_maps": gaussian(seeds[6], (DEPTH_TOTAL, 3, HIDDEN_SIZE, HIDDEN_SIZE), HIDDEN_SIZE ** -0.5, 0.1875, ((0, 4),)),
        "emission_coefficients": gaussian(seeds[7], (DEPTH_TOTAL, HIDDEN_SIZE, HIDDEN_SIZE), (max(HIDDEN_SIZE // 16, 4)) ** -0.5, 0.75, ((0, 4),)),
        "feature_addressing": gaussian(seeds[8], (DEPTH_TOTAL, HIDDEN_SIZE, FF), HIDDEN_SIZE ** -0.5, 0.1875, ((0, 4),)),
        "feature_payload": gaussian(seeds[9], (DEPTH_TOTAL, FF, HIDDEN_SIZE), FF ** -0.5, 0.09375, ((0, 4),)),
        "feature_receptance": gaussian(seeds[10], (DEPTH_TOTAL, HIDDEN_SIZE, HIDDEN_SIZE), HIDDEN_SIZE ** -0.5, 0.1875, ((0, 4),)),
        "dividend_memory": gaussian(seeds[11], (DEPTH_TOTAL, SEQS, HIDDEN_SIZE), 1.0, 6.0, ((0, 4), (1, 32)), jnp.float32),
        "divisor_memory": jnp.clip(jnp.exp(math.log(4.0) - 2.0794415 * jax.random.uniform(seeds[12], (DEPTH_TOTAL, SEQS, HIDDEN_SIZE), jnp.float32) ** shard_levels(seeds[12], (DEPTH_TOTAL, SEQS, HIDDEN_SIZE), ((0, 4), (1, 32)), -0.2, 0.2)), 0.5, 4.0),
        "memory_power_shift": jnp.clip(jax.random.uniform(seeds[13], (DEPTH_TOTAL, SEQS, HIDDEN_SIZE), jnp.float32, -1.0, 1.0) * shard_levels(seeds[13], (DEPTH_TOTAL, SEQS, HIDDEN_SIZE), ((0, 4), (1, 32)), -0.4, 0.0), -1.0, 1.0),
        "prior_normed_lines": gaussian(seeds[14], (DEPTH_TOTAL, 2, SEQS, HIDDEN_SIZE), 1.0, 6.0, ((0, 4), (2, 32))),
    }


FRESH = -1e+30
HIGH = lax.Precision.HIGHEST

@jax.custom_vjp
def low(v):
    return lax.optimization_barrier(v.astype(jnp.bfloat16)).astype(jnp.float32)

@jax.custom_vjp
def low_back(v):
    return v

def low_keep(v):
    return (low(v), None)

def low_pass(kept, grad):
    return (grad,)

def back_keep(v):
    return (v, None)

def back_low(kept, grad):
    return (low(grad),)
low.defvjp(low_keep, low_pass)
low_back.defvjp(back_keep, back_low)

def product(rows, weight):
    flat = rows.reshape(-1, rows.shape[-1])
    result = jnp.dot(flat, weight, precision=HIGH, preferred_element_type=jnp.float32)
    return result.reshape(rows.shape[:-1] + (weight.shape[-1],))

def norm_rows(rows, gain, offset):
    center = lax.optimization_barrier(jnp.mean(rows, axis=-1, keepdims=True))
    centered = rows - center
    variance = lax.optimization_barrier(jnp.mean(centered * centered, axis=-1, keepdims=True))
    return centered * lax.rsqrt(variance + 1e-05) * gain + offset

def shifted_mix(normed, first_row, mixing):
    shifted = jnp.concatenate([first_row[:, None, :], normed[:, :-1, :]], axis=1)
    return normed * mixing + shifted * (1.0 - mixing)

def scan_advance(addressing_lines, payload_lines, fading_factor, position_boost, starting_memory):

    def advance(carry, pieces):
        dividend_amount, accumulated_coefficient, shift_amount = carry
        addressing_now, value_now = pieces
        boosted_score = position_boost + addressing_now
        uppermost = jnp.maximum(shift_amount, boosted_score)
        old_part = jnp.exp(shift_amount - uppermost)
        fresh_portion = jnp.exp(boosted_score - uppermost)
        result = (old_part * dividend_amount + fresh_portion * value_now) / (old_part * accumulated_coefficient + fresh_portion)
        faded = shift_amount - fading_factor
        top_next = jnp.maximum(faded, addressing_now)
        old_next = jnp.exp(faded - top_next)
        new_next = jnp.exp(addressing_now - top_next)
        carry_next = (old_next * dividend_amount + new_next * value_now, old_next * accumulated_coefficient + new_next, top_next)
        return (carry_next, result)
    _, results = lax.scan(jax.checkpoint(advance), starting_memory, (jnp.swapaxes(addressing_lines, 0, 1), jnp.swapaxes(payload_lines, 0, 1)))
    return jnp.swapaxes(results, 0, 1)

def depth_position(element_amount, direction_array, fading_factor_log, position_boost, affine_map, emission_map, addressing_map, payload_map, receptance_map, dividend_amount, accumulated_coefficient, shift_amount, position_before, toggle_marker):
    residual = low_back(element_amount)
    normed = norm_rows(residual, direction_array[0], direction_array[1])
    first_row = position_before[0] * toggle_marker
    mix_key = low(shifted_mix(normed, first_row, direction_array[2]))
    mix_value = low(shifted_mix(normed, first_row, direction_array[3]))
    mix_gate = low(shifted_mix(normed, first_row, direction_array[4]))
    addressing_lines = low_back(product(mix_key, affine_map[0]))
    payload_lines = low_back(product(mix_value, affine_map[1]))
    gate_rows = low_back(product(mix_gate, affine_map[2]))
    starting_memory = (dividend_amount * toggle_marker, accumulated_coefficient * toggle_marker, jnp.where(toggle_marker > 0.0, shift_amount, FRESH))
    blended_lines = scan_advance(addressing_lines, payload_lines, jnp.exp(fading_factor_log), position_boost, starting_memory)
    recurrent_core = low(jax.nn.sigmoid(gate_rows) * blended_lines)
    middle = residual + low_back(product(recurrent_core, emission_map))
    normed_two = norm_rows(middle, direction_array[5], direction_array[6])
    second_row = position_before[1] * toggle_marker
    mix_hidden = low(shifted_mix(normed_two, second_row, direction_array[7]))
    mix_outer = low(shifted_mix(normed_two, second_row, direction_array[8]))
    hidden_pre = low_back(product(mix_hidden, addressing_map))
    hidden = low(jnp.square(jax.nn.relu(hidden_pre)))
    channel = low_back(product(hidden, payload_map))
    outer_pre = low_back(product(mix_outer, receptance_map))
    return low(middle + jax.nn.sigmoid(outer_pre) * channel)

def reference(bottom_stack_feed, loss_sensitivity, resumes_segment, mixing_coefficients, fading_log, feature_boost, attention_maps, emission_coefficients, feature_addressing, feature_payload, feature_receptance, dividend_memory, divisor_memory, memory_power_shift, prior_normed_lines):
    toggle_marker = resumes_segment.astype(jnp.float32)[:, None]
    start_rows = bottom_stack_feed.astype(jnp.float32)
    random_directions = jnp.zeros((DEPTH_TOTAL,) + start_rows.shape, jnp.float32)

    def tower_depths(random_directions, mixing_coefficients, fading_log, feature_boost, attention_maps, emission_coefficients, feature_addressing, feature_payload, feature_receptance, dividend_memory, divisor_memory, memory_power_shift, prior_normed_lines):
        position_now = start_rows
        results = []
        for position_number in range(DEPTH_TOTAL):
            position_now = depth_position(position_now + random_directions[position_number], mixing_coefficients[position_number], fading_log[position_number], feature_boost[position_number], attention_maps[position_number], emission_coefficients[position_number], feature_addressing[position_number], feature_payload[position_number], feature_receptance[position_number], dividend_memory[position_number], divisor_memory[position_number], memory_power_shift[position_number], prior_normed_lines[position_number], toggle_marker)
            results.append(position_now)
        return jnp.stack(results)
    emitted_lines, adjoint_sweep = jax.vjp(tower_depths, random_directions, mixing_coefficients, fading_log, feature_boost, attention_maps.astype(jnp.float32), emission_coefficients.astype(jnp.float32), feature_addressing.astype(jnp.float32), feature_payload.astype(jnp.float32), feature_receptance.astype(jnp.float32), dividend_memory, divisor_memory, memory_power_shift, prior_normed_lines.astype(jnp.float32))
    upstream = jnp.zeros_like(emitted_lines).at[DEPTH_TOTAL - 1].set(loss_sensitivity.astype(jnp.float32))
    grads = adjoint_sweep(upstream)
    return (emitted_lines.astype(jnp.bfloat16), grads[0].astype(jnp.bfloat16), grads[1], grads[2], grads[3], grads[4], grads[5], grads[6], grads[7], grads[8], grads[9], grads[10], grads[11], grads[12])
```

```python
import functools

import jax
import jax.numpy as jnp
from jax import lax
from jax.experimental import pallas as pl
from jax.experimental.pallas import tpu as pltpu
from jax.sharding import PartitionSpec as P

WIDTH = 1024
INNER = 4096
LENGTH = 64
SEQS = 2
ROWS = SEQS * LENGTH
GROUPS = WIDTH // 128
FRESH = -1e30
EPS = 1e-05
F32 = jnp.float32
BF16 = jnp.bfloat16

VM = pl.BlockSpec(memory_space=pltpu.VMEM)
HB = pl.BlockSpec(memory_space=pl.ANY)
SM = pl.BlockSpec(memory_space=pltpu.SMEM)
PARAMS = pltpu.CompilerParams(vmem_limit_bytes=18 * 1024 * 1024)

WEIGHTS = (
    ((3, WIDTH, WIDTH), BF16),
    ((WIDTH, WIDTH), BF16),
    ((WIDTH, INNER), BF16),
    ((INNER, WIDTH), BF16),
    ((WIDTH, WIDTH), BF16),
)
SAVED = (
    ((ROWS, WIDTH), BF16),
    ((ROWS, WIDTH), BF16),
    ((6, ROWS, WIDTH), BF16),
    ((ROWS, INNER), BF16),
    ((ROWS, INNER), BF16),
    ((5, ROWS, WIDTH), F32),
    ((8, ROWS * GROUPS, 128), F32),
)
GRADS = (
    ((ROWS, WIDTH), BF16),
    ((6, ROWS, WIDTH), BF16),
    ((ROWS, INNER), BF16),
    ((16, WIDTH), F32),
    ((3, SEQS, WIDTH), F32),
    ((2, SEQS, WIDTH), F32),
)


def dot(left, right):
    return jnp.dot(left, right, preferred_element_type=F32)


def against(grad, weight):
    return lax.dot_general(
        grad, weight, (((1,), (1,)), ((), ())), preferred_element_type=F32
    )


def row_index():
    return lax.broadcasted_iota(jnp.int32, (ROWS, WIDTH), 0)


def normed_rows(rows):
    center = jnp.mean(rows, axis=-1, keepdims=True)
    centered = rows - center
    variance = jnp.mean(centered * centered, axis=-1, keepdims=True)
    scale = lax.rsqrt(variance + EPS)
    return centered * scale, scale


def moved_down(normed, first):
    index = row_index()
    return jnp.where(
        index == 0,
        first[0],
        jnp.where(index == LENGTH, first[1], pltpu.roll(normed, 1, 0)),
    )


def moved_up(rows):
    index = row_index()
    return jnp.where(
        (index == LENGTH - 1) | (index == ROWS - 1),
        0.0,
        pltpu.roll(rows, ROWS - 1, 0),
    )


def first_rows(prior_ref, mix, marks):
    return [prior_ref[mix, s : s + 1, :].astype(F32) * marks[s] for s in range(SEQS)]


def to_tokens(ref, block, value):
    ref[pl.ds(block, ROWS, stride=GROUPS), :] = value


def from_tokens(ref, block):
    return ref[pl.ds(block, ROWS, stride=GROUPS), :]


def tile_of(ref, row, small):
    for g in range(GROUPS):
        small[g : g + 1, :] = ref[row : row + 1, g * 128 : (g + 1) * 128]
    return small[...]


def forward_body(
    marks, x_ref, vec_ref, fade_ref, boost_ref, num_ref, den_ref, lev_ref, prior_ref,
    weights, ready, out_ref, saved, scratch,
):
    wm, wo, wa, wp, wr = weights
    ent_ref, lay_ref, mix_ref, hid_ref, act_ref, wide_ref, scan_ref = saved
    sk, sv, sy, small = scratch
    x = x_ref[...]
    ent_ref[...] = x
    rows = x.astype(F32)
    unit, _ = normed_rows(rows)
    normed = unit * vec_ref[0:1, :] + vec_ref[1:2, :]
    below = moved_down(normed, first_rows(prior_ref, 0, marks))
    for j in range(3):
        v = vec_ref[2 + j : 3 + j, :]
        mix_ref[j] = (normed * v + below * (1.0 - v)).astype(BF16)
    ready(0)
    for target, j in ((sk, 0), (sv, 1)):
        for c in range(0, WIDTH, 256):
            part = dot(mix_ref[j], wm[j, :, c : c + 256])
            for h in range(2):
                to_tokens(target, c // 128 + h, part[:, h * 128 : (h + 1) * 128])
    wide_ref[0] = jax.nn.sigmoid(dot(mix_ref[2], wm[2]))

    rate = jnp.exp(tile_of(fade_ref, 0, small))
    boost = tile_of(boost_ref, 0, small)
    start = []
    for s in range(SEQS):
        level = tile_of(lev_ref, s, small)
        start.append(jnp.where(marks[s] > 0.0, level, FRESH))
        start.append(tile_of(num_ref, s, small) * marks[s])
        start.append(tile_of(den_ref, s, small) * marks[s])

    def token(t, carry):
        carry_next = []
        for s in range(SEQS):
            level, num, den = carry[3 * s : 3 * s + 3]
            at = pl.ds(pl.multiple_of((t + LENGTH * s) * GROUPS, GROUPS), GROUPS)
            key, value = sk[at, :], sv[at, :]
            boosted = boost + key
            decayed = jnp.exp(-jnp.abs(level - boosted))
            state_on_top = level > boosted
            old = jnp.where(state_on_top, 1.0, decayed)
            fresh = jnp.where(state_on_top, decayed, 1.0)
            inverse = 1.0 / (old * den + fresh)
            old = old * inverse
            fresh = fresh * inverse
            result = old * num + fresh * value
            faded = level - rate
            level = jnp.maximum(faded, key)
            decayed = jnp.exp(-jnp.abs(faded - key))
            state_on_top = faded > key
            keep = jnp.where(state_on_top, 1.0, decayed)
            new = jnp.where(state_on_top, decayed, 1.0)
            sy[at, :] = result
            scan_ref[0, at, :] = old
            scan_ref[1, at, :] = fresh
            scan_ref[2, at, :] = value - result
            scan_ref[3, at, :] = keep
            scan_ref[4, at, :] = new
            scan_ref[5, at, :] = num
            scan_ref[6, at, :] = den
            scan_ref[7, at, :] = value
            carry_next += [level, keep * num + new * value, keep * den + new]
        return tuple(carry_next)

    def tokens(block, carry):
        for j in range(8):
            carry = token(block * 8 + j, carry)
        return carry

    lax.fori_loop(0, LENGTH // 8, tokens, tuple(start))
    for g in range(GROUPS):
        at = slice(g * 128, (g + 1) * 128)
        gate = wide_ref[0, :, at]
        mixed = gate * from_tokens(sy, g)
        mix_ref[3, :, at] = mixed.astype(BF16)
        wide_ref[1, :, at] = mixed * (1.0 - gate)
    ready(1)
    wide_ref[2] = rows + dot(mix_ref[3], wo[...])
    unit, _ = normed_rows(wide_ref[2])
    normed = unit * vec_ref[5:6, :] + vec_ref[6:7, :]
    below = moved_down(normed, first_rows(prior_ref, 1, marks))
    for j in range(2):
        v = vec_ref[7 + j : 8 + j, :]
        mix_ref[4 + j] = (normed * v + below * (1.0 - v)).astype(BF16)
    ready(4)
    wide_ref[4] = jax.nn.sigmoid(dot(mix_ref[5], wr[...]))
    ready(2)

    @pl.loop(0, INNER // 512)
    def _(j):
        at = pl.ds(pl.multiple_of(j * 512, 512), 512)
        active = jnp.maximum(dot(mix_ref[4], wa[:, at]), 0.0)
        act_ref[:, at] = active.astype(BF16)
        hid_ref[:, at] = (active * active).astype(BF16)

    ready(3)

    @pl.loop(0, WIDTH // 256)
    def _(j):
        at = pl.ds(pl.multiple_of(j * 256, 256), 256)
        channel = dot(hid_ref[...], wp[:, at])
        wide_ref[3, :, at] = channel
        lay_ref[:, at] = (wide_ref[2, :, at] + wide_ref[4, :, at] * channel).astype(BF16)

    out_ref[...] = lay_ref[...]


N_SMALL = 8


def forward_first_kernel(flag, begins, x_ref, *refs):
    small_in = refs[: N_SMALL - 1]
    hbm = refs[N_SMALL - 1 : N_SMALL + 4]
    out_ref = refs[N_SMALL + 4]
    kept = refs[N_SMALL + 5 : N_SMALL + 10]
    saved = refs[N_SMALL + 10 : N_SMALL + 17]
    scratch = refs[N_SMALL + 17 : N_SMALL + 21]
    sem = refs[N_SMALL + 21]
    copies = [pltpu.make_async_copy(hbm[i], kept[i], sem.at[i]) for i in range(5)]
    for i in (0, 1, 4, 2, 3):
        copies[i].start()

    @pl.when(flag[0] == 1)
    def _():
        marks = [begins[s].astype(F32) for s in range(SEQS)]
        forward_body(
            marks, x_ref, *small_in, kept, lambda i: copies[i].wait(), out_ref, saved, scratch
        )

    @pl.when(flag[0] == 0)
    def _():
        for c in copies:
            c.wait()


def forward_kernel(flag, begins, x_ref, *refs):
    small_in = refs[: N_SMALL - 1]
    n = N_SMALL - 1 + 12
    out_ref = refs[n]
    kept = refs[n + 1 : n + 6]
    saved = refs[n + 6 : n + 13]
    scratch = refs[n + 13 :]

    @pl.when(flag[0] == 1)
    def _():
        marks = [begins[s].astype(F32) for s in range(SEQS)]
        forward_body(
            marks, x_ref, *small_in, kept, lambda i: None, out_ref, saved, scratch
        )


def norm_back(rows, gain, offset, first, parts, vec_out, prior_out, marks):
    unit, scale = normed_rows(rows)
    normed = unit * gain + offset
    change = normed - moved_down(normed, first)
    up, stay = None, None
    for grad, weight, place in parts:
        vec_out(place, jnp.sum(grad * change, axis=0, keepdims=True))
        kept = grad * weight
        passed = grad - kept
        stay = kept if stay is None else stay + kept
        up = passed if up is None else up + passed
    for s in range(SEQS):
        prior_out(s, up[s * LENGTH : s * LENGTH + 1, :] * marks[s])
    grad = stay + moved_up(up)
    return unit, scale, grad


def backward_kernel(first, flag, begins, dy_ref, *refs):
    vec_ref, fade_ref, prior_ref = refs[:3]
    n = 3 + 12 + (0 if first else 6)
    out_ref = refs[n]
    wm, wo, wa, wp, wr = refs[n + 1 : n + 6]
    ent_ref, lay_ref, mix_ref, hid_ref, act_ref, wide_ref, scan_ref = refs[n + 6 : n + 13]
    ing_ref, dys_ref, dhp_ref, vecg_ref, stg_ref, rowg_ref = refs[n + 13 : n + 19]
    sg, sdk, sdv, small, wide, wide_two, wide_three = refs[n + 19 :]

    def vec_out(place, value):
        vecg_ref[place : place + 1, :] = value

    @pl.when(flag[0] == 1)
    def _():
        marks = [begins[s].astype(F32) for s in range(SEQS)]
        dy = dy_ref[...].astype(F32)
        gate = wide_ref[4]
        through = dy * gate
        dys_ref[4] = through.astype(BF16)
        dys_ref[5] = (through * wide_ref[3] * (1.0 - gate)).astype(BF16)

        @pl.loop(0, INNER // 512)
        def _(j):
            at = pl.ds(pl.multiple_of(j * 512, 512), 512)
            part = against(dys_ref[4], wp[at, :])
            dhp_ref[:, at] = (2.0 * act_ref[:, at].astype(F32) * part).astype(BF16)

        @pl.loop(0, WIDTH // 256)
        def _(j):
            at = pl.ds(pl.multiple_of(j * 256, 256), 256)
            wide[:, at] = against(dhp_ref[...], wa[at, :])
            wide_two[:, at] = against(dys_ref[5], wr[at, :])

        def prior_two(s, value):
            rowg_ref[1, s : s + 1, :] = value

        gain = vec_ref[5:6, :]
        unit, scale, grad = norm_back(
            wide_ref[2], gain, vec_ref[6:7, :], first_rows(prior_ref, 1, marks),
            ((wide[...], vec_ref[7:8, :], 7), (wide_two[...], vec_ref[8:9, :], 8)),
            vec_out, prior_two, marks,
        )
        vec_out(5, jnp.sum(grad * unit, axis=0, keepdims=True))
        vec_out(6, jnp.sum(grad, axis=0, keepdims=True))
        grad = grad * gain
        mean = jnp.mean(grad, axis=-1, keepdims=True)
        along = jnp.mean(grad * unit, axis=-1, keepdims=True)
        middle = dy_ref[...].astype(F32) + scale * (grad - mean - unit * along)
        wide_three[...] = middle
        dys_ref[3] = middle.astype(BF16)
        for c in range(0, WIDTH, 256):
            part = against(dys_ref[3], wo[c : c + 256, :])
            at = slice(c, c + 256)
            dys_ref[2, :, at] = (part * wide_ref[1, :, at]).astype(BF16)
            part = part * wide_ref[0, :, at]
            for h in range(2):
                to_tokens(sg, c // 128 + h, part[:, h * 128 : (h + 1) * 128])

        zero = jnp.zeros((GROUPS, 128), F32)

        def token(t, carry):
            carry_next = []
            boosted, faded = carry[4], carry[5]
            for s in range(SEQS):
                dnum, dden = carry[2 * s : 2 * s + 2]
                at = pl.ds(pl.multiple_of((t + LENGTH * s) * GROUPS, GROUPS), GROUPS)
                g = sg[at, :]
                value = scan_ref[7, at, :]
                beyond = scan_ref[2, at, :]
                keep = scan_ref[3, at, :]
                new = scan_ref[4, at, :]
                from_old = scan_ref[0, at, :] * g
                from_new = scan_ref[1, at, :] * g
                direct = from_new * beyond
                boosted = boosted + direct
                sdv[at, :] = from_new + new * dnum
                sdk[at, :] = direct + new * (dnum * value + dden)
                faded = faded - keep * (dnum * scan_ref[5, at, :] + dden * scan_ref[6, at, :])
                carry_next += [
                    from_old + keep * dnum,
                    keep * dden - from_old * (value - beyond),
                ]
            return tuple(carry_next) + (boosted, faded)

        def tokens(block, carry):
            for j in range(8):
                carry = token(LENGTH - 1 - block * 8 - j, carry)
            return carry

        ends = lax.fori_loop(0, LENGTH // 8, tokens, (zero,) * 6)

        def spread(put, value):
            small[...] = value
            for g in range(GROUPS):
                put(slice(g * 128, (g + 1) * 128), small[g : g + 1, :])

        for s in range(SEQS):
            dnum, dden = ends[2 * s : 2 * s + 2]
            at = pl.ds(LENGTH * s * GROUPS, GROUPS)
            moved = dnum * scan_ref[5, at, :] + dden * scan_ref[6, at, :]
            for k, value in enumerate((dnum, dden, moved)):

                def put(cols, piece, k=k, s=s):
                    stg_ref[k, s : s + 1, cols] = piece

                spread(put, value * marks[s])

        def put_decay(cols, piece):
            vecg_ref[9:10, cols] = piece

        def put_boost(cols, piece):
            vecg_ref[10:11, cols] = piece

        spread(put_decay, ends[5])
        vecg_ref[9:10, :] = vecg_ref[9:10, :] * jnp.exp(fade_ref[0:1, :])
        spread(put_boost, ends[4])

        for g in range(GROUPS):
            at = slice(g * 128, (g + 1) * 128)
            dys_ref[0, :, at] = from_tokens(sdk, g).astype(BF16)
            dys_ref[1, :, at] = from_tokens(sdv, g).astype(BF16)

        rows = ent_ref[...].astype(F32)
        grads = [against(dys_ref[j], wm[j]) for j in range(3)]

        def prior_one(s, value):
            rowg_ref[0, s : s + 1, :] = value

        gain = vec_ref[0:1, :]
        unit, scale, grad = norm_back(
            rows, gain, vec_ref[1:2, :], first_rows(prior_ref, 0, marks),
            [(grads[j], vec_ref[2 + j : 3 + j, :], 2 + j) for j in range(3)],
            vec_out, prior_one, marks,
        )
        vec_out(0, jnp.sum(grad * unit, axis=0, keepdims=True))
        vec_out(1, jnp.sum(grad, axis=0, keepdims=True))
        grad = grad * gain
        mean = jnp.mean(grad, axis=-1, keepdims=True)
        along = jnp.mean(grad * unit, axis=-1, keepdims=True)
        entry = (wide_three[...] + scale * (grad - mean - unit * along)).astype(BF16)
        ing_ref[...] = entry
        out_ref[...] = entry


def plain(shapes):
    return tuple(jax.ShapeDtypeStruct(s, d) for s, d in shapes)


def in_vmem(shapes):
    return tuple(pltpu.VMEM(s, d) for s, d in shapes)


def hold(arrays):
    return tuple(pltpu.with_memory_space_constraint(a, pltpu.VMEM) for a in arrays)


ROWS_OUT = jax.ShapeDtypeStruct((ROWS, WIDTH), BF16)
TOKENS = pltpu.VMEM((ROWS * GROUPS, 128), F32)
SMALL = pltpu.VMEM((GROUPS, 128), F32)
WIDE = pltpu.VMEM((ROWS, WIDTH), F32)


def forward_first(flag, begins, rows, small, weights):
    results = pl.pallas_call(
        forward_first_kernel,
        out_shape=(ROWS_OUT,) + in_vmem(WEIGHTS) + in_vmem(SAVED),
        in_specs=[SM, SM] + [VM] * N_SMALL + [HB] * 5,
        out_specs=(VM,) * 13,
        scratch_shapes=[TOKENS, TOKENS, TOKENS, SMALL, pltpu.SemaphoreType.DMA((5,))],
        compiler_params=PARAMS,
    )(flag, begins, rows, *small, *weights)
    return results[0], results[1:6], results[6:]


def forward_next(flag, begins, rows, small, weights, saved):
    results = pl.pallas_call(
        forward_kernel,
        out_shape=(ROWS_OUT,) + plain(WEIGHTS) + plain(SAVED),
        in_specs=[SM, SM] + [VM] * (N_SMALL + 12),
        out_specs=(VM,) * 13,
        input_output_aliases={2 + N_SMALL + i: 1 + i for i in range(12)},
        scratch_shapes=[TOKENS, TOKENS, TOKENS, SMALL],
        compiler_params=PARAMS,
    )(flag, begins, rows, *small, *hold(weights), *hold(saved))
    return results[0], results[1:6], results[6:]


def backward_call(flag, begins, grad, small, weights, saved, grads):
    first = grads is None
    held = hold(weights) + hold(saved) + (() if first else hold(grads))
    results = pl.pallas_call(
        functools.partial(backward_kernel, first),
        out_shape=(ROWS_OUT,)
        + plain(WEIGHTS)
        + plain(SAVED)
        + (in_vmem(GRADS) if first else plain(GRADS)),
        in_specs=[SM, SM] + [VM] * (4 + len(held)),
        out_specs=(VM,) * 19,
        input_output_aliases={6 + i: 1 + i for i in range(len(held))},
        scratch_shapes=[TOKENS, TOKENS, TOKENS, SMALL, WIDE, WIDE, WIDE],
        compiler_params=PARAMS,
    )(flag, begins, grad, *small, *held)
    return results[0], results[1:6], results[6:13], results[13:]


def transposed(left, right):
    return lax.dot_general(
        left, right, (((0,), (0,)), ((), ())), preferred_element_type=F32
    ).astype(BF16)


def body(
    bottom_stack_feed,
    loss_sensitivity,
    resumes_segment,
    mixing_coefficients,
    fading_log,
    feature_boost,
    attention_maps,
    emission_coefficients,
    feature_addressing,
    feature_payload,
    feature_receptance,
    dividend_memory,
    divisor_memory,
    memory_power_shift,
    prior_normed_lines,
):
    sections = lax.axis_size("section")
    section = lax.axis_index("section")
    flags = [(section == t).astype(jnp.int32)[None] for t in range(sections)]
    small = (
        mixing_coefficients[0],
        fading_log,
        feature_boost,
        dividend_memory[0],
        divisor_memory[0],
        memory_power_shift[0],
        prior_normed_lines[0],
    )
    weights = (
        attention_maps[0],
        emission_coefficients[0],
        feature_addressing[0],
        feature_payload[0],
        feature_receptance[0],
    )
    rows, weights, saved = forward_first(
        flags[0], resumes_segment, bottom_stack_feed.reshape(ROWS, WIDTH), small, weights
    )
    for t in range(1, sections):
        rows = lax.ppermute(rows, "section", [(t - 1, t)])
        rows, weights, saved = forward_next(
            flags[t], resumes_segment, rows, small, weights, saved
        )
    back_small = (small[0], small[1], small[6])
    grad, weights, saved, grads = backward_call(
        flags[-1], resumes_segment, loss_sensitivity.reshape(ROWS, WIDTH), back_small,
        weights, saved, None,
    )
    for t in range(sections - 2, -1, -1):
        grad = lax.ppermute(grad, "section", [(t + 1, t)])
        grad, weights, saved, grads = backward_call(
            flags[t], resumes_segment, grad, back_small, weights, saved, grads
        )
    entry, layer, mixes, hidden, _, _, _ = saved
    entry_grad, outer, dhp, vecg, state_grads, row_grads = grads
    parts = [transposed(mixes[j], outer[j]) for j in range(4)]
    parts.append(transposed(mixes[4], dhp))
    parts.append(transposed(mixes[5], outer[5]))
    parts.append(jnp.pad(vecg.T, ((0, 0), (0, 112))).astype(BF16))
    payload = transposed(hidden, outer[4])
    shard = lax.psum_scatter(
        jnp.concatenate(parts, axis=1), "dp", scatter_dimension=0, tiled=True
    ).astype(F32)
    payload = lax.psum_scatter(payload, "dp", scatter_dimension=0, tiled=True).astype(F32)
    vectors = shard[:, 9 * WIDTH :].T
    return (
        layer.reshape(1, SEQS, LENGTH, WIDTH),
        entry_grad.reshape(1, SEQS, LENGTH, WIDTH),
        vectors[None, :9],
        vectors[9:10],
        vectors[10:11],
        jnp.stack([shard[:, j * WIDTH : (j + 1) * WIDTH] for j in range(3)])[None],
        shard[None, :, 3 * WIDTH : 4 * WIDTH],
        shard[None, :, 4 * WIDTH : 8 * WIDTH],
        payload[None],
        shard[None, :, 8 * WIDTH : 9 * WIDTH],
        state_grads[0][None],
        state_grads[1][None],
        state_grads[2][None],
        row_grads[None],
    )


def solution(mesh):
    placed = (
        P("dp", None, None),
        P("dp", None, None),
        P("dp"),
        P("section", None, None),
        P("section", None),
        P("section", None),
        P("section", None, None, None),
        P("section", None, None),
        P("section", None, None),
        P("section", None, None),
        P("section", None, None),
        P("section", "dp", None),
        P("section", "dp", None),
        P("section", "dp", None),
        P("section", None, "dp", None),
    )
    return jax.shard_map(
        body,
        mesh=mesh,
        in_specs=placed,
        out_specs=(
            P("section", "dp", None, None),
            P("section", "dp", None, None),
            P("section", None, "dp"),
            P("section", "dp"),
            P("section", "dp"),
            P("section", None, "dp", None),
            P("section", "dp", None),
            P("section", "dp", None),
            P("section", "dp", None),
            P("section", "dp", None),
            P("section", "dp", None),
            P("section", "dp", None),
            P("section", "dp", None),
            P("section", None, "dp", None),
        ),
        check_vma=False,
    )
```

```python
import functools

import jax
import jax.numpy as jnp
from jax import lax
from jax.experimental import pallas as pl
from jax.experimental.pallas import tpu as pltpu
from jax.sharding import PartitionSpec as P

WIDTH = 1024
INNER = 4096
LENGTH = 64
SEQS = 2
ROWS = SEQS * LENGTH
GROUPS = WIDTH // 128
FRESH = -1e30
EPS = 1e-05
F32 = jnp.float32
BF16 = jnp.bfloat16

VM = pl.BlockSpec(memory_space=pltpu.VMEM)
HB = pl.BlockSpec(memory_space=pl.ANY)
SM = pl.BlockSpec(memory_space=pltpu.SMEM)
EDGE = ROWS + 16
QUARTER = 1536
SHARE = 1792


HELD_LIMIT = 14


def limit(mebibytes):
    return pltpu.CompilerParams(vmem_limit_bytes=mebibytes * 1024 * 1024)

WEIGHTS = (
    ((3, WIDTH, WIDTH), BF16),
    ((WIDTH, WIDTH), BF16),
    ((WIDTH, INNER), BF16),
    ((INNER, WIDTH), BF16),
    ((WIDTH, WIDTH), BF16),
)
CONSTS = (
    ((9, WIDTH), F32),
    ((1, WIDTH), F32),
    ((1, WIDTH), F32),
    ((SEQS, WIDTH), F32),
    ((SEQS, WIDTH), F32),
    ((SEQS, WIDTH), F32),
    ((2, SEQS, WIDTH), BF16),
)
SAVED = (
    ((ROWS, WIDTH), BF16),
    ((ROWS, WIDTH), BF16),
    ((ROWS, INNER), BF16),
    ((5, ROWS, WIDTH), F32),
    ((8, ROWS * GROUPS, 128), F32),
)
EDGES = (
    ((EDGE, 2 * WIDTH), BF16),
    ((EDGE, 2 * WIDTH), BF16),
)
GRADS = (
    ((ROWS, WIDTH), BF16),
    ((4, ROWS, QUARTER), BF16),
    ((4, ROWS, QUARTER), BF16),
    ((3, SEQS, WIDTH), F32),
    ((2, SEQS, WIDTH), F32),
)
N_CONSTS, N_WEIGHTS, N_SAVED, N_EDGES, N_GRADS = 7, 5, 5, 2, 5
N_BASE = N_CONSTS + N_WEIGHTS + N_SAVED


def dot(left, right):
    return jnp.dot(left, right, preferred_element_type=F32)


def against(grad, weight):
    return lax.dot_general(
        grad, weight, (((1,), (1,)), ((), ())), preferred_element_type=F32
    )


def across(left, right):
    return lax.dot_general(
        left, right, (((0,), (0,)), ((), ())), preferred_element_type=F32
    )


def coordinates(place):
    dp = place[1]
    return place[0], dp >> 3, (dp >> 1) & 3, dp & 1


def row_index():
    return lax.broadcasted_iota(jnp.int32, (ROWS, WIDTH), 0)


def normed_rows(rows):
    center = jnp.mean(rows, axis=-1, keepdims=True)
    centered = rows - center
    variance = jnp.mean(centered * centered, axis=-1, keepdims=True)
    scale = lax.rsqrt(variance + EPS)
    return centered * scale, scale


def moved_down(normed, first):
    index = row_index()
    return jnp.where(
        index == 0,
        first[0],
        jnp.where(index == LENGTH, first[1], pltpu.roll(normed, 1, 0)),
    )


def moved_up(rows):
    index = row_index()
    return jnp.where(
        (index == LENGTH - 1) | (index == ROWS - 1),
        0.0,
        pltpu.roll(rows, ROWS - 1, 0),
    )


def first_rows(prior_ref, mix, marks):
    return [prior_ref[mix, s : s + 1, :].astype(F32) * marks[s] for s in range(SEQS)]


def edge_rows(first):
    index = lax.broadcasted_iota(jnp.int32, (EDGE - ROWS, WIDTH), 0)
    return jnp.where(index == 0, first[0], jnp.where(index == 1, first[1], 0.0)).astype(BF16)


def put(core, which, keep_ref, send_ref, at, value):
    @pl.when(core == which)
    def _():
        keep_ref[at] = value

    @pl.when(core != which)
    def _():
        send_ref[at] = value


def to_tokens(ref, block, value):
    ref[pl.ds(block, ROWS, stride=GROUPS), :] = value


def from_tokens(ref, block):
    return ref[pl.ds(block, ROWS, stride=GROUPS), :]


def tile_of(ref, row, small):
    for g in range(GROUPS):
        small[g : g + 1, :] = ref[row : row + 1, g * 128 : (g + 1) * 128]
    return small[...]


def forward_body(core, marks, x_ref, consts, weights, ready, out_ref, saved, edges, scratch):
    vec_ref, fade_ref, boost_ref, num_ref, den_ref, lev_ref, prior_ref = consts
    wm, wo, wa, wp, wr = weights
    ent_ref, lay_ref, act_ref, wide_ref, scan_ref = saved
    own_ref, other_ref = edges
    sk, sv, sy, small, mix_ref, hid_ref = scratch
    low, high = slice(0, WIDTH), slice(WIDTH, 2 * WIDTH)
    top, bottom = slice(0, ROWS), slice(ROWS, EDGE)
    if x_ref is not None:
        ent_ref[...] = x_ref[...]
    rows = ent_ref[...].astype(F32)
    unit, _ = normed_rows(rows)
    normed = unit * vec_ref[0:1, :] + vec_ref[1:2, :]
    first = first_rows(prior_ref, 0, marks)
    below = moved_down(normed, first)
    for j in range(3):
        v = vec_ref[2 + j : 3 + j, :]
        mix_ref[j] = (normed * v + below * (1.0 - v)).astype(BF16)
    put(core, 0, own_ref, other_ref, (top, high), normed.astype(BF16))
    put(core, 0, own_ref, other_ref, (bottom, high), edge_rows(first))
    ready(0)
    for target, j in ((sk, 0), (sv, 1)):
        for c in range(0, WIDTH, 256):
            part = dot(mix_ref[j], wm[j, :, c : c + 256])
            for h in range(2):
                to_tokens(target, c // 128 + h, part[:, h * 128 : (h + 1) * 128])
    wide_ref[0] = jax.nn.sigmoid(dot(mix_ref[2], wm[2]))

    rate = jnp.exp(tile_of(fade_ref, 0, small))
    boost = tile_of(boost_ref, 0, small)
    start = []
    for s in range(SEQS):
        level = tile_of(lev_ref, s, small)
        start.append(jnp.where(marks[s] > 0.0, level, FRESH))
        start.append(tile_of(num_ref, s, small) * marks[s])
        start.append(tile_of(den_ref, s, small) * marks[s])

    def token(t, carry):
        carry_next = []
        for s in range(SEQS):
            level, num, den = carry[3 * s : 3 * s + 3]
            at = pl.ds(pl.multiple_of((t + LENGTH * s) * GROUPS, GROUPS), GROUPS)
            key, value = sk[at, :], sv[at, :]
            boosted = boost + key
            decayed = jnp.exp(-jnp.abs(level - boosted))
            state_on_top = level > boosted
            old = jnp.where(state_on_top, 1.0, decayed)
            fresh = jnp.where(state_on_top, decayed, 1.0)
            inverse = 1.0 / (old * den + fresh)
            old = old * inverse
            fresh = fresh * inverse
            result = old * num + fresh * value
            faded = level - rate
            level = jnp.maximum(faded, key)
            decayed = jnp.exp(-jnp.abs(faded - key))
            state_on_top = faded > key
            keep = jnp.where(state_on_top, 1.0, decayed)
            new = jnp.where(state_on_top, decayed, 1.0)
            sy[at, :] = result
            scan_ref[0, at, :] = old
            scan_ref[1, at, :] = fresh
            scan_ref[2, at, :] = value - result
            scan_ref[3, at, :] = keep
            scan_ref[4, at, :] = new
            scan_ref[5, at, :] = num
            scan_ref[6, at, :] = den
            scan_ref[7, at, :] = value
            carry_next += [level, keep * num + new * value, keep * den + new]
        return tuple(carry_next)

    def tokens(block, carry):
        for j in range(8):
            carry = token(block * 8 + j, carry)
        return carry

    lax.fori_loop(0, LENGTH // 8, tokens, tuple(start))
    for g in range(GROUPS):
        at = slice(g * 128, (g + 1) * 128)
        gate = wide_ref[0, :, at]
        mixed = gate * from_tokens(sy, g)
        mix_ref[0, :, at] = mixed.astype(BF16)
        wide_ref[1, :, at] = mixed * (1.0 - gate)
    put(core, 1, own_ref, other_ref, (top, high), mix_ref[0])
    ready(1)
    wide_ref[2] = rows + dot(mix_ref[0], wo[...])
    unit, _ = normed_rows(wide_ref[2])
    normed = unit * vec_ref[5:6, :] + vec_ref[6:7, :]
    first = first_rows(prior_ref, 1, marks)
    below = moved_down(normed, first)
    for j in range(2):
        v = vec_ref[7 + j : 8 + j, :]
        mix_ref[1 + j] = (normed * v + below * (1.0 - v)).astype(BF16)
    for ref in edges:
        ref[top, low] = normed.astype(BF16)
        ref[bottom, low] = edge_rows(first)
    ready(4)
    wide_ref[4] = jax.nn.sigmoid(dot(mix_ref[2], wr[...]))
    ready(2)

    @pl.loop(0, INNER // 512)
    def _(j):
        at = pl.ds(pl.multiple_of(j * 512, 512), 512)
        active = jnp.maximum(dot(mix_ref[1], wa[:, at]), 0.0)
        act_ref[:, at] = active.astype(BF16)
        hid_ref[:, at] = (active * active).astype(BF16)

    ready(3)

    @pl.loop(0, WIDTH // 256)
    def _(j):
        at = pl.ds(pl.multiple_of(j * 256, 256), 256)
        channel = dot(hid_ref[...], wp[:, at])
        wide_ref[3, :, at] = channel
        lay_ref[:, at] = (wide_ref[2, :, at] + wide_ref[4, :, at] * channel).astype(BF16)

    out_ref[...] = lay_ref[...]


def groups(refs, *sizes):
    cut, at = [], 0
    for size in sizes:
        cut.append(refs[at : at + size])
        at += size
    return cut + [refs[at:]]


def forward_first_kernel(place, begins, x_ref, *refs):
    small_in, hbm, (out_ref,), consts, kept, saved, edges, rest = groups(
        refs, N_CONSTS, N_WEIGHTS, 1, N_CONSTS, N_WEIGHTS, N_SAVED, N_EDGES
    )
    section, _, _, core = coordinates(place)
    sem, small_sem = rest[-2:]
    copies = [pltpu.make_async_copy(hbm[i], kept[i], sem.at[i]) for i in range(N_WEIGHTS)]
    arriving = [pltpu.make_async_copy(x_ref, saved[0], small_sem.at[N_CONSTS])]
    for i in range(N_CONSTS):
        arriving.append(pltpu.make_async_copy(small_in[i], consts[i], small_sem.at[i]))
    for c in arriving:
        c.start()
    for i in (0, 1, 4, 2, 3):
        copies[i].start()
    for c in arriving:
        c.wait()

    @pl.when(section == 0)
    def _():
        marks = [begins[s].astype(F32) for s in range(SEQS)]
        forward_body(
            core, marks, None, consts, kept, lambda i: copies[i].wait(), out_ref, saved,
            edges, rest[:-2],
        )

    @pl.when(section != 0)
    def _():
        for c in copies:
            c.wait()


def forward_kernel(layer, place, begins, x_ref, *refs):
    _, (out_ref,), consts, kept, saved, edges, scratch = groups(
        refs, N_BASE + N_EDGES, 1, N_CONSTS, N_WEIGHTS, N_SAVED, N_EDGES
    )
    section, _, _, core = coordinates(place)

    @pl.when(section == layer)
    def _():
        marks = [begins[s].astype(F32) for s in range(SEQS)]
        forward_body(
            core, marks, x_ref, consts, kept, lambda i: None, out_ref, saved, edges, scratch
        )


def norm_back(rows, gain, offset, first, parts, vec_out, prior_out, marks):
    unit, scale = normed_rows(rows)
    normed = unit * gain + offset
    change = normed - moved_down(normed, first)
    up, stay = None, None
    for grad, weight, row in parts:
        vec_out(row, jnp.sum(grad * change, axis=0, keepdims=True))
        kept = grad * weight
        passed = grad - kept
        stay = kept if stay is None else stay + kept
        up = passed if up is None else up + passed
    for s in range(SEQS):
        prior_out(s, up[s * LENGTH : s * LENGTH + 1, :] * marks[s])
    grad = stay + moved_up(up)
    return unit, scale, grad


def backward_kernel(first, layer, place, begins, dy_ref, *refs):
    extra = N_EDGES if first else 0
    _, (out_ref,), consts, kept, saved, grads, _, scratch = groups(
        refs, N_BASE + (extra if first else N_GRADS), 1, N_CONSTS, N_WEIGHTS, N_SAVED, N_GRADS, extra
    )
    vec_ref, fade_ref, prior_ref = consts[0], consts[1], consts[6]
    wm, wo, wa, wp, wr = kept
    ent_ref, lay_ref, act_ref, wide_ref, scan_ref = saved
    ing_ref, keep_ref, send_ref, stg_ref, rowg_ref = grads
    sg, sdk, sdv, small, wide, wide_two, wide_three, dys_ref, dhp_ref, vecg_ref = scratch
    section, y, z, core = coordinates(place)
    everything = slice(None)

    def vec_out(row, value):
        vecg_ref[row : row + 1, :] = value

    def share(which, column, size, quarter, value):
        distance = (quarter - (y if which else z)) & 3
        at = (distance, everything, slice(column, column + size))
        put(core, which, keep_ref, send_ref, at, value)

    @pl.when(section == layer)
    def _():
        marks = [begins[s].astype(F32) for s in range(SEQS)]
        dy = dy_ref[...].astype(F32)
        gate = wide_ref[4]
        through = dy * gate
        dys_ref[4] = through.astype(BF16)
        dys_ref[5] = (through * wide_ref[3] * (1.0 - gate)).astype(BF16)
        for j in range(INNER // 512):
            at = slice(j * 512, (j + 1) * 512)
            part = against(dys_ref[4], wp[at, :])
            dhp_ref[:, at] = (2.0 * act_ref[:, at].astype(F32) * part).astype(BF16)
            share(j // 4, 0, 512, j % 4, dhp_ref[:, at])
        for q in range(4):
            at = slice(q * 256, (q + 1) * 256)
            share(0, 512, 256, q, dys_ref[4, :, at])
            share(1, 512, 256, q, dys_ref[4, :, at])
            share(1, 768, 256, q, dys_ref[5, :, at])

        @pl.loop(0, WIDTH // 256)
        def _(j):
            at = pl.ds(pl.multiple_of(j * 256, 256), 256)
            wide[:, at] = against(dhp_ref[...], wa[at, :])
            wide_two[:, at] = against(dys_ref[5], wr[at, :])

        def prior_two(s, value):
            rowg_ref[1, s : s + 1, :] = value

        gain = vec_ref[5:6, :]
        unit, scale, grad = norm_back(
            wide_ref[2], gain, vec_ref[6:7, :], first_rows(prior_ref, 1, marks),
            ((wide[...], vec_ref[7:8, :], 7), (wide_two[...], vec_ref[8:9, :], 8)),
            vec_out, prior_two, marks,
        )
        vec_out(5, jnp.sum(grad * unit, axis=0, keepdims=True))
        vec_out(6, jnp.sum(grad, axis=0, keepdims=True))
        grad = grad * gain
        mean = jnp.mean(grad, axis=-1, keepdims=True)
        along = jnp.mean(grad * unit, axis=-1, keepdims=True)
        middle = dy_ref[...].astype(F32) + scale * (grad - mean - unit * along)
        wide_three[...] = middle
        dys_ref[3] = middle.astype(BF16)
        for q in range(4):
            at = slice(q * 256, (q + 1) * 256)
            share(1, 1024, 256, q, dys_ref[3, :, at])
            part = against(dys_ref[3], wo[at, :])
            dys_ref[2, :, at] = (part * wide_ref[1, :, at]).astype(BF16)
            part = part * wide_ref[0, :, at]
            for h in range(2):
                to_tokens(sg, q * 2 + h, part[:, h * 128 : (h + 1) * 128])

        zero = jnp.zeros((GROUPS, 128), F32)

        def token(t, carry):
            carry_next = []
            boosted, faded = carry[4], carry[5]
            for s in range(SEQS):
                dnum, dden = carry[2 * s : 2 * s + 2]
                at = pl.ds(pl.multiple_of((t + LENGTH * s) * GROUPS, GROUPS), GROUPS)
                g = sg[at, :]
                value = scan_ref[7, at, :]
                beyond = scan_ref[2, at, :]
                keep = scan_ref[3, at, :]
                new = scan_ref[4, at, :]
                from_old = scan_ref[0, at, :] * g
                from_new = scan_ref[1, at, :] * g
                direct = from_new * beyond
                boosted = boosted + direct
                sdv[at, :] = from_new + new * dnum
                sdk[at, :] = direct + new * (dnum * value + dden)
                faded = faded - keep * (dnum * scan_ref[5, at, :] + dden * scan_ref[6, at, :])
                carry_next += [
                    from_old + keep * dnum,
                    keep * dden - from_old * (value - beyond),
                ]
            return tuple(carry_next) + (boosted, faded)

        def tokens(block, carry):
            for j in range(8):
                carry = token(LENGTH - 1 - block * 8 - j, carry)
            return carry

        ends = lax.fori_loop(0, LENGTH // 8, tokens, (zero,) * 6)

        def spread(put_piece, value):
            small[...] = value
            for g in range(GROUPS):
                put_piece(slice(g * 128, (g + 1) * 128), small[g : g + 1, :])

        for s in range(SEQS):
            dnum, dden = ends[2 * s : 2 * s + 2]
            at = pl.ds(LENGTH * s * GROUPS, GROUPS)
            moved = dnum * scan_ref[5, at, :] + dden * scan_ref[6, at, :]
            for k, value in enumerate((dnum, dden, moved)):

                def put_state(cols, piece, k=k, s=s):
                    stg_ref[k, s : s + 1, cols] = piece

                spread(put_state, value * marks[s])

        def put_decay(cols, piece):
            vecg_ref[9:10, cols] = piece

        def put_boost(cols, piece):
            vecg_ref[10:11, cols] = piece

        spread(put_decay, ends[5])
        vecg_ref[9:10, :] = vecg_ref[9:10, :] * jnp.exp(fade_ref[0:1, :])
        spread(put_boost, ends[4])

        for g in range(GROUPS):
            at = slice(g * 128, (g + 1) * 128)
            dys_ref[0, :, at] = from_tokens(sdk, g).astype(BF16)
            dys_ref[1, :, at] = from_tokens(sdv, g).astype(BF16)
        for q in range(4):
            at = slice(q * 256, (q + 1) * 256)
            for j in range(3):
                share(0, 768 + 256 * j, 256, q, dys_ref[j, :, at])

        rows = ent_ref[...].astype(F32)
        pulled = [against(dys_ref[j], wm[j]) for j in range(3)]

        def prior_one(s, value):
            rowg_ref[0, s : s + 1, :] = value

        gain = vec_ref[0:1, :]
        unit, scale, grad = norm_back(
            rows, gain, vec_ref[1:2, :], first_rows(prior_ref, 0, marks),
            [(pulled[j], vec_ref[2 + j : 3 + j, :], 2 + j) for j in range(3)],
            vec_out, prior_one, marks,
        )
        vec_out(0, jnp.sum(grad * unit, axis=0, keepdims=True))
        vec_out(1, jnp.sum(grad, axis=0, keepdims=True))
        for q in range(4):
            packed = jnp.concatenate(
                [vecg_ref[:, b * 256 : (b + 1) * 256] for b in range(4)], axis=0
            ).astype(BF16)
            put(
                core, 1, keep_ref, send_ref,
                (q, slice(0, 64), slice(1280, 1536)), packed,
            )
        grad = grad * gain
        mean = jnp.mean(grad, axis=-1, keepdims=True)
        along = jnp.mean(grad * unit, axis=-1, keepdims=True)
        entry = (wide_three[...] + scale * (grad - mean - unit * along)).astype(BF16)
        ing_ref[...] = entry
        out_ref[...] = entry


def join_kernel(pieces, first, second, *refs):
    sem = refs[-1]
    copies = []
    for k in range(pieces):
        for h, ref in enumerate((first, second)):
            source = ref if pieces == 1 else ref.at[k]
            rows = source.shape[0]
            copies.append(
                pltpu.make_async_copy(
                    source, refs[k].at[pl.ds(h * rows, rows), :], sem.at[2 * k + h]
                )
            )
    for c in copies:
        c.start()
    for c in copies:
        c.wait()


def mixes_kernel(chosen, last, place, own, one, two, three, vec_ref, wa, *refs):
    if last:
        (x_ref, layer, entry, states, firsts), outs, scratch = groups(refs, 5, 8)
        _, x_near, *results = outs
        sources = (layer, entry) + tuple(states.at[k] for k in range(3)) + (firsts,)
        near_sem, result_sem = scratch[-2:]
        drained = [
            pltpu.make_async_copy(source, target, result_sem.at[i])
            for i, (source, target) in enumerate(zip(sources, results))
        ]
        for c in drained:
            c.start()
    else:
        x_ref, scratch = refs[2], refs[3:]
    edge, wide, stage, edge_sem, wide_sem, out_sem = scratch[:6]
    section, _, _, core = coordinates(place)

    @pl.when(chosen(section))
    def _():
        blocks = (own, one, two, three)
        loads = [
            pltpu.make_async_copy(
                blocks[n // 2].at[pl.ds(n % 2 * EDGE, EDGE), :], edge.at[n % 2], edge_sem.at[n % 2]
            )
            for n in range(8)
        ]
        columns = [
            pltpu.make_async_copy(
                wa.at[:, pl.ds(pl.multiple_of((2 * j + core) * 128, 128), 128)],
                wide.at[:, pl.ds(j * 128, 128)],
                wide_sem.at[j],
            )
            for j in range(16)
        ]
        outs = [
            pltpu.make_async_copy(
                stage.at[n % 2], x_ref.at[pl.ds(n * ROWS, ROWS), :], out_sem.at[n % 2]
            )
            for n in range(8)
        ]
        loads[0].start()
        for c in columns:
            c.start()

        def mix(normed, below, j):
            v = vec_ref[j : j + 1, :]
            return (normed * v + below * (1.0 - v)).astype(BF16)

        for n in range(8):
            if n + 1 < 8:
                loads[n + 1].start()
            loads[n].wait()
            if n >= 2:
                outs[n - 2].wait()
            block, here = edge.at[n % 2], stage.at[n % 2]

            def parts(c, block=block):
                cols = slice(c * WIDTH, (c + 1) * WIDTH)
                normed = block[:ROWS, cols].astype(F32)
                first = block[ROWS:, cols].astype(F32)
                return normed, moved_down(normed, (first[0:1, :], first[1:2, :]))

            normed, below = parts(0)
            here[:, 2048:3072] = mix(normed, below, 7)

            @pl.when(core == 0)
            def _(here=here, parts=parts):
                normed, below = parts(1)
                for j in range(3):
                    here[:, 3072 + j * WIDTH : 4096 + j * WIDTH] = mix(normed, below, 2 + j)

            @pl.when(core == 1)
            def _(here=here, parts=parts, block=block):
                normed, below = parts(0)
                here[:, 3072:4096] = mix(normed, below, 8)
                here[:, 4096:5120] = block[:ROWS, WIDTH:]

            if n == 0:
                for c in columns:
                    c.wait()

            @pl.loop(0, 4)
            def _(j, here=here):
                at = pl.ds(pl.multiple_of(j * 512, 512), 512)
                active = jnp.maximum(dot(here[:, 2048:3072], wide[:, at]), 0.0)
                here[:, at] = (active * active).astype(BF16)

            outs[n].start()
        for n in (6, 7):
            outs[n].wait()

    if last:
        near = [
            pltpu.make_async_copy(
                x_ref.at[:, pl.ds(u * WIDTH, WIDTH)], x_near.at[u], near_sem.at[u]
            )
            for u in range(6)
        ]
        for c in near:
            c.start()
        for c in near + drained:
            c.wait()


def weight_kernel(place, x_ref, *refs):
    blocks, outs = refs[:4], refs[4:8]
    dy, share, dy_sem, out_sem = refs[8:]
    _, y, z, core = coordinates(place)
    loads = [
        pltpu.make_async_copy(
            blocks[k], dy.at[pl.ds(k * 2 * ROWS, 2 * ROWS), :], dy_sem.at[k]
        )
        for k in range(4)
    ]
    for c in loads:
        c.start()

    def rows_of(there_y, there_z):
        along_y, along_z = (there_y - y) & 3, (there_z - z) & 3
        summed = jnp.where(core == 0, along_y, along_z)
        joined = jnp.where(core == 0, along_z, along_y)
        return pl.multiple_of(summed * 256 + joined * 64, 64)

    starts = [rows_of(b // 4, b % 4) for b in range(16)]

    def unit(u, size, source, target):
        for c in range(0, WIDTH, 256):
            part = across(x_ref[u, :, c : c + 256], dy[:, source : source + size]).astype(BF16)
            for b in range(4):
                share[pl.ds(starts[c // 64 + b], 64), target : target + size] = part[
                    b * 64 : (b + 1) * 64, :
                ]

    for c in loads:
        c.wait()
    unit(2, 512, 0, 0)
    for u in range(2):
        for c in range(0, WIDTH, 256):
            part = across(x_ref[u, :, c : c + 256], dy[:, 512:768]).astype(BF16)
            for b in range(2):
                start = starts[(u * WIDTH + c) // 128 + b]
                for half in range(2):
                    share[pl.ds(start, 64), 1280 + half * 256 : 1536 + half * 256] = part[
                        b * 128 + half * 64 : b * 128 + (half + 1) * 64, :
                    ]
    for u in range(3, 5):
        unit(u, 256, u * 256, 512 + (u - 3) * 256)

    @pl.when(core == 0)
    def _():
        unit(5, 256, 1280, 1024)

    @pl.when(core == 1)
    def _():
        total = jnp.zeros((64, 256), F32)
        for d in range(8):
            total = total + dy[d * ROWS : d * ROWS + 64, 1280:1536].astype(F32)
        for b in range(4):
            piece = jnp.concatenate(
                [total[b * 16 : (b + 1) * 16, :], jnp.zeros((112, 256), F32)], axis=0
            ).T.astype(BF16)
            for e in range(4):
                at = pl.ds(starts[b * 4 + e], 64)
                share[at, 1024:1152] = piece[e * 64 : (e + 1) * 64, :]
                share[at, 1152:1280] = jnp.zeros((64, 128), BF16)

    copies = [
        pltpu.make_async_copy(share.at[pl.ds(k * 256, 256), :], outs[k], out_sem.at[k])
        for k in range(4)
    ]
    for c in copies:
        c.start()
    for c in copies:
        c.wait()


def sum_kernel(own, one, two, three, *outs):
    total = own[...].astype(F32) + one[...].astype(F32) + two[...].astype(F32)
    total = (total + three[...].astype(F32)).astype(BF16)
    for k in range(4):
        outs[k][...] = total[k * 64 : (k + 1) * 64, :]


def gather_kernel(place, own, one, two, three, keep_ref, send_ref, pay_ref):
    _, y, z, core = coordinates(place)
    here = jnp.where(core == 0, z, y)
    mine = pl.multiple_of(core * 32, 32)
    theirs = pl.multiple_of(32 - core * 32, 32)
    for k, ref in enumerate((own, one, two, three)):
        quarter = (here - k) & 3
        wide = pl.ds(pl.multiple_of(quarter * 512, 512), 512)
        for rows, target in ((mine, keep_ref), (theirs, send_ref)):
            target[:, wide] = ref[pl.ds(rows, 32), 0:512]
            for u in range(3):
                at = pl.ds(pl.multiple_of(2048 + u * WIDTH + quarter * 256, 256), 256)
                target[:, at] = ref[pl.ds(rows, 32), 512 + u * 256 : 768 + u * 256]
        at = pl.ds(pl.multiple_of(quarter * 256, 256), 256)
        for half in range(2):
            pay_ref[half * 64 : (half + 1) * 64, at] = ref[
                :, 1280 + half * 256 : 1536 + half * 256
            ].astype(F32)


def final_kernel(place, kept, come, proj_ref, out_ref, key_ref, gate_ref, vec_ref, dec_ref, boo_ref):
    core = coordinates(place)[3]

    def write(set_zero, set_one):
        key_ref[:, 0:2048] = set_zero[:, 0:2048].astype(F32)
        key_ref[:, 2048:4096] = set_one[:, 0:2048].astype(F32)
        for u in range(3):
            at = slice(2048 + u * WIDTH, 3072 + u * WIDTH)
            proj_ref[u] = set_zero[:, at].astype(F32)
        gate_ref[...] = set_one[:, 2048:3072].astype(F32)
        out_ref[...] = set_one[:, 3072:4096].astype(F32)
        vectors = set_one[:, 4096:4224].astype(F32).T
        for j in range(9):
            vec_ref[j] = vectors[j : j + 1, :]
        dec_ref[...] = vectors[9:10, :]
        boo_ref[...] = vectors[10:11, :]

    @pl.when(core == 0)
    def _():
        write(kept, come)

    @pl.when(core == 1)
    def _():
        write(come, kept)


def plain(shapes):
    return tuple(jax.ShapeDtypeStruct(s, d) for s, d in shapes)


def in_vmem(shapes):
    return tuple(pltpu.VMEM(s, d) for s, d in shapes)


def hold(arrays):
    return tuple(pltpu.with_memory_space_constraint(a, pltpu.VMEM) for a in arrays)


def in_hbm(*arrays):
    return tuple(pltpu.with_memory_space_constraint(a, pltpu.HBM) for a in arrays)


def array(*shape, kind=BF16):
    return jax.ShapeDtypeStruct(shape, kind)


ROWS_OUT = array(ROWS, WIDTH)
TOKENS = pltpu.VMEM((ROWS * GROUPS, 128), F32)
SMALL = pltpu.VMEM((GROUPS, 128), F32)
WIDE = pltpu.VMEM((ROWS, WIDTH), F32)
FORWARD_SCRATCH = [
    TOKENS, TOKENS, TOKENS, SMALL,
    pltpu.VMEM((3, ROWS, WIDTH), BF16),
    pltpu.VMEM((ROWS, INNER), BF16),
]
DMA = pltpu.SemaphoreType.DMA


def forward_first(place, begins, rows, small, weights):
    shapes = CONSTS + WEIGHTS + SAVED + EDGES
    results = pl.pallas_call(
        forward_first_kernel,
        cost_estimate=cost(12),
        out_shape=(ROWS_OUT,) + in_vmem(shapes),
        in_specs=[SM, SM] + [HB] * (1 + N_CONSTS + N_WEIGHTS),
        out_specs=(VM,) * (1 + len(shapes)),
        scratch_shapes=FORWARD_SCRATCH + [DMA((N_WEIGHTS,)), DMA((N_CONSTS + 1,))],
        compiler_params=limit(HELD_LIMIT),
    )(place, begins, *in_hbm(rows, *small, *weights))
    return results[0], results[1:]


def forward_next(layer, place, begins, rows, held):
    shapes = CONSTS + WEIGHTS + SAVED + EDGES
    results = pl.pallas_call(
        functools.partial(forward_kernel, layer),
        cost_estimate=cost(10),
        out_shape=(ROWS_OUT,) + plain(shapes),
        in_specs=[SM, SM] + [VM] * (1 + len(shapes)),
        out_specs=(VM,) * (1 + len(shapes)),
        input_output_aliases={3 + i: 1 + i for i in range(len(shapes))},
        scratch_shapes=FORWARD_SCRATCH,
        compiler_params=limit(HELD_LIMIT),
    )(place, begins, *hold((rows,)), *hold(held))
    return results[0], results[1:]


def backward_call(layer, place, begins, grad, held, edges=()):
    first = len(edges) > 0
    base = CONSTS + WEIGHTS + SAVED
    alias = {3 + i: 1 + i for i in range(len(held))}
    for i in range(len(edges)):
        alias[3 + len(held) + i] = 1 + len(held) + N_GRADS + i
    results = pl.pallas_call(
        functools.partial(backward_kernel, first, layer),
        cost_estimate=cost(14),
        out_shape=(ROWS_OUT,)
        + plain(base)
        + (in_vmem(GRADS) + plain(EDGES) if first else plain(GRADS)),
        in_specs=[SM, SM] + [VM] * (1 + len(held) + len(edges)),
        out_specs=(VM,) * (1 + N_BASE + N_GRADS + len(edges)),
        input_output_aliases=alias,
        scratch_shapes=[
            TOKENS, TOKENS, TOKENS, SMALL, WIDE, WIDE, WIDE,
            pltpu.VMEM((6, ROWS, WIDTH), BF16),
            pltpu.VMEM((ROWS, INNER), BF16),
            pltpu.VMEM((16, WIDTH), F32),
        ],
        compiler_params=limit(HELD_LIMIT),
    )(place, begins, *hold((grad,)), *hold(held), *hold(edges))
    end = 1 + N_BASE + N_GRADS
    return results[0], results[1:end], results[end:]


def cost(microseconds):
    return pl.CostEstimate(
        flops=0, bytes_accessed=int(microseconds * 3_000_000), transcendentals=0
    )


def join(first, second, pieces=1):
    rows, columns = first.shape[-2:]
    return pl.pallas_call(
        functools.partial(join_kernel, pieces),
        out_shape=(pltpu.HBM((2 * rows, columns), BF16),) * pieces,
        in_specs=[VM, VM],
        out_specs=(HB,) * pieces,
        scratch_shapes=[DMA((2 * pieces,))],
        compiler_params=limit(1),
        cost_estimate=cost(3),
    )(*hold((first, second)))


MIXES_SCRATCH = [
    pltpu.VMEM((2, EDGE, 2 * WIDTH), BF16),
    pltpu.VMEM((WIDTH, 2048), BF16),
    pltpu.VMEM((2, ROWS, 6 * WIDTH), BF16),
    DMA((2,)),
    DMA((16,)),
    DMA((2,)),
]
X_SHAPE = (8 * ROWS, 6 * WIDTH)


def mixes(chosen, place, blocks, vec, wa, other):
    return pl.pallas_call(
        functools.partial(mixes_kernel, chosen, False),
        cost_estimate=cost(15),
        out_shape=(array(*other.shape, kind=other.dtype), pltpu.HBM(X_SHAPE, BF16)),
        in_specs=[SM] + [HB] * 4 + [VM] + [HB] * 2,
        out_specs=(HB, HB),
        input_output_aliases={7: 0},
        scratch_shapes=MIXES_SCRATCH,
        compiler_params=limit(HELD_LIMIT),
    )(place, *in_hbm(*blocks), vec, *in_hbm(wa), other)


def mixes_last(chosen, place, blocks, vec, wa, x, results):
    rows, state = pltpu.HBM((ROWS, WIDTH), BF16), pltpu.HBM((SEQS, WIDTH), F32)
    outs = pl.pallas_call(
        functools.partial(mixes_kernel, chosen, True),
        cost_estimate=cost(10),
        out_shape=(
            pltpu.HBM(X_SHAPE, BF16),
            pltpu.VMEM((6, 8 * ROWS, WIDTH), BF16),
            rows, rows, state, state, state,
            pltpu.HBM((2, SEQS, WIDTH), F32),
        ),
        in_specs=[SM] + [HB] * 4 + [VM] + [HB] * 6,
        out_specs=(HB, VM) + (HB,) * 6,
        input_output_aliases={7: 0},
        scratch_shapes=MIXES_SCRATCH + [DMA((6,)), DMA((6,))],
        compiler_params=limit(HELD_LIMIT),
    )(place, *in_hbm(*blocks), vec, *in_hbm(wa, x), *results)
    return outs[1], outs[2:]


def weight_grads(place, x, blocks):
    return pl.pallas_call(
        weight_kernel,
        cost_estimate=cost(10),
        out_shape=(pltpu.HBM((2 * ROWS, SHARE), BF16),) * 4,
        in_specs=[SM, VM] + [HB] * 4,
        out_specs=(HB,) * 4,
        scratch_shapes=[
            pltpu.VMEM((8 * ROWS, QUARTER), BF16),
            pltpu.VMEM((8 * ROWS, SHARE), BF16),
            DMA((4,)),
            DMA((4,)),
        ],
        compiler_params=limit(16),
    )(place, *hold((x,)), *blocks)


def device(y, z, core):
    return (y * 4 + z) * 2 + core


def swapped(block):
    return lax.ppermute(block, "dp", [(d, d ^ 1) for d in range(32)])


def sent(block, distance, first_axis):
    route = []
    for y in range(4):
        for z in range(4):
            for core in range(2):
                if (core == 0) == first_axis:
                    there = device(y, (z + distance) % 4, core)
                else:
                    there = device((y + distance) % 4, z, core)
                route.append((device(y, z, core), there))
    return lax.ppermute(block, "dp", route)


def body(
    bottom_stack_feed,
    loss_sensitivity,
    resumes_segment,
    mixing_coefficients,
    fading_log,
    feature_boost,
    attention_maps,
    emission_coefficients,
    feature_addressing,
    feature_payload,
    feature_receptance,
    dividend_memory,
    divisor_memory,
    memory_power_shift,
    prior_normed_lines,
):
    sections = lax.axis_size("section")
    place = jnp.stack([lax.axis_index("section"), lax.axis_index("dp")])
    begins = resumes_segment
    small = (
        mixing_coefficients[0],
        fading_log,
        feature_boost,
        dividend_memory[0],
        divisor_memory[0],
        memory_power_shift[0],
        prior_normed_lines[0],
    )
    weights = (
        attention_maps[0],
        emission_coefficients[0],
        feature_addressing[0],
        feature_payload[0],
        feature_receptance[0],
    )
    rows, held = forward_first(
        place, begins, bottom_stack_feed.reshape(ROWS, WIDTH), small, weights
    )
    for t in range(1, sections):
        rows = lax.ppermute(rows, "section", [(t - 1, t)])
        rows, held = forward_next(t, place, begins, rows, held)
    held, edges = held[:N_BASE], held[N_BASE:]
    grad, held, edges = backward_call(
        sections - 1, place, begins, loss_sensitivity.reshape(ROWS, WIDTH), held, edges
    )
    grad = lax.ppermute(grad, "section", [(sections - 1, sections - 2)])
    (own,) = join(edges[0], swapped(edges[1]))
    blocks = (own,) + tuple(sent(own, k, True) for k in range(1, 4))
    for t in range(sections - 2, 0, -1):
        grad, held, _ = backward_call(t, place, begins, grad, held)
        if t == 1:
            grad, x = mixes(
                lambda s: s != 1, place, blocks, small[0], weights[2], grad
            )
        grad = lax.ppermute(grad, "section", [(t, t - 1)])
    _, held, _ = backward_call(0, place, begins, grad, held)
    entry_grad, keep, send, state_grads, row_grads = held[N_BASE:]
    layer = held[N_CONSTS + N_WEIGHTS + 1]
    x, results = mixes_last(
        lambda s: s == 1, place, blocks, small[0], weights[2], x,
        (layer, entry_grad, state_grads, row_grads),
    )
    layer, entry_grad, *state_grads, row_grads = results
    pieces = join(keep, swapped(send), 4)
    pieces = (pieces[0],) + tuple(sent(pieces[k], k, True) for k in range(1, 4))
    shares = weight_grads(place, x, pieces)
    shares = (shares[0],) + tuple(sent(shares[k], k, False) for k in range(1, 4))
    parts = pl.pallas_call(
        sum_kernel,
        cost_estimate=cost(2),
        out_shape=(array(64, SHARE),) * 4,
        in_specs=[VM] * 4,
        out_specs=(VM,) * 4,
        compiler_params=limit(12),
    )(*shares)
    parts = (parts[0],) + tuple(sent(parts[k], k, True) for k in range(1, 4))
    kept, going, payload = pl.pallas_call(
        gather_kernel,
        cost_estimate=cost(2),
        out_shape=(
            array(32, 5 * WIDTH),
            array(32, 5 * WIDTH),
            array(ROWS, WIDTH, kind=F32),
        ),
        in_specs=[SM] + [VM] * 4,
        out_specs=(VM,) * 3,
    )(place, *parts)
    projection, out_weight, key, gate, vectors, decay, boost = pl.pallas_call(
        final_kernel,
        cost_estimate=cost(2),
        out_shape=(
            array(3, 32, WIDTH, kind=F32),
            array(32, WIDTH, kind=F32),
            array(32, INNER, kind=F32),
            array(32, WIDTH, kind=F32),
            array(9, 1, 32, kind=F32),
            array(1, 32, kind=F32),
            array(1, 32, kind=F32),
        ),
        in_specs=[SM, VM, VM],
        out_specs=(VM,) * 7,
    )(place, kept, swapped(going))
    return (
        layer.reshape(1, SEQS, LENGTH, WIDTH),
        entry_grad.reshape(1, SEQS, LENGTH, WIDTH),
        jnp.swapaxes(vectors, 0, 1),
        decay,
        boost,
        projection[None],
        out_weight[None],
        key[None],
        payload[None],
        gate[None],
        state_grads[0][None],
        state_grads[1][None],
        state_grads[2][None],
        row_grads[None],
    )


def solution(mesh):
    placed = (
        P("dp", None, None),
        P("dp", None, None),
        P("dp"),
        P("section", None, None),
        P("section", None),
        P("section", None),
        P("section", None, None, None),
        P("section", None, None),
        P("section", None, None),
        P("section", None, None),
        P("section", None, None),
        P("section", "dp", None),
        P("section", "dp", None),
        P("section", "dp", None),
        P("section", None, "dp", None),
    )
    return jax.shard_map(
        body,
        mesh=mesh,
        in_specs=placed,
        out_specs=(
            P("section", "dp", None, None),
            P("section", "dp", None, None),
            P("section", None, "dp"),
            P("section", "dp"),
            P("section", "dp"),
            P("section", None, "dp", None),
            P("section", "dp", None),
            P("section", "dp", None),
            P("section", "dp", None),
            P("section", "dp", None),
            P("section", "dp", None),
            P("section", "dp", None),
            P("section", "dp", None),
            P("section", None, "dp", None),
        ),
        check_vma=False,
    )
```

```python
import functools

import jax
import jax.numpy as jnp
from jax import lax
from jax.experimental import pallas as pl
from jax.experimental.pallas import tpu as pltpu
from jax.sharding import PartitionSpec as P

WIDTH = 1024
INNER = 4096
LENGTH = 64
SEQS = 2
ROWS = SEQS * LENGTH
GROUPS = WIDTH // 128
FRESH = -1e30
EPS = 1e-05
F32 = jnp.float32
BF16 = jnp.bfloat16

VM = pl.BlockSpec(memory_space=pltpu.VMEM)
HB = pl.BlockSpec(memory_space=pl.ANY)
SM = pl.BlockSpec(memory_space=pltpu.SMEM)
EDGE = ROWS + 16
QUARTER = 768
SHARES = (1024, 768)


HELD_LIMIT = 14
UNROLL = 4
WINDOW = 4
FLOPS = 10**9
BACK_COST = (14, 1, 14, 14)


def limit(mebibytes):
    return pltpu.CompilerParams(vmem_limit_bytes=mebibytes * 1024 * 1024)

EMISSION, RECEPTANCE = 3, 4
BLOCKS = (5, 4, 4)
WEIGHTS = tuple(((n, WIDTH, WIDTH), BF16) for n in BLOCKS)
CONSTS = (
    ((9, 1, WIDTH), F32),
    ((1, WIDTH), F32),
    ((1, WIDTH), F32),
    ((SEQS, WIDTH), F32),
    ((SEQS, WIDTH), F32),
    ((SEQS, WIDTH), F32),
    ((2, SEQS, WIDTH), BF16),
)
SAVED = (
    ((ROWS, WIDTH), BF16),
    ((ROWS, WIDTH), BF16),
    ((ROWS, INNER), BF16),
    ((5, ROWS, WIDTH), F32),
    ((8, ROWS * GROUPS, 128), F32),
)
EDGES = (
    ((EDGE, 2 * WIDTH), BF16),
    ((EDGE, 2 * WIDTH), BF16),
)
GRADS = (
    ((ROWS, WIDTH), BF16),
    ((4, ROWS, QUARTER), BF16),
    ((4, ROWS, QUARTER), BF16),
    ((4, ROWS, QUARTER), BF16),
    ((4, ROWS, QUARTER), BF16),
    ((3, SEQS, WIDTH), F32),
    ((2, SEQS, WIDTH), F32),
)
N_CONSTS, N_WEIGHTS, N_SAVED, N_EDGES, N_GRADS = 7, 3, 5, 2, 7
N_BASE = N_CONSTS + N_WEIGHTS + N_SAVED


def dot(left, right):
    return jnp.dot(left, right, preferred_element_type=F32)


def against(grad, weight):
    return lax.dot_general(
        grad, weight, (((1,), (1,)), ((), ())), preferred_element_type=F32
    )


def across(left, right):
    return lax.dot_general(
        left, right, (((0,), (0,)), ((), ())), preferred_element_type=F32
    )


def columns_loop(total, size):
    def run(function):
        if total // size <= UNROLL:
            for j in range(total // size):
                function(pl.ds(j * size, size))
            return

        @pl.loop(0, total // size)
        def _(j):
            function(pl.ds(pl.multiple_of(j * size, size), size))

    return run


def coordinates(section, dp):
    dp = dp[0]
    return section[0], dp >> 3, (dp >> 1) & 3, dp & 1


def row_index():
    return lax.broadcasted_iota(jnp.int32, (ROWS, WIDTH), 0)


def normed_rows(rows):
    center = jnp.mean(rows, axis=-1, keepdims=True)
    centered = rows - center
    variance = jnp.mean(centered * centered, axis=-1, keepdims=True)
    scale = lax.rsqrt(variance + EPS)
    return centered * scale, scale


def moved_down(normed, first):
    index = row_index()
    return jnp.where(
        index == 0,
        first[0],
        jnp.where(index == LENGTH, first[1], pltpu.roll(normed, 1, 0)),
    )


def moved_up(rows):
    index = row_index()
    return jnp.where(
        (index == LENGTH - 1) | (index == ROWS - 1),
        0.0,
        pltpu.roll(rows, ROWS - 1, 0),
    )


def first_rows(prior_ref, mix, marks):
    return [prior_ref[mix, s : s + 1, :].astype(F32) * marks[s] for s in range(SEQS)]


def edge_rows(first):
    index = lax.broadcasted_iota(jnp.int32, (EDGE - ROWS, WIDTH), 0)
    return jnp.where(index == 0, first[0], jnp.where(index == 1, first[1], 0.0)).astype(BF16)


def put(core, which, keep_ref, send_ref, at, value):
    @pl.when(core == which)
    def _():
        keep_ref[at] = value

    @pl.when(core != which)
    def _():
        send_ref[at] = value


def to_tokens(ref, block, value):
    ref[pl.ds(block, ROWS, stride=GROUPS), :] = value


def from_tokens(ref, block):
    return ref[pl.ds(block, ROWS, stride=GROUPS), :]


def tile_of(ref, row, small):
    for g in range(GROUPS):
        small[g : g + 1, :] = ref[row : row + 1, g * 128 : (g + 1) * 128]
    return small[...]


def forward_body(core, marks, x_ref, consts, weights, ready, out_ref, saved, edges, scratch):
    streamed = x_ref is None
    vec_ref, fade_ref, boost_ref, num_ref, den_ref, lev_ref, prior_ref = consts
    square, keys, payload = weights
    ent_ref, lay_ref, act_ref, wide_ref, scan_ref = saved
    own_ref, other_ref = edges
    sk, sv, sy, small, mix_ref, hid_ref = scratch
    low, high = slice(0, WIDTH), slice(WIDTH, 2 * WIDTH)
    top, bottom = slice(0, ROWS), slice(ROWS, EDGE)
    if x_ref is not None:
        ent_ref[...] = x_ref[...]
    rows = ent_ref[...].astype(F32)
    unit, _ = normed_rows(rows)
    normed = unit * vec_ref[0] + vec_ref[1]
    first = first_rows(prior_ref, 0, marks)
    below = moved_down(normed, first)
    for j in range(3):
        v = vec_ref[2 + j]
        mix_ref[j] = (normed * v + below * (1.0 - v)).astype(BF16)
    put(core, 0, own_ref, other_ref, (top, high), normed.astype(BF16))
    put(core, 0, own_ref, other_ref, (bottom, high), edge_rows(first))
    for target, j in ((sk, 0), (sv, 1)):
        ready(j)

        @columns_loop(WIDTH, 512)
        def _(at, j=j):
            wide_ref[3, :, at] = dot(mix_ref[j], square[j, :, at])

        for g in range(GROUPS):
            to_tokens(target, g, wide_ref[3, :, g * 128 : (g + 1) * 128])
    ready(2)

    @columns_loop(WIDTH, 512)
    def _(at):
        wide_ref[0, :, at] = jax.nn.sigmoid(dot(mix_ref[2], square[2, :, at]))

    rate = jnp.exp(tile_of(fade_ref, 0, small))
    boost = tile_of(boost_ref, 0, small)
    start = []
    for s in range(SEQS):
        level = tile_of(lev_ref, s, small)
        start.append(jnp.where(marks[s] > 0.0, level, FRESH))
        start.append(tile_of(num_ref, s, small) * marks[s])
        start.append(tile_of(den_ref, s, small) * marks[s])

    def token(t, carry):
        carry_next = []
        for s in range(SEQS):
            level, num, den = carry[3 * s : 3 * s + 3]
            at = pl.ds(pl.multiple_of((t + LENGTH * s) * GROUPS, GROUPS), GROUPS)
            key, value = sk[at, :], sv[at, :]
            boosted = boost + key
            decayed = jnp.exp(-jnp.abs(level - boosted))
            state_on_top = level > boosted
            old = jnp.where(state_on_top, 1.0, decayed)
            fresh = jnp.where(state_on_top, decayed, 1.0)
            inverse = 1.0 / (old * den + fresh)
            old = old * inverse
            fresh = fresh * inverse
            result = old * num + fresh * value
            faded = level - rate
            level = jnp.maximum(faded, key)
            decayed = jnp.exp(-jnp.abs(faded - key))
            state_on_top = faded > key
            keep = jnp.where(state_on_top, 1.0, decayed)
            new = jnp.where(state_on_top, decayed, 1.0)
            sy[at, :] = result
            scan_ref[0, at, :] = old
            scan_ref[1, at, :] = fresh
            scan_ref[2, at, :] = value - result
            scan_ref[3, at, :] = keep
            scan_ref[4, at, :] = new
            scan_ref[5, at, :] = num
            scan_ref[6, at, :] = den
            scan_ref[7, at, :] = value
            carry_next += [level, keep * num + new * value, keep * den + new]
        return tuple(carry_next)

    def tokens(block, carry):
        for j in range(8):
            carry = token(block * 8 + j, carry)
        return carry

    lax.fori_loop(0, LENGTH // 8, tokens, tuple(start))
    for g in range(GROUPS):
        at = slice(g * 128, (g + 1) * 128)
        gate = wide_ref[0, :, at]
        mixed = gate * from_tokens(sy, g)
        mix_ref[0, :, at] = mixed.astype(BF16)
        wide_ref[1, :, at] = mixed * (1.0 - gate)
    put(core, 1, own_ref, other_ref, (top, high), mix_ref[0])
    ready(3)

    @columns_loop(WIDTH, 512)
    def _(at):
        wide_ref[2, :, at] = ent_ref[:, at].astype(F32) + dot(mix_ref[0], square[EMISSION, :, at])

    unit, _ = normed_rows(wide_ref[2])
    normed = unit * vec_ref[5] + vec_ref[6]
    first = first_rows(prior_ref, 1, marks)
    below = moved_down(normed, first)
    for j in range(2):
        v = vec_ref[7 + j]
        mix_ref[1 + j] = (normed * v + below * (1.0 - v)).astype(BF16)
    for ref in edges:
        ref[top, low] = normed.astype(BF16)
        ref[bottom, low] = edge_rows(first)
    ready(4)

    @columns_loop(WIDTH, 512)
    def _(at):
        wide_ref[4, :, at] = jax.nn.sigmoid(dot(mix_ref[2], square[RECEPTANCE, :, at]))

    def hidden(j):
        at = pl.ds(pl.multiple_of(j * 512, 512), 512)
        within = pl.ds(pl.multiple_of((j & 1) * 512, 512), 512)
        active = jnp.maximum(dot(mix_ref[1], keys[j >> 1, :, within]), 0.0)
        act_ref[:, at] = active.astype(BF16)
        hid_ref[:, at] = (active * active).astype(BF16)

    def leave(at, channel):
        wide_ref[3, :, at] = channel
        lay_ref[:, at] = (wide_ref[2, :, at] + wide_ref[4, :, at] * channel).astype(BF16)

    def part(b, at):
        return dot(hid_ref[:, b * WIDTH : (b + 1) * WIDTH], payload[b, :, at])

    if not streamed:
        pl.loop(0, INNER // 512)(hidden)

        @columns_loop(WIDTH, 256)
        def _(at):
            leave(at, part(0, at) + part(1, at) + part(2, at) + part(3, at))

    else:
        for b in range(4):
            ready(5 + b)
            pl.loop(2 * b, 2 * b + 2)(hidden)
        for b in range(4):
            ready(9 + b)

            @columns_loop(WIDTH, 512)
            def _(at, b=b):
                channel = part(b, at)
                if b > 0:
                    channel = channel + wide_ref[3, :, at]
                if b < 3:
                    wide_ref[3, :, at] = channel
                else:
                    leave(at, channel)

    out_ref[...] = lay_ref[...]


def groups(refs, *sizes):
    cut, at = [], 0
    for size in sizes:
        cut.append(refs[at : at + size])
        at += size
    return cut + [refs[at:]]


def weight_pieces(maps, emission, key, payload, receptance):
    pieces = [maps.at[j] for j in range(3)] + [emission, receptance]
    for b in range(4):
        pieces.append(key.at[:, pl.ds(b * WIDTH, WIDTH)])
    for b in range(4):
        pieces.append(payload.at[pl.ds(b * WIDTH, WIDTH), :])
    return pieces


def forward_first_kernel(section, dp, begins, x_ref, *refs):
    small_in, hbm, (out_ref,), consts, kept, saved, edges, rest = groups(
        refs, N_CONSTS, 5, 1, N_CONSTS, N_WEIGHTS, N_SAVED, N_EDGES
    )
    section, _, _, core = coordinates(section, dp)
    sem, small_sem = rest[-2:]
    copies = [
        pltpu.make_async_copy(source, target, sem.at[i])
        for i, (source, target) in enumerate(
            zip(
                weight_pieces(*hbm),
                [ref.at[i] for ref, n in zip(kept, BLOCKS) for i in range(n)],
            )
        )
    ]
    arriving = [pltpu.make_async_copy(x_ref, saved[0], small_sem.at[N_CONSTS])]
    for i in range(N_CONSTS):
        arriving.append(pltpu.make_async_copy(small_in[i], consts[i], small_sem.at[i]))
    for c in arriving + copies[:WINDOW]:
        c.start()
    for c in arriving:
        c.wait()

    def ready(i):
        copies[i].wait()
        if i + WINDOW < len(copies):
            copies[i + WINDOW].start()

    @pl.when(section == 0)
    def _():
        marks = [begins[s].astype(F32) for s in range(SEQS)]
        forward_body(
            core, marks, None, consts, kept, ready, out_ref, saved, edges, rest[:-2]
        )

    @pl.when(section != 0)
    def _():
        for c in copies[WINDOW:]:
            c.start()
        for c in copies:
            c.wait()


def flip(ref):
    side = 256
    for i in range(WIDTH // side):
        for j in range(i + 1):
            one = (slice(i * side, (i + 1) * side), slice(j * side, (j + 1) * side))
            two = (one[1], one[0])
            first = ref[one].T
            if i != j:
                ref[one] = ref[two].T
            ref[two] = first


def forward_kernel(layer, section, dp, begins, x_ref, *refs):
    _, (out_ref,), consts, kept, saved, edges, scratch = groups(
        refs, N_BASE + N_EDGES, 1, N_CONSTS, N_WEIGHTS, N_SAVED, N_EDGES
    )
    section, _, _, core = coordinates(section, dp)

    @pl.when(section == layer)
    def _():
        marks = [begins[s].astype(F32) for s in range(SEQS)]
        forward_body(
            core, marks, x_ref, consts, kept, lambda i: None, out_ref, saved, edges, scratch
        )

    @pl.when(section == layer - 1)
    def _():
        for ref, n in zip(kept, BLOCKS):

            @pl.loop(0, n)
            def _(i, ref=ref):
                flip(ref.at[i])


def norm_back(rows, gain, offset, first, parts, vec_out, prior_out, marks):
    unit, scale = normed_rows(rows)
    normed = unit * gain + offset
    change = normed - moved_down(normed, first)
    up, stay = None, None
    for grad, weight, row in parts:
        vec_out(row, jnp.sum(grad * change, axis=0, keepdims=True))
        kept = grad * weight
        passed = grad - kept
        stay = kept if stay is None else stay + kept
        up = passed if up is None else up + passed
    for s in range(SEQS):
        prior_out(s, up[s * LENGTH : s * LENGTH + 1, :] * marks[s])
    grad = stay + moved_up(up)
    return unit, scale, grad


def backward_kernel(first, flipped, layer, section, dp, begins, dy_ref, *refs):
    _, (out_ref,), consts, kept, saved, grads, scratch = groups(
        refs, N_BASE + (0 if first else N_GRADS), 1, N_CONSTS, N_WEIGHTS, N_SAVED, N_GRADS
    )
    vec_ref, fade_ref, prior_ref = consts[0], consts[1], consts[6]
    square, keys, payload = kept
    ent_ref, lay_ref, act_ref, wide_ref, scan_ref = saved
    ing_ref, keep_one, send_one, keep_two, send_two, stg_ref, rowg_ref = grads
    sg, sdk, sdv, small, wide, wide_two, wide_three, wide_four, dys_ref, dhp_ref, vecg_ref = scratch
    section, y, z, core = coordinates(section, dp)
    everything = slice(None)

    def vec_out(row, value):
        vecg_ref[row : row + 1, :] = value

    def share(which, column, size, quarter, value):
        distance = (quarter - jnp.where(which == 1, y, z)) & 3
        pair = (keep_one, send_one) if column < QUARTER else (keep_two, send_two)
        column = column % QUARTER
        put(core, which, *pair, (distance, everything, slice(column, column + size)), value)

    def pull(grad, blocks, i, at):
        if flipped:
            return dot(grad, blocks[i, :, at])
        return against(grad, blocks[i, at, :])

    def through_payload(grad, j):
        return pull(grad, payload, j >> 1, pl.ds(pl.multiple_of((j & 1) * 512, 512), 512))

    def through_key(grad_ref, j):
        at = pl.ds(pl.multiple_of(j * 256, 256), 256)
        total = None
        for b in range(4):
            part = pull(grad_ref[:, b * WIDTH : (b + 1) * WIDTH], keys, b, at)
            total = part if total is None else total + part
        return total

    @pl.when(section == layer)
    def _():
        marks = [begins[s].astype(F32) for s in range(SEQS)]
        dy = dy_ref[...].astype(F32)
        gate = wide_ref[4]
        through = dy * gate
        dys_ref[4] = through.astype(BF16)
        dys_ref[5] = (through * wide_ref[3] * (1.0 - gate)).astype(BF16)

        @pl.loop(0, INNER // 512, unroll=2)
        def _(j):
            at = pl.ds(pl.multiple_of(j * 512, 512), 512)
            part = through_payload(dys_ref[4], j)
            piece = (2.0 * act_ref[:, at].astype(F32) * part).astype(BF16)
            dhp_ref[:, at] = piece
            share(j >> 2, 0, 512, j & 3, piece)

        for q in range(4):
            at = slice(q * 256, (q + 1) * 256)
            share(0, 512, 256, q, dys_ref[4, :, at])
            share(1, 512, 256, q, dys_ref[4, :, at])
            share(1, 768, 256, q, dys_ref[5, :, at])

        @pl.loop(0, WIDTH // 256)
        def _(j):
            at = pl.ds(pl.multiple_of(j * 256, 256), 256)
            wide[:, at] = through_key(dhp_ref, j)
            wide_two[:, at] = pull(dys_ref[5], square, RECEPTANCE, at)

        def prior_two(s, value):
            rowg_ref[1, s : s + 1, :] = value

        gain = vec_ref[5]
        unit, scale, grad = norm_back(
            wide_ref[2], gain, vec_ref[6], first_rows(prior_ref, 1, marks),
            ((wide[...], vec_ref[7], 7), (wide_two[...], vec_ref[8], 8)),
            vec_out, prior_two, marks,
        )
        vec_out(5, jnp.sum(grad * unit, axis=0, keepdims=True))
        vec_out(6, jnp.sum(grad, axis=0, keepdims=True))
        grad = grad * gain
        mean = jnp.mean(grad, axis=-1, keepdims=True)
        along = jnp.mean(grad * unit, axis=-1, keepdims=True)
        middle = dy_ref[...].astype(F32) + scale * (grad - mean - unit * along)
        wide_three[...] = middle
        dys_ref[3] = middle.astype(BF16)

        for q in range(4):
            at = pl.ds(q * 256, 256)
            share(1, 1024, 256, q, dys_ref[3, :, at])
            part = pull(dys_ref[3], square, EMISSION, at)
            dys_ref[2, :, at] = (part * wide_ref[1, :, at]).astype(BF16)
            wide[:, at] = part * wide_ref[0, :, at]

        for g in range(GROUPS):
            to_tokens(sg, g, wide[:, g * 128 : (g + 1) * 128])

        zero = jnp.zeros((GROUPS, 128), F32)

        def token(t, carry):
            carry_next = []
            boosted, faded = carry[4], carry[5]
            for s in range(SEQS):
                dnum, dden = carry[2 * s : 2 * s + 2]
                at = pl.ds(pl.multiple_of((t + LENGTH * s) * GROUPS, GROUPS), GROUPS)
                g = sg[at, :]
                value = scan_ref[7, at, :]
                beyond = scan_ref[2, at, :]
                keep = scan_ref[3, at, :]
                new = scan_ref[4, at, :]
                from_old = scan_ref[0, at, :] * g
                from_new = scan_ref[1, at, :] * g
                direct = from_new * beyond
                boosted = boosted + direct
                sdv[at, :] = from_new + new * dnum
                sdk[at, :] = direct + new * (dnum * value + dden)
                faded = faded - keep * (dnum * scan_ref[5, at, :] + dden * scan_ref[6, at, :])
                carry_next += [
                    from_old + keep * dnum,
                    keep * dden - from_old * (value - beyond),
                ]
            return tuple(carry_next) + (boosted, faded)

        def tokens(block, carry):
            for j in range(8):
                carry = token(LENGTH - 1 - block * 8 - j, carry)
            return carry

        ends = lax.fori_loop(0, LENGTH // 8, tokens, (zero,) * 6)

        def spread(put_piece, value):
            small[...] = value
            for g in range(GROUPS):
                put_piece(slice(g * 128, (g + 1) * 128), small[g : g + 1, :])

        for s in range(SEQS):
            dnum, dden = ends[2 * s : 2 * s + 2]
            at = pl.ds(LENGTH * s * GROUPS, GROUPS)
            moved = dnum * scan_ref[5, at, :] + dden * scan_ref[6, at, :]
            for k, value in enumerate((dnum, dden, moved)):

                def put_state(cols, piece, k=k, s=s):
                    stg_ref[k, s : s + 1, cols] = piece

                spread(put_state, value * marks[s])

        def put_decay(cols, piece):
            vecg_ref[9:10, cols] = piece

        def put_boost(cols, piece):
            vecg_ref[10:11, cols] = piece

        spread(put_decay, ends[5])
        vecg_ref[9:10, :] = vecg_ref[9:10, :] * jnp.exp(fade_ref[0:1, :])
        spread(put_boost, ends[4])

        for g in range(GROUPS):
            at = slice(g * 128, (g + 1) * 128)
            dys_ref[0, :, at] = from_tokens(sdk, g).astype(BF16)
            dys_ref[1, :, at] = from_tokens(sdv, g).astype(BF16)
        for q in range(4):
            at = slice(q * 256, (q + 1) * 256)
            for j in range(3):
                share(0, 768 + 256 * j, 256, q, dys_ref[j, :, at])

        rows = ent_ref[...].astype(F32)
        pulled = (wide, wide_two, wide_four)
        for j in range(3):

            @columns_loop(WIDTH, 512)
            def _(at, j=j):
                pulled[j][:, at] = pull(dys_ref[j], square, j, at)


        def prior_one(s, value):
            rowg_ref[0, s : s + 1, :] = value

        gain = vec_ref[0]
        unit, scale, grad = norm_back(
            rows, gain, vec_ref[1], first_rows(prior_ref, 0, marks),
            [(pulled[j][...], vec_ref[2 + j], 2 + j) for j in range(3)],
            vec_out, prior_one, marks,
        )
        vec_out(0, jnp.sum(grad * unit, axis=0, keepdims=True))
        vec_out(1, jnp.sum(grad, axis=0, keepdims=True))
        for q in range(4):
            packed = jnp.concatenate(
                [vecg_ref[:, b * 256 : (b + 1) * 256] for b in range(4)], axis=0
            ).astype(BF16)
            put(
                core, 1, keep_two, send_two,
                (q, slice(0, 64), slice(512, 768)), packed,
            )
        grad = grad * gain
        mean = jnp.mean(grad, axis=-1, keepdims=True)
        along = jnp.mean(grad * unit, axis=-1, keepdims=True)
        entry = (wide_three[...] + scale * (grad - mean - unit * along)).astype(BF16)
        ing_ref[...] = entry
        out_ref[...] = entry


def join_edges_kernel(first, second, out, sem):
    copies = [
        pltpu.make_async_copy(ref, out.at[pl.ds(h * EDGE, EDGE), :], sem.at[h])
        for h, ref in enumerate((first, second))
    ]
    for c in copies:
        c.start()
    for c in copies:
        c.wait()


def join_kernel(first, second, *outs):
    for k in range(4):
        outs[k][:ROWS, :] = first[k]
        outs[k][ROWS:, :] = second[k]


def mixes_kernel(chosen, section, dp, own, one, two, three, vec_ref, wa, *refs):
    x_one, x_two, *scratch = refs[-10:]
    edge, wide, stage, hidden, first_mix, edge_sem, wide_sem, out_sem = scratch
    section, _, _, core = coordinates(section, dp)

    @pl.when(chosen(section))
    def _():
        def load(n):
            block = (own, one, two, three)[n // 2]
            return pltpu.make_async_copy(
                block.at[pl.ds(n % 2 * EDGE, EDGE), :], edge.at[n], edge_sem.at[n]
            )

        def columns(u):
            return [
                pltpu.make_async_copy(
                    wa.at[:, pl.ds(pl.multiple_of((16 * u + 2 * j + core) * 128, 128), 128)],
                    wide.at[:, pl.ds(j * 128, 128)],
                    wide_sem.at[j],
                )
                for j in range(8)
            ]

        def out_mixes(n):
            rows = pl.ds(pl.multiple_of(n * ROWS, ROWS), ROWS)
            return pltpu.make_async_copy(
                stage.at[n & 1], x_two.at[:, rows, :], out_sem.at[n & 1]
            )

        def out_hidden(u, t):
            cols = pl.ds(pl.multiple_of(t * 256, 256), 256)
            return pltpu.make_async_copy(
                hidden.at[t & 1], x_one.at[u, :, cols], out_sem.at[2 + (t & 1)]
            )

        out_first = pltpu.make_async_copy(first_mix, x_one.at[2], out_sem.at[4])

        def mix(normed, below, j):
            v = vec_ref[j]
            return (normed * v + below * (1.0 - v)).astype(BF16)

        for n in range(8):
            load(n).start()
        for c in columns(0):
            c.start()
        for n in range(8):
            load(n).wait()

        @pl.loop(0, 8)
        def _(n):
            @pl.when(n >= 2)
            def _():
                out_mixes(n - 2).wait()

            block, here = edge.at[n], stage.at[n & 1]

            def parts(c):
                cols = slice(c * WIDTH, (c + 1) * WIDTH)
                normed = block[:ROWS, cols].astype(F32)
                first = block[ROWS:, cols].astype(F32)
                return normed, moved_down(normed, (first[0:1, :], first[1:2, :]))

            normed, below = parts(0)
            first_mix[pl.ds(pl.multiple_of(n * ROWS, ROWS), ROWS), :] = mix(normed, below, 7)

            @pl.when(core == 0)
            def _():
                normed, below = parts(1)
                for j in range(3):
                    here[j] = mix(normed, below, 2 + j)

            @pl.when(core == 1)
            def _():
                here[0] = mix(normed, below, 8)
                here[1] = block[:ROWS, WIDTH:]

            out_mixes(n).start()

        out_first.start()
        for u in range(2):
            for c in columns(u):
                c.wait()

            @pl.loop(0, 4)
            def _(t, u=u):
                @pl.when(t >= 2)
                def _():
                    out_hidden(u, t - 2).wait()

                cols = pl.ds(pl.multiple_of(t * 256, 256), 256)
                for r in range(4):
                    rows = slice(r * 256, (r + 1) * 256)
                    active = jnp.maximum(dot(first_mix[rows, :], wide[:, cols]), 0.0)
                    hidden[t & 1, rows, :] = (active * active).astype(BF16)
                out_hidden(u, t).start()

            if u == 0:
                for c in columns(1):
                    c.start()
            for t in (2, 3):
                out_hidden(u, t).wait()
        for n in (6, 7):
            out_mixes(n).wait()
        out_first.wait()


def drain_kernel(layer, entry, states, firsts, *refs):
    results, sem = refs[:-1], refs[-1]
    sources = (layer, entry) + tuple(states.at[k] for k in range(3)) + (firsts,)
    copies = [
        pltpu.make_async_copy(source, target, sem.at[i])
        for i, (source, target) in enumerate(zip(sources, results))
    ]
    for c in copies:
        c.start()
    for c in copies:
        c.wait()


def row_starts(y, z, core):
    starts = []
    for there in range(16):
        along_y, along_z = (there // 4 - y) & 3, (there % 4 - z) & 3
        summed = jnp.where(core == 0, along_y, along_z)
        joined = jnp.where(core == 0, along_z, along_y)
        starts.append(pl.multiple_of(summed * 256 + joined * 64, 64))
    return starts


def weight_kernel(second, section, dp, x_ref, *refs):
    blocks, outs = refs[:4], refs[4:8]
    dy, share = refs[8:]
    _, y, z, core = coordinates(section, dp)
    for k in range(4):
        dy[k * 2 * ROWS : (k + 1) * 2 * ROWS, :] = blocks[k][...]
    starts = row_starts(y, z, core)

    def unit(u, size, source, target):
        for c in range(0, WIDTH, 256):
            part = across(x_ref[u, :, c : c + 256], dy[:, source : source + size]).astype(BF16)
            for b in range(4):
                share[pl.ds(starts[c // 64 + b], 64), target : target + size] = part[
                    b * 64 : (b + 1) * 64, :
                ]

    if not second:
        unit(2, 512, 0, 0)
        for u in range(2):
            for c in range(0, WIDTH, 256):
                part = across(x_ref[u, :, c : c + 256], dy[:, 512:768]).astype(BF16)
                for b in range(2):
                    start = starts[(u * WIDTH + c) // 128 + b]
                    for half in range(2):
                        share[pl.ds(start, 64), 512 + half * 256 : 768 + half * 256] = part[
                            b * 128 + half * 64 : b * 128 + (half + 1) * 64, :
                        ]
    else:
        unit(0, 256, 0, 0)
        unit(1, 256, 256, 256)

        @pl.when(core == 0)
        def _():
            unit(2, 256, 512, 512)

        @pl.when(core == 1)
        def _():
            total = jnp.zeros((64, 256), F32)
            for d in range(8):
                total = total + dy[d * ROWS : d * ROWS + 64, 512:768].astype(F32)
            for b in range(4):
                piece = jnp.concatenate(
                    [total[b * 16 : (b + 1) * 16, :], jnp.zeros((112, 256), F32)], axis=0
                ).T.astype(BF16)
                for e in range(4):
                    at = pl.ds(starts[b * 4 + e], 64)
                    share[at, 512:640] = piece[e * 64 : (e + 1) * 64, :]
                    share[at, 640:768] = jnp.zeros((64, 128), BF16)

    for k in range(4):
        outs[k][...] = share[k * 256 : (k + 1) * 256, :]


def sum_kernel(own, one, two, three, *outs):
    total = own[...].astype(F32) + one[...].astype(F32) + two[...].astype(F32)
    total = (total + three[...].astype(F32)).astype(BF16)
    for k in range(4):
        outs[k][...] = total[k * 64 : (k + 1) * 64, :]


def gather_kernel(second, section, dp, own, one, two, three, keep_ref, send_ref, *payload):
    _, y, z, core = coordinates(section, dp)
    here = jnp.where(core == 0, z, y)
    mine = pl.multiple_of(core * 32, 32)
    theirs = pl.multiple_of(32 - core * 32, 32)
    for k, ref in enumerate((own, one, two, three)):
        quarter = (here - k) & 3
        for rows, target in ((mine, keep_ref), (theirs, send_ref)):
            if not second:
                at = pl.ds(pl.multiple_of(quarter * 512, 512), 512)
                target[:, at] = ref[pl.ds(rows, 32), 0:512]
            else:
                for u in range(3):
                    at = pl.ds(pl.multiple_of(u * WIDTH + quarter * 256, 256), 256)
                    target[:, at] = ref[pl.ds(rows, 32), u * 256 : (u + 1) * 256]
        if not second:
            at = pl.ds(pl.multiple_of(quarter * 256, 256), 256)
            for half in range(2):
                payload[0][half * 64 : (half + 1) * 64, at] = ref[
                    :, 512 + half * 256 : 768 + half * 256
                ].astype(F32)


def final_kernel(second, section, dp, kept, come, *outs):
    core = coordinates(section, dp)[3]

    def write(set_zero, set_one):
        if not second:
            outs[0][:, 0:2048] = set_zero[...].astype(F32)
            outs[0][:, 2048:4096] = set_one[...].astype(F32)
            return
        proj_ref, out_ref, gate_ref, vec_ref, dec_ref, boo_ref = outs
        for u in range(3):
            proj_ref[u] = set_zero[:, u * WIDTH : (u + 1) * WIDTH].astype(F32)
        gate_ref[...] = set_one[:, 0:1024].astype(F32)
        out_ref[...] = set_one[:, 1024:2048].astype(F32)
        vectors = set_one[:, 2048:2176].astype(F32).T
        for j in range(9):
            vec_ref[j] = vectors[j : j + 1, :]
        dec_ref[...] = vectors[9:10, :]
        boo_ref[...] = vectors[10:11, :]

    @pl.when(core == 0)
    def _():
        write(kept, come)

    @pl.when(core == 1)
    def _():
        write(come, kept)


def plain(shapes):
    return tuple(jax.ShapeDtypeStruct(s, d) for s, d in shapes)


def in_vmem(shapes):
    return tuple(pltpu.VMEM(s, d) for s, d in shapes)


def hold(arrays):
    return tuple(pltpu.with_memory_space_constraint(a, pltpu.VMEM) for a in arrays)


def in_hbm(*arrays):
    return tuple(pltpu.with_memory_space_constraint(a, pltpu.HBM) for a in arrays)


def array(*shape, kind=BF16):
    return jax.ShapeDtypeStruct(shape, kind)


ROWS_OUT = array(ROWS, WIDTH)
TOKENS = pltpu.VMEM((ROWS * GROUPS, 128), F32)
SMALL = pltpu.VMEM((GROUPS, 128), F32)
WIDE = pltpu.VMEM((ROWS, WIDTH), F32)
FORWARD_SCRATCH = [
    TOKENS, TOKENS, TOKENS, SMALL,
    pltpu.VMEM((3, ROWS, WIDTH), BF16),
    pltpu.VMEM((ROWS, INNER), BF16),
]
DMA = pltpu.SemaphoreType.DMA


def forward_first(place, begins, rows, small, weights):
    shapes = CONSTS + WEIGHTS + SAVED + EDGES
    results = pl.pallas_call(
        forward_first_kernel,
        cost_estimate=cost(12),
        out_shape=(ROWS_OUT,) + in_vmem(shapes),
        in_specs=[SM] * 3 + [HB] * (1 + N_CONSTS + 5),
        out_specs=(VM,) * (1 + len(shapes)),
        scratch_shapes=FORWARD_SCRATCH + [DMA((13,)), DMA((N_CONSTS + 1,))],
        compiler_params=limit(HELD_LIMIT),
    )(*place, begins, *in_hbm(rows, *small, *weights))
    return results[0], results[1:]


def forward_next(layer, place, begins, rows, held):
    shapes = CONSTS + WEIGHTS + SAVED + EDGES
    results = pl.pallas_call(
        functools.partial(forward_kernel, layer),
        cost_estimate=cost(10),
        out_shape=(ROWS_OUT,) + plain(shapes),
        in_specs=[SM] * 3 + [VM] * (1 + len(shapes)),
        out_specs=(VM,) * (1 + len(shapes)),
        input_output_aliases={4 + i: 1 + i for i in range(len(shapes))},
        scratch_shapes=FORWARD_SCRATCH,
        compiler_params=limit(HELD_LIMIT),
    )(*place, begins, *hold((rows,)), *hold(held))
    return results[0], results[1:]


def backward_call(layer, place, begins, grad, held):
    first = len(held) == N_BASE
    base = CONSTS + WEIGHTS + SAVED
    results = pl.pallas_call(
        functools.partial(backward_kernel, first, not first, layer),
        cost_estimate=cost(BACK_COST[layer]),
        out_shape=(ROWS_OUT,) + plain(base) + (in_vmem(GRADS) if first else plain(GRADS)),
        in_specs=[SM] * 3 + [VM] * (1 + len(held)),
        out_specs=(VM,) * (1 + N_BASE + N_GRADS),
        input_output_aliases={4 + i: 1 + i for i in range(len(held))},
        scratch_shapes=[
            TOKENS, TOKENS, TOKENS, SMALL, WIDE, WIDE, WIDE, WIDE,
            pltpu.VMEM((6, ROWS, WIDTH), BF16),
            pltpu.VMEM((ROWS, INNER), BF16),
            pltpu.VMEM((16, WIDTH), F32),
        ],
        compiler_params=limit(HELD_LIMIT),
    )(*place, begins, *hold((grad,)), *hold(held))
    return results[0], results[1:]


def cost(microseconds):
    return pl.CostEstimate(
        flops=int(microseconds * FLOPS), bytes_accessed=0, transcendentals=0
    )


def join_edges(first, second):
    return pl.pallas_call(
        join_edges_kernel,
        cost_estimate=cost(3),
        out_shape=pltpu.HBM((2 * EDGE, 2 * WIDTH), BF16),
        in_specs=[VM, VM],
        out_specs=HB,
        scratch_shapes=[DMA((2,))],
        compiler_params=limit(1),
    )(*hold((first, second)))


def join(first, second):
    return pl.pallas_call(
        join_kernel,
        cost_estimate=cost(1),
        out_shape=in_vmem((((2 * ROWS, QUARTER), BF16),) * 4),
        in_specs=[VM, VM],
        out_specs=(VM,) * 4,
        compiler_params=limit(HELD_LIMIT),
    )(*hold((first, second)))


MIXES_SCRATCH = [
    pltpu.VMEM((8, EDGE, 2 * WIDTH), BF16),
    pltpu.VMEM((WIDTH, WIDTH), BF16),
    pltpu.VMEM((2, 3, ROWS, WIDTH), BF16),
    pltpu.VMEM((2, 8 * ROWS, 256), BF16),
    pltpu.VMEM((8 * ROWS, WIDTH), BF16),
    DMA((8,)),
    DMA((8,)),
    DMA((5,)),
]
X_HALF = pltpu.HBM((3, 8 * ROWS, WIDTH), BF16)


def mixes(chosen, place, blocks, vec, wa, passed):
    made = len(passed) == 2
    shapes = (X_HALF, X_HALF)
    if not made:
        shapes = tuple(array(*a.shape, kind=a.dtype) for a in passed) + shapes
    return pl.pallas_call(
        functools.partial(mixes_kernel, chosen),
        cost_estimate=cost(15),
        out_shape=shapes,
        in_specs=[SM] * 2 + [HB] * 4 + [VM] + [HB] * (1 + len(passed)),
        out_specs=(HB,) * len(shapes),
        input_output_aliases={8 + i: i for i in range(len(passed))},
        scratch_shapes=MIXES_SCRATCH,
        compiler_params=limit(HELD_LIMIT),
    )(*place, *in_hbm(*blocks), vec, *in_hbm(wa), *(in_hbm(*passed) if made else passed))


def drained(layer, entry, states, firsts):
    rows, state = pltpu.HBM((ROWS, WIDTH), BF16), pltpu.HBM((SEQS, WIDTH), F32)
    return pl.pallas_call(
        drain_kernel,
        cost_estimate=cost(1),
        out_shape=(rows, rows, state, state, state, pltpu.HBM((2, SEQS, WIDTH), F32)),
        in_specs=[HB] * 4,
        out_specs=(HB,) * 6,
        scratch_shapes=[DMA((6,))],
        compiler_params=limit(1),
    )(layer, entry, states, firsts)


def weight_grads(second, place, x, blocks):
    columns = SHARES[second]
    return pl.pallas_call(
        functools.partial(weight_kernel, second),
        cost_estimate=cost(4),
        out_shape=in_vmem((((2 * ROWS, columns), BF16),) * 4),
        in_specs=[SM] * 2 + [VM] * 5,
        out_specs=(VM,) * 4,
        scratch_shapes=[
            pltpu.VMEM((8 * ROWS, QUARTER), BF16),
            pltpu.VMEM((8 * ROWS, columns), BF16),
        ],
        compiler_params=limit(HELD_LIMIT),
    )(*place, *hold((x, *blocks)))


def summed(second, shares):
    return pl.pallas_call(
        sum_kernel,
        cost_estimate=cost(1),
        out_shape=in_vmem((((64, SHARES[second]), BF16),) * 4),
        in_specs=[VM] * 4,
        out_specs=(VM,) * 4,
        compiler_params=limit(HELD_LIMIT),
    )(*hold(shares))


def gathered(second, place, parts):
    outs = in_vmem((((32, 3 * WIDTH), BF16),) * 2)
    if not second:
        outs = in_vmem((((32, 2 * WIDTH), BF16),) * 2) + (pltpu.HBM((ROWS, WIDTH), F32),)
    return pl.pallas_call(
        functools.partial(gather_kernel, second),
        cost_estimate=cost(1),
        out_shape=outs,
        in_specs=[SM] * 2 + [VM] * 4,
        out_specs=(VM,) * len(outs),
        compiler_params=limit(HELD_LIMIT),
    )(*place, *hold(parts))


def final(second, place, kept, come):
    outs = (
        array(3, 32, WIDTH, kind=F32),
        array(32, WIDTH, kind=F32),
        array(32, WIDTH, kind=F32),
        array(9, 1, 32, kind=F32),
        array(1, 32, kind=F32),
        array(1, 32, kind=F32),
    )
    if not second:
        outs = (array(32, INNER, kind=F32),)
    return pl.pallas_call(
        functools.partial(final_kernel, second),
        cost_estimate=cost(1),
        out_shape=outs,
        in_specs=[SM] * 2 + [VM] * 2,
        out_specs=(VM,) * len(outs),
        compiler_params=limit(HELD_LIMIT),
    )(*place, *hold((kept, come)))


def device(y, z, core):
    return (y * 4 + z) * 2 + core


def swapped(block):
    return lax.ppermute(block, "dp", [(d, d ^ 1) for d in range(32)])


def sent(block, distance, first_axis):
    route = []
    for y in range(4):
        for z in range(4):
            for core in range(2):
                if (core == 0) == first_axis:
                    there = device(y, (z + distance) % 4, core)
                else:
                    there = device((y + distance) % 4, z, core)
                route.append((device(y, z, core), there))
    return lax.ppermute(block, "dp", route)


def body(
    bottom_stack_feed,
    loss_sensitivity,
    resumes_segment,
    mixing_coefficients,
    fading_log,
    feature_boost,
    attention_maps,
    emission_coefficients,
    feature_addressing,
    feature_payload,
    feature_receptance,
    dividend_memory,
    divisor_memory,
    memory_power_shift,
    prior_normed_lines,
):
    sections = lax.axis_size("section")
    place = (lax.axis_index("section")[None], lax.axis_index("dp")[None])
    begins = resumes_segment
    vec = jnp.swapaxes(mixing_coefficients, 0, 1)
    small = (
        vec,
        fading_log,
        feature_boost,
        dividend_memory[0],
        divisor_memory[0],
        memory_power_shift[0],
        prior_normed_lines[0],
    )
    weights = (
        attention_maps[0],
        emission_coefficients[0],
        feature_addressing[0],
        feature_payload[0],
        feature_receptance[0],
    )
    rows, held = forward_first(
        place, begins, bottom_stack_feed.reshape(ROWS, WIDTH), small, weights
    )
    for t in range(1, sections):
        rows = lax.ppermute(rows, "section", [(t - 1, t)])
        rows, held = forward_next(t, place, begins, rows, held)
    held, edges = held[:N_BASE], held[N_BASE:]
    grad, held = backward_call(
        sections - 1, place, begins, loss_sensitivity.reshape(ROWS, WIDTH), held
    )
    grad = lax.ppermute(grad, "section", [(sections - 1, sections - 2)])
    own = join_edges(edges[0], swapped(edges[1]))
    blocks = (own,) + tuple(sent(own, k, True) for k in range(1, 4))
    for t in range(sections - 2, 0, -1):
        grad, held = backward_call(t, place, begins, grad, held)
        if t == 1:
            grad, *x = mixes(lambda s: s != 1, place, blocks, vec, weights[2], (grad,))
        grad = lax.ppermute(grad, "section", [(t, t - 1)])
    _, held = backward_call(0, place, begins, grad, held)
    entry_grad, *row_sets, state_grads, row_grads = held[N_BASE:]
    layer = held[N_CONSTS + N_WEIGHTS + 1]
    x = mixes(lambda s: s == 1, place, blocks, vec, weights[2], x)
    layer, entry_grad, *state_grads, row_grads = drained(
        layer, entry_grad, state_grads, row_grads
    )

    def half(second, after=None):
        keep, send = row_sets[2 * second : 2 * second + 2]
        if after is not None:
            send, *_ = lax.optimization_barrier((send, *after))
        pieces = join(keep, swapped(send))
        joined = pieces[0]
        pieces = (pieces[0],) + tuple(sent(pieces[k], k, True) for k in range(1, 4))
        shares = weight_grads(second, place, x[second], pieces)
        shares = (shares[0],) + tuple(sent(shares[k], k, False) for k in range(1, 4))
        parts = summed(second, shares)
        parts = (parts[0],) + tuple(sent(parts[k], k, True) for k in range(1, 4))
        kept, going, *payload = gathered(second, place, parts)
        return final(second, place, kept, swapped(going)), payload, joined

    (key,), (payload,), joined = half(False, x)
    (projection, out_weight, gate, vectors, decay, boost), _, _ = half(True, (joined, row_grads))
    return (
        layer.reshape(1, SEQS, LENGTH, WIDTH),
        entry_grad.reshape(1, SEQS, LENGTH, WIDTH),
        jnp.swapaxes(vectors, 0, 1),
        decay,
        boost,
        projection[None],
        out_weight[None],
        key[None],
        payload[None],
        gate[None],
        state_grads[0][None],
        state_grads[1][None],
        state_grads[2][None],
        row_grads[None],
    )


def solution(mesh):
    placed = (
        P("dp", None, None),
        P("dp", None, None),
        P("dp"),
        P("section", None, None),
        P("section", None),
        P("section", None),
        P("section", None, None, None),
        P("section", None, None),
        P("section", None, None),
        P("section", None, None),
        P("section", None, None),
        P("section", "dp", None),
        P("section", "dp", None),
        P("section", "dp", None),
        P("section", None, "dp", None),
    )
    return jax.shard_map(
        body,
        mesh=mesh,
        in_specs=placed,
        out_specs=(
            P("section", "dp", None, None),
            P("section", "dp", None, None),
            P("section", None, "dp"),
            P("section", "dp"),
            P("section", "dp"),
            P("section", None, "dp", None),
            P("section", "dp", None),
            P("section", "dp", None),
            P("section", "dp", None),
            P("section", "dp", None),
            P("section", "dp", None),
            P("section", "dp", None),
            P("section", "dp", None),
            P("section", None, "dp", None),
        ),
        check_vma=False,
    )
```

```python
import functools

import jax
import jax.numpy as jnp
from jax import lax
from jax.experimental import pallas as pl
from jax.experimental.pallas import tpu as pltpu
from jax.sharding import PartitionSpec as P

WIDTH = 1024
INNER = 4096
LENGTH = 64
SEQS = 2
ROWS = SEQS * LENGTH
GROUPS = WIDTH // 128
FRESH = -1e30
EPS = 1e-05
F32 = jnp.float32
BF16 = jnp.bfloat16

VM = pl.BlockSpec(memory_space=pltpu.VMEM)
HB = pl.BlockSpec(memory_space=pl.ANY)
SM = pl.BlockSpec(memory_space=pltpu.SMEM)
EDGE = ROWS + 16
QUARTER = 768
SHARES = (1024, 768)


HELD_LIMIT = 14
UNROLL = 4
WINDOW = 4
FLOPS = 10**9
BACK_COST = (14, 1, 14, 14)


def limit(mebibytes):
    return pltpu.CompilerParams(vmem_limit_bytes=mebibytes * 1024 * 1024)

EMISSION, RECEPTANCE = 3, 4
BLOCKS = (5, 4, 4)
WEIGHTS = tuple(((n, WIDTH, WIDTH), BF16) for n in BLOCKS)
CONSTS = (
    ((9, 1, WIDTH), F32),
    ((1, WIDTH), F32),
    ((1, WIDTH), F32),
    ((SEQS, WIDTH), F32),
    ((SEQS, WIDTH), F32),
    ((SEQS, WIDTH), F32),
    ((2, SEQS, WIDTH), BF16),
)
SAVED = (
    ((ROWS, WIDTH), BF16),
    ((ROWS, WIDTH), BF16),
    ((ROWS, INNER), BF16),
    ((5, ROWS, WIDTH), F32),
    ((8, ROWS * GROUPS, 128), F32),
)
EDGES = (
    ((EDGE, 2 * WIDTH), BF16),
    ((EDGE, 2 * WIDTH), BF16),
)
GRADS = (
    ((ROWS, WIDTH), BF16),
    ((4, ROWS, QUARTER), BF16),
    ((4, ROWS, QUARTER), BF16),
    ((4, ROWS, QUARTER), BF16),
    ((4, ROWS, QUARTER), BF16),
    ((3, SEQS, WIDTH), F32),
    ((2, SEQS, WIDTH), F32),
)
N_CONSTS, N_WEIGHTS, N_SAVED, N_EDGES, N_GRADS = 7, 3, 5, 2, 7
N_BASE = N_CONSTS + N_WEIGHTS + N_SAVED


def dot(left, right):
    return jnp.dot(left, right, preferred_element_type=F32)


def against(grad, weight):
    return lax.dot_general(
        grad, weight, (((1,), (1,)), ((), ())), preferred_element_type=F32
    )


def across(left, right):
    return lax.dot_general(
        left, right, (((0,), (0,)), ((), ())), preferred_element_type=F32
    )


def columns_loop(total, size):
    def run(function):
        if total // size <= UNROLL:
            for j in range(total // size):
                function(pl.ds(j * size, size))
            return

        @pl.loop(0, total // size)
        def _(j):
            function(pl.ds(pl.multiple_of(j * size, size), size))

    return run


def coordinates(section, dp):
    dp = dp[0]
    return section[0], dp >> 3, (dp >> 1) & 3, dp & 1


def row_index():
    return lax.broadcasted_iota(jnp.int32, (ROWS, WIDTH), 0)


def normed_rows(rows):
    center = jnp.mean(rows, axis=-1, keepdims=True)
    centered = rows - center
    variance = jnp.mean(centered * centered, axis=-1, keepdims=True)
    scale = lax.rsqrt(variance + EPS)
    return centered * scale, scale


def moved_down(normed, first):
    index = row_index()
    return jnp.where(
        index == 0,
        first[0],
        jnp.where(index == LENGTH, first[1], pltpu.roll(normed, 1, 0)),
    )


def moved_up(rows):
    index = row_index()
    return jnp.where(
        (index == LENGTH - 1) | (index == ROWS - 1),
        0.0,
        pltpu.roll(rows, ROWS - 1, 0),
    )


def first_rows(prior_ref, mix, marks):
    return [prior_ref[mix, s : s + 1, :].astype(F32) * marks[s] for s in range(SEQS)]


def edge_rows(first):
    index = lax.broadcasted_iota(jnp.int32, (EDGE - ROWS, WIDTH), 0)
    return jnp.where(index == 0, first[0], jnp.where(index == 1, first[1], 0.0)).astype(BF16)


def store_sets(core, keep_ref, send_ref, pieces):
    for this in range(2):

        @pl.when(core == this)
        def _(this=this):
            for which, at, value in pieces:
                (keep_ref if which == this else send_ref)[at] = value()


def to_tokens(ref, block, value):
    ref[pl.ds(block, ROWS, stride=GROUPS), :] = value


def from_tokens(ref, block):
    return ref[pl.ds(block, ROWS, stride=GROUPS), :]


def tile_of(ref, row, small):
    for g in range(GROUPS):
        small[g : g + 1, :] = ref[row : row + 1, g * 128 : (g + 1) * 128]
    return small[...]


def forward_body(core, marks, x_ref, consts, weights, ready, out_ref, saved, edges, scratch):
    streamed = x_ref is None
    vec_ref, fade_ref, boost_ref, num_ref, den_ref, lev_ref, prior_ref = consts
    square, keys, payload = weights
    ent_ref, lay_ref, act_ref, wide_ref, scan_ref = saved
    own_ref, other_ref = edges
    sk, sv, sy, small, mix_ref, hid_ref = scratch
    low, high = slice(0, WIDTH), slice(WIDTH, 2 * WIDTH)
    top, bottom = slice(0, ROWS), slice(ROWS, EDGE)
    if x_ref is not None:
        ent_ref[...] = x_ref[...]
    rows = ent_ref[...].astype(F32)
    unit, _ = normed_rows(rows)
    normed = unit * vec_ref[0] + vec_ref[1]
    first = first_rows(prior_ref, 0, marks)
    below = moved_down(normed, first)
    for j in range(3):
        v = vec_ref[2 + j]
        mix_ref[j] = (normed * v + below * (1.0 - v)).astype(BF16)
    mix_ref[3] = normed.astype(BF16)
    first_one = first
    for target, j in ((sk, 0), (sv, 1)):
        ready(j)

        @columns_loop(WIDTH, 512)
        def _(at, j=j):
            wide_ref[3, :, at] = dot(mix_ref[j], square[j, :, at])

        for g in range(GROUPS):
            to_tokens(target, g, wide_ref[3, :, g * 128 : (g + 1) * 128])
    ready(2)

    @columns_loop(WIDTH, 512)
    def _(at):
        wide_ref[0, :, at] = jax.nn.sigmoid(dot(mix_ref[2], square[2, :, at]))

    rate = jnp.exp(tile_of(fade_ref, 0, small))
    boost = tile_of(boost_ref, 0, small)
    start = []
    for s in range(SEQS):
        level = tile_of(lev_ref, s, small)
        start.append(jnp.where(marks[s] > 0.0, level, FRESH))
        start.append(tile_of(num_ref, s, small) * marks[s])
        start.append(tile_of(den_ref, s, small) * marks[s])

    def token(t, carry):
        carry_next = []
        for s in range(SEQS):
            level, num, den = carry[3 * s : 3 * s + 3]
            at = pl.ds(pl.multiple_of((t + LENGTH * s) * GROUPS, GROUPS), GROUPS)
            key, value = sk[at, :], sv[at, :]
            boosted = boost + key
            decayed = jnp.exp(-jnp.abs(level - boosted))
            state_on_top = level > boosted
            old = jnp.where(state_on_top, 1.0, decayed)
            fresh = jnp.where(state_on_top, decayed, 1.0)
            inverse = 1.0 / (old * den + fresh)
            old = old * inverse
            fresh = fresh * inverse
            result = old * num + fresh * value
            faded = level - rate
            level = jnp.maximum(faded, key)
            decayed = jnp.exp(-jnp.abs(faded - key))
            state_on_top = faded > key
            keep = jnp.where(state_on_top, 1.0, decayed)
            new = jnp.where(state_on_top, decayed, 1.0)
            sy[at, :] = result
            scan_ref[0, at, :] = old
            scan_ref[1, at, :] = fresh
            scan_ref[2, at, :] = value - result
            scan_ref[3, at, :] = keep
            scan_ref[4, at, :] = new
            scan_ref[5, at, :] = num
            scan_ref[6, at, :] = den
            scan_ref[7, at, :] = value
            carry_next += [level, keep * num + new * value, keep * den + new]
        return tuple(carry_next)

    def tokens(block, carry):
        for j in range(8):
            carry = token(block * 8 + j, carry)
        return carry

    lax.fori_loop(0, LENGTH // 8, tokens, tuple(start))
    for g in range(GROUPS):
        at = slice(g * 128, (g + 1) * 128)
        gate = wide_ref[0, :, at]
        mixed = gate * from_tokens(sy, g)
        mix_ref[0, :, at] = mixed.astype(BF16)
        wide_ref[1, :, at] = mixed * (1.0 - gate)
    store_sets(
        core, own_ref, other_ref,
        (
            (0, (top, high), lambda: mix_ref[3]),
            (0, (bottom, high), lambda: edge_rows(first_one)),
            (1, (top, high), lambda: mix_ref[0]),
        ),
    )
    ready(3)

    @columns_loop(WIDTH, 512)
    def _(at):
        wide_ref[2, :, at] = ent_ref[:, at].astype(F32) + dot(mix_ref[0], square[EMISSION, :, at])

    unit, _ = normed_rows(wide_ref[2])
    normed = unit * vec_ref[5] + vec_ref[6]
    first = first_rows(prior_ref, 1, marks)
    below = moved_down(normed, first)
    for j in range(2):
        v = vec_ref[7 + j]
        mix_ref[1 + j] = (normed * v + below * (1.0 - v)).astype(BF16)
    for ref in edges:
        ref[top, low] = normed.astype(BF16)
        ref[bottom, low] = edge_rows(first)
    ready(4)

    @columns_loop(WIDTH, 512)
    def _(at):
        wide_ref[4, :, at] = jax.nn.sigmoid(dot(mix_ref[2], square[RECEPTANCE, :, at]))

    def hidden(j):
        at = pl.ds(pl.multiple_of(j * 512, 512), 512)
        within = pl.ds(pl.multiple_of((j & 1) * 512, 512), 512)
        active = jnp.maximum(dot(mix_ref[1], keys[j >> 1, :, within]), 0.0)
        act_ref[:, at] = active.astype(BF16)
        hid_ref[:, at] = (active * active).astype(BF16)

    def leave(at, channel):
        wide_ref[3, :, at] = channel
        lay_ref[:, at] = (wide_ref[2, :, at] + wide_ref[4, :, at] * channel).astype(BF16)

    def part(b, at):
        return dot(hid_ref[:, b * WIDTH : (b + 1) * WIDTH], payload[b, :, at])

    if not streamed:
        pl.loop(0, INNER // 512)(hidden)

        @columns_loop(WIDTH, 256)
        def _(at):
            leave(at, part(0, at) + part(1, at) + part(2, at) + part(3, at))

    else:
        for b in range(4):
            ready(5 + b)
            pl.loop(2 * b, 2 * b + 2)(hidden)
        for b in range(4):
            ready(9 + b)

            @columns_loop(WIDTH, 512)
            def _(at, b=b):
                channel = part(b, at)
                if b > 0:
                    channel = channel + wide_ref[3, :, at]
                if b < 3:
                    wide_ref[3, :, at] = channel
                else:
                    leave(at, channel)

    out_ref[...] = lay_ref[...]


def groups(refs, *sizes):
    cut, at = [], 0
    for size in sizes:
        cut.append(refs[at : at + size])
        at += size
    return cut + [refs[at:]]


def weight_pieces(maps, emission, key, payload, receptance):
    pieces = [maps.at[j] for j in range(3)] + [emission, receptance]
    for b in range(4):
        pieces.append(key.at[:, pl.ds(b * WIDTH, WIDTH)])
    for b in range(4):
        pieces.append(payload.at[pl.ds(b * WIDTH, WIDTH), :])
    return pieces


def forward_first_kernel(section, dp, begins, x_ref, *refs):
    small_in, hbm, (out_ref,), consts, kept, saved, edges, rest = groups(
        refs, N_CONSTS, 5, 1, N_CONSTS, N_WEIGHTS, N_SAVED, N_EDGES
    )
    section, _, _, core = coordinates(section, dp)
    sem, small_sem = rest[-2:]
    copies = [
        pltpu.make_async_copy(source, target, sem.at[i])
        for i, (source, target) in enumerate(
            zip(
                weight_pieces(*hbm),
                [ref.at[i] for ref, n in zip(kept, BLOCKS) for i in range(n)],
            )
        )
    ]
    arriving = [pltpu.make_async_copy(x_ref, saved[0], small_sem.at[N_CONSTS])]
    for i in range(N_CONSTS):
        arriving.append(pltpu.make_async_copy(small_in[i], consts[i], small_sem.at[i]))
    for c in arriving + copies[:WINDOW]:
        c.start()
    for c in arriving:
        c.wait()

    def ready(i):
        copies[i].wait()
        if i + WINDOW < len(copies):
            copies[i + WINDOW].start()

    @pl.when(section == 0)
    def _():
        marks = [begins[s].astype(F32) for s in range(SEQS)]
        forward_body(
            core, marks, None, consts, kept, ready, out_ref, saved, edges, rest[:-2]
        )

    @pl.when(section != 0)
    def _():
        for c in copies[WINDOW:]:
            c.start()
        for c in copies:
            c.wait()


def flip(ref):
    side = 256
    for i in range(WIDTH // side):
        for j in range(i + 1):
            one = (slice(i * side, (i + 1) * side), slice(j * side, (j + 1) * side))
            two = (one[1], one[0])
            first = ref[one].T
            if i != j:
                ref[one] = ref[two].T
            ref[two] = first


def forward_kernel(layer, section, dp, begins, x_ref, *refs):
    _, (out_ref,), consts, kept, saved, edges, scratch = groups(
        refs, N_BASE + N_EDGES, 1, N_CONSTS, N_WEIGHTS, N_SAVED, N_EDGES
    )
    section, _, _, core = coordinates(section, dp)

    @pl.when(section == layer)
    def _():
        marks = [begins[s].astype(F32) for s in range(SEQS)]
        forward_body(
            core, marks, x_ref, consts, kept, lambda i: None, out_ref, saved, edges, scratch
        )


def norm_back(rows, gain, offset, first, parts, vec_out, prior_out, marks):
    unit, scale = normed_rows(rows)
    normed = unit * gain + offset
    change = normed - moved_down(normed, first)
    up, stay = None, None
    for grad, weight, row in parts:
        vec_out(row, jnp.sum(grad * change, axis=0, keepdims=True))
        kept = grad * weight
        passed = grad - kept
        stay = kept if stay is None else stay + kept
        up = passed if up is None else up + passed
    for s in range(SEQS):
        prior_out(s, up[s * LENGTH : s * LENGTH + 1, :] * marks[s])
    grad = stay + moved_up(up)
    return unit, scale, grad


def backward_kernel(first, flipped, layer, section, dp, begins, dy_ref, *refs):
    _, (out_ref,), consts, kept, saved, grads, scratch = groups(
        refs, N_BASE + (0 if first else N_GRADS), 1, N_CONSTS, N_WEIGHTS, N_SAVED, N_GRADS
    )
    vec_ref, fade_ref, prior_ref = consts[0], consts[1], consts[6]
    square, keys, payload = kept
    ent_ref, lay_ref, act_ref, wide_ref, scan_ref = saved
    ing_ref, keep_one, send_one, keep_two, send_two, stg_ref, rowg_ref = grads
    sg, sdk, sdv, small, wide, wide_two, wide_three, wide_four, dys_ref, dhp_ref, vecg_ref = scratch
    section, y, z, core = coordinates(section, dp)
    def vec_out(row, value):
        vecg_ref[row : row + 1, :] = value

    def store(keep_ref, send_ref, items, shared=None):
        for this in range(2):

            @pl.when(core == this)
            def _(this=this):
                @pl.loop(0, 4)
                def _(q):
                    for which, column, size, value in items:
                        ref = keep_ref if which == this else send_ref
                        distance = (q - (y if which else z)) & 3
                        ref[distance, :, column : column + size] = value(q)
                    if shared is not None:
                        ref = keep_ref if this == 1 else send_ref
                        ref[q, 0:64, 512:768] = shared

    def quarter(row):
        return lambda q: dys_ref[row, :, pl.ds(pl.multiple_of(q * 256, 256), 256)]

    def pull(grad, blocks, i, at):
        if flipped:
            return dot(grad, blocks[i, :, at])
        return against(grad, blocks[i, at, :])

    def through_payload(grad, j):
        return pull(grad, payload, j >> 1, pl.ds(pl.multiple_of((j & 1) * 512, 512), 512))

    def through_key(grad_ref, j):
        at = pl.ds(pl.multiple_of(j * 256, 256), 256)
        total = None
        for b in range(4):
            part = pull(grad_ref[:, b * WIDTH : (b + 1) * WIDTH], keys, b, at)
            total = part if total is None else total + part
        return total

    @pl.when(section == layer)
    def _():
        marks = [begins[s].astype(F32) for s in range(SEQS)]
        dy = dy_ref[...].astype(F32)
        gate = wide_ref[4]
        through = dy * gate
        dys_ref[4] = through.astype(BF16)
        dys_ref[5] = (through * wide_ref[3] * (1.0 - gate)).astype(BF16)

        @pl.loop(0, INNER // 512, unroll=2)
        def _(j):
            at = pl.ds(pl.multiple_of(j * 512, 512), 512)
            part = through_payload(dys_ref[4], j)
            dhp_ref[:, at] = (2.0 * act_ref[:, at].astype(F32) * part).astype(BF16)

        def hidden(start):
            return lambda q: dhp_ref[:, pl.ds(pl.multiple_of(start + q * 512, 512), 512)]

        store(
            keep_one, send_one,
            ((0, 0, 512, hidden(0)), (1, 0, 512, hidden(2048)),
             (0, 512, 256, quarter(4)), (1, 512, 256, quarter(4))),
        )

        @pl.loop(0, WIDTH // 256)
        def _(j):
            at = pl.ds(pl.multiple_of(j * 256, 256), 256)
            wide[:, at] = through_key(dhp_ref, j)
            wide_two[:, at] = pull(dys_ref[5], square, RECEPTANCE, at)

        def prior_two(s, value):
            rowg_ref[1, s : s + 1, :] = value

        gain = vec_ref[5]
        unit, scale, grad = norm_back(
            wide_ref[2], gain, vec_ref[6], first_rows(prior_ref, 1, marks),
            ((wide[...], vec_ref[7], 7), (wide_two[...], vec_ref[8], 8)),
            vec_out, prior_two, marks,
        )
        vec_out(5, jnp.sum(grad * unit, axis=0, keepdims=True))
        vec_out(6, jnp.sum(grad, axis=0, keepdims=True))
        grad = grad * gain
        mean = jnp.mean(grad, axis=-1, keepdims=True)
        along = jnp.mean(grad * unit, axis=-1, keepdims=True)
        middle = dy_ref[...].astype(F32) + scale * (grad - mean - unit * along)
        wide_three[...] = middle
        dys_ref[3] = middle.astype(BF16)

        for q in range(4):
            at = pl.ds(q * 256, 256)
            part = pull(dys_ref[3], square, EMISSION, at)
            dys_ref[2, :, at] = (part * wide_ref[1, :, at]).astype(BF16)
            wide[:, at] = part * wide_ref[0, :, at]

        for g in range(GROUPS):
            to_tokens(sg, g, wide[:, g * 128 : (g + 1) * 128])

        zero = jnp.zeros((GROUPS, 128), F32)

        def token(t, carry):
            carry_next = []
            boosted, faded = carry[4], carry[5]
            for s in range(SEQS):
                dnum, dden = carry[2 * s : 2 * s + 2]
                at = pl.ds(pl.multiple_of((t + LENGTH * s) * GROUPS, GROUPS), GROUPS)
                g = sg[at, :]
                value = scan_ref[7, at, :]
                beyond = scan_ref[2, at, :]
                keep = scan_ref[3, at, :]
                new = scan_ref[4, at, :]
                from_old = scan_ref[0, at, :] * g
                from_new = scan_ref[1, at, :] * g
                direct = from_new * beyond
                boosted = boosted + direct
                sdv[at, :] = from_new + new * dnum
                sdk[at, :] = direct + new * (dnum * value + dden)
                faded = faded - keep * (dnum * scan_ref[5, at, :] + dden * scan_ref[6, at, :])
                carry_next += [
                    from_old + keep * dnum,
                    keep * dden - from_old * (value - beyond),
                ]
            return tuple(carry_next) + (boosted, faded)

        def tokens(block, carry):
            for j in range(8):
                carry = token(LENGTH - 1 - block * 8 - j, carry)
            return carry

        ends = lax.fori_loop(0, LENGTH // 8, tokens, (zero,) * 6)

        def spread(put_piece, value):
            small[...] = value
            for g in range(GROUPS):
                put_piece(slice(g * 128, (g + 1) * 128), small[g : g + 1, :])

        for s in range(SEQS):
            dnum, dden = ends[2 * s : 2 * s + 2]
            at = pl.ds(LENGTH * s * GROUPS, GROUPS)
            moved = dnum * scan_ref[5, at, :] + dden * scan_ref[6, at, :]
            for k, value in enumerate((dnum, dden, moved)):

                def put_state(cols, piece, k=k, s=s):
                    stg_ref[k, s : s + 1, cols] = piece

                spread(put_state, value * marks[s])

        def put_decay(cols, piece):
            vecg_ref[9:10, cols] = piece

        def put_boost(cols, piece):
            vecg_ref[10:11, cols] = piece

        spread(put_decay, ends[5])
        vecg_ref[9:10, :] = vecg_ref[9:10, :] * jnp.exp(fade_ref[0:1, :])
        spread(put_boost, ends[4])

        for g in range(GROUPS):
            at = slice(g * 128, (g + 1) * 128)
            dys_ref[0, :, at] = from_tokens(sdk, g).astype(BF16)
            dys_ref[1, :, at] = from_tokens(sdv, g).astype(BF16)
        rows = ent_ref[...].astype(F32)
        pulled = (wide, wide_two, wide_four)
        for j in range(3):

            @columns_loop(WIDTH, 512)
            def _(at, j=j):
                pulled[j][:, at] = pull(dys_ref[j], square, j, at)


        def prior_one(s, value):
            rowg_ref[0, s : s + 1, :] = value

        gain = vec_ref[0]
        unit, scale, grad = norm_back(
            rows, gain, vec_ref[1], first_rows(prior_ref, 0, marks),
            [(pulled[j][...], vec_ref[2 + j], 2 + j) for j in range(3)],
            vec_out, prior_one, marks,
        )
        vec_out(0, jnp.sum(grad * unit, axis=0, keepdims=True))
        vec_out(1, jnp.sum(grad, axis=0, keepdims=True))
        packed = jnp.concatenate(
            [vecg_ref[:, b * 256 : (b + 1) * 256] for b in range(4)], axis=0
        ).astype(BF16)
        store(
            keep_two, send_two,
            ((0, 0, 256, quarter(0)), (0, 256, 256, quarter(1)), (0, 512, 256, quarter(2)),
             (1, 0, 256, quarter(5)), (1, 256, 256, quarter(3))),
            packed,
        )
        grad = grad * gain
        mean = jnp.mean(grad, axis=-1, keepdims=True)
        along = jnp.mean(grad * unit, axis=-1, keepdims=True)
        entry = (wide_three[...] + scale * (grad - mean - unit * along)).astype(BF16)
        ing_ref[...] = entry
        out_ref[...] = entry

    if first:

        @pl.when(section != layer)
        def _():
            for ref, n in zip(kept, BLOCKS):

                @pl.loop(0, n)
                def _(i, ref=ref):
                    flip(ref.at[i])


def join_edges_kernel(first, second, out, sem):
    copies = [
        pltpu.make_async_copy(ref, out.at[pl.ds(h * EDGE, EDGE), :], sem.at[h])
        for h, ref in enumerate((first, second))
    ]
    for c in copies:
        c.start()
    for c in copies:
        c.wait()


def join_kernel(first, second, *outs):
    for k in range(4):
        outs[k][:ROWS, :] = first[k]
        outs[k][ROWS:, :] = second[k]


def mixes_kernel(section, dp, own, one, two, three, vec_ref, wa, *refs):
    x_one, x_two, *scratch = refs[-10:]
    edge, wide, stage, hidden, first_mix, edge_sem, wide_sem, out_sem = scratch
    core = coordinates(section, dp)[3]

    def load(n):
        block = (own, one, two, three)[n // 2]
        return pltpu.make_async_copy(
            block.at[pl.ds(n % 2 * EDGE, EDGE), :], edge.at[n], edge_sem.at[n]
        )

    def columns(u):
        return [
            pltpu.make_async_copy(
                wa.at[:, pl.ds(pl.multiple_of((16 * u + 2 * j + core) * 128, 128), 128)],
                wide.at[:, pl.ds(j * 128, 128)],
                wide_sem.at[j],
            )
            for j in range(8)
        ]

    def out_mixes(n):
        rows = pl.ds(pl.multiple_of(n * ROWS, ROWS), ROWS)
        return pltpu.make_async_copy(
            stage.at[n & 1], x_two.at[:, rows, :], out_sem.at[n & 1]
        )

    def out_hidden(u, t):
        cols = pl.ds(pl.multiple_of(t * 256, 256), 256)
        return pltpu.make_async_copy(
            hidden.at[t & 1], x_one.at[u, :, cols], out_sem.at[2 + (t & 1)]
        )

    out_first = pltpu.make_async_copy(first_mix, x_one.at[2], out_sem.at[4])

    def mix(normed, below, j):
        v = vec_ref[j]
        return (normed * v + below * (1.0 - v)).astype(BF16)

    for n in range(8):
        load(n).start()
    for c in columns(0):
        c.start()
    for n in range(8):
        load(n).wait()

    @pl.loop(0, 8)
    def _(n):
        @pl.when(n >= 2)
        def _():
            out_mixes(n - 2).wait()

        block, here = edge.at[n], stage.at[n & 1]

        def parts(c):
            cols = slice(c * WIDTH, (c + 1) * WIDTH)
            normed = block[:ROWS, cols].astype(F32)
            first = block[ROWS:, cols].astype(F32)
            return normed, moved_down(normed, (first[0:1, :], first[1:2, :]))

        normed, below = parts(0)
        first_mix[pl.ds(pl.multiple_of(n * ROWS, ROWS), ROWS), :] = mix(normed, below, 7)

        @pl.when(core == 0)
        def _():
            normed, below = parts(1)
            for j in range(3):
                here[j] = mix(normed, below, 2 + j)

        @pl.when(core == 1)
        def _():
            here[0] = mix(normed, below, 8)
            here[1] = block[:ROWS, WIDTH:]

        out_mixes(n).start()

    out_first.start()
    for u in range(2):
        for c in columns(u):
            c.wait()

        @pl.loop(0, 4)
        def _(t, u=u):
            @pl.when(t >= 2)
            def _():
                out_hidden(u, t - 2).wait()

            cols = pl.ds(pl.multiple_of(t * 256, 256), 256)
            for r in range(4):
                rows = slice(r * 256, (r + 1) * 256)
                active = jnp.maximum(dot(first_mix[rows, :], wide[:, cols]), 0.0)
                hidden[t & 1, rows, :] = (active * active).astype(BF16)
            out_hidden(u, t).start()

        if u == 0:
            for c in columns(1):
                c.start()
        for t in (2, 3):
            out_hidden(u, t).wait()
    for n in (6, 7):
        out_mixes(n).wait()
    out_first.wait()


def drain_kernel(layer, entry, states, firsts, *refs):
    results, sem = refs[:-1], refs[-1]
    sources = (layer, entry) + tuple(states.at[k] for k in range(3)) + (firsts,)
    copies = [
        pltpu.make_async_copy(source, target, sem.at[i])
        for i, (source, target) in enumerate(zip(sources, results))
    ]
    for c in copies:
        c.start()
    for c in copies:
        c.wait()


def row_starts(y, z, core):
    starts = []
    for there in range(16):
        along_y, along_z = (there // 4 - y) & 3, (there % 4 - z) & 3
        summed = jnp.where(core == 0, along_y, along_z)
        joined = jnp.where(core == 0, along_z, along_y)
        starts.append(pl.multiple_of(summed * 256 + joined * 64, 64))
    return starts


def weight_kernel(second, section, dp, x_ref, *refs):
    blocks, outs = refs[:4], refs[4:8]
    dy, share = refs[8:]
    _, y, z, core = coordinates(section, dp)
    for k in range(4):
        dy[k * 2 * ROWS : (k + 1) * 2 * ROWS, :] = blocks[k][...]
    starts = row_starts(y, z, core)

    def unit(u, size, source, target):
        for c in range(0, WIDTH, 256):
            part = across(x_ref[u, :, c : c + 256], dy[:, source : source + size]).astype(BF16)
            for b in range(4):
                share[pl.ds(starts[c // 64 + b], 64), target : target + size] = part[
                    b * 64 : (b + 1) * 64, :
                ]

    if not second:
        unit(2, 512, 0, 0)
        for u in range(2):
            for c in range(0, WIDTH, 256):
                part = across(x_ref[u, :, c : c + 256], dy[:, 512:768]).astype(BF16)
                for b in range(2):
                    start = starts[(u * WIDTH + c) // 128 + b]
                    for half in range(2):
                        share[pl.ds(start, 64), 512 + half * 256 : 768 + half * 256] = part[
                            b * 128 + half * 64 : b * 128 + (half + 1) * 64, :
                        ]
    else:
        unit(0, 256, 0, 0)
        unit(1, 256, 256, 256)

        @pl.when(core == 0)
        def _():
            unit(2, 256, 512, 512)

        @pl.when(core == 1)
        def _():
            total = jnp.zeros((64, 256), F32)
            for d in range(8):
                total = total + dy[d * ROWS : d * ROWS + 64, 512:768].astype(F32)
            for b in range(4):
                piece = jnp.concatenate(
                    [total[b * 16 : (b + 1) * 16, :], jnp.zeros((112, 256), F32)], axis=0
                ).T.astype(BF16)
                for e in range(4):
                    at = pl.ds(starts[b * 4 + e], 64)
                    share[at, 512:640] = piece[e * 64 : (e + 1) * 64, :]
                    share[at, 640:768] = jnp.zeros((64, 128), BF16)

    for k in range(4):
        outs[k][...] = share[k * 256 : (k + 1) * 256, :]


def sum_kernel(own, one, two, three, *outs):
    total = own[...].astype(F32) + one[...].astype(F32) + two[...].astype(F32)
    total = (total + three[...].astype(F32)).astype(BF16)
    for k in range(4):
        outs[k][...] = total[k * 64 : (k + 1) * 64, :]


def gather_kernel(second, section, dp, own, one, two, three, keep_ref, send_ref, *payload):
    _, y, z, core = coordinates(section, dp)
    here = jnp.where(core == 0, z, y)
    mine = pl.multiple_of(core * 32, 32)
    theirs = pl.multiple_of(32 - core * 32, 32)
    for k, ref in enumerate((own, one, two, three)):
        quarter = (here - k) & 3
        for rows, target in ((mine, keep_ref), (theirs, send_ref)):
            if not second:
                at = pl.ds(pl.multiple_of(quarter * 512, 512), 512)
                target[:, at] = ref[pl.ds(rows, 32), 0:512]
            else:
                for u in range(3):
                    at = pl.ds(pl.multiple_of(u * WIDTH + quarter * 256, 256), 256)
                    target[:, at] = ref[pl.ds(rows, 32), u * 256 : (u + 1) * 256]
        if not second:
            at = pl.ds(pl.multiple_of(quarter * 256, 256), 256)
            for half in range(2):
                payload[0][half * 64 : (half + 1) * 64, at] = ref[
                    :, 512 + half * 256 : 768 + half * 256
                ].astype(F32)


def final_kernel(second, section, dp, kept, come, *outs):
    core = coordinates(section, dp)[3]

    def write(set_zero, set_one):
        if not second:
            outs[0][:, 0:2048] = set_zero[...].astype(F32)
            outs[0][:, 2048:4096] = set_one[...].astype(F32)
            return
        proj_ref, out_ref, gate_ref, vec_ref, dec_ref, boo_ref = outs
        for u in range(3):
            proj_ref[u] = set_zero[:, u * WIDTH : (u + 1) * WIDTH].astype(F32)
        gate_ref[...] = set_one[:, 0:1024].astype(F32)
        out_ref[...] = set_one[:, 1024:2048].astype(F32)
        vectors = set_one[:, 2048:2176].astype(F32).T
        for j in range(9):
            vec_ref[j] = vectors[j : j + 1, :]
        dec_ref[...] = vectors[9:10, :]
        boo_ref[...] = vectors[10:11, :]

    @pl.when(core == 0)
    def _():
        write(kept, come)

    @pl.when(core == 1)
    def _():
        write(come, kept)


def plain(shapes):
    return tuple(jax.ShapeDtypeStruct(s, d) for s, d in shapes)


def in_vmem(shapes):
    return tuple(pltpu.VMEM(s, d) for s, d in shapes)


def hold(arrays):
    return tuple(pltpu.with_memory_space_constraint(a, pltpu.VMEM) for a in arrays)


def in_hbm(*arrays):
    return tuple(pltpu.with_memory_space_constraint(a, pltpu.HBM) for a in arrays)


def array(*shape, kind=BF16):
    return jax.ShapeDtypeStruct(shape, kind)


ROWS_OUT = array(ROWS, WIDTH)
TOKENS = pltpu.VMEM((ROWS * GROUPS, 128), F32)
SMALL = pltpu.VMEM((GROUPS, 128), F32)
WIDE = pltpu.VMEM((ROWS, WIDTH), F32)
FORWARD_SCRATCH = [
    TOKENS, TOKENS, TOKENS, SMALL,
    pltpu.VMEM((4, ROWS, WIDTH), BF16),
    pltpu.VMEM((ROWS, INNER), BF16),
]
DMA = pltpu.SemaphoreType.DMA


def forward_first(place, begins, rows, small, weights):
    shapes = CONSTS + WEIGHTS + SAVED + EDGES
    results = pl.pallas_call(
        forward_first_kernel,
        cost_estimate=cost(12),
        out_shape=(ROWS_OUT,) + in_vmem(shapes),
        in_specs=[SM] * 3 + [HB] * (1 + N_CONSTS + 5),
        out_specs=(VM,) * (1 + len(shapes)),
        scratch_shapes=FORWARD_SCRATCH + [DMA((13,)), DMA((N_CONSTS + 1,))],
        compiler_params=limit(HELD_LIMIT),
    )(*place, begins, *in_hbm(rows, *small, *weights))
    return results[0], results[1:]


def forward_next(layer, place, begins, rows, held):
    shapes = CONSTS + WEIGHTS + SAVED + EDGES
    results = pl.pallas_call(
        functools.partial(forward_kernel, layer),
        cost_estimate=cost(10),
        out_shape=(ROWS_OUT,) + plain(shapes),
        in_specs=[SM] * 3 + [VM] * (1 + len(shapes)),
        out_specs=(VM,) * (1 + len(shapes)),
        input_output_aliases={4 + i: 1 + i for i in range(len(shapes))},
        scratch_shapes=FORWARD_SCRATCH,
        compiler_params=limit(HELD_LIMIT),
    )(*place, begins, *hold((rows,)), *hold(held))
    return results[0], results[1:]


def backward_call(layer, place, begins, grad, held):
    first = len(held) == N_BASE
    base = CONSTS + WEIGHTS + SAVED
    results = pl.pallas_call(
        functools.partial(backward_kernel, first, not first, layer),
        cost_estimate=cost(BACK_COST[layer]),
        out_shape=(ROWS_OUT,) + plain(base) + (in_vmem(GRADS) if first else plain(GRADS)),
        in_specs=[SM] * 3 + [VM] * (1 + len(held)),
        out_specs=(VM,) * (1 + N_BASE + N_GRADS),
        input_output_aliases={4 + i: 1 + i for i in range(len(held))},
        scratch_shapes=[
            TOKENS, TOKENS, TOKENS, SMALL, WIDE, WIDE, WIDE, WIDE,
            pltpu.VMEM((6, ROWS, WIDTH), BF16),
            pltpu.VMEM((ROWS, INNER), BF16),
            pltpu.VMEM((16, WIDTH), F32),
        ],
        compiler_params=limit(HELD_LIMIT),
    )(*place, begins, *hold((grad,)), *hold(held))
    return results[0], results[1:]


def cost(microseconds):
    return pl.CostEstimate(
        flops=int(microseconds * FLOPS), bytes_accessed=0, transcendentals=0
    )


def join_edges(first, second):
    return pl.pallas_call(
        join_edges_kernel,
        cost_estimate=cost(3),
        out_shape=pltpu.HBM((2 * EDGE, 2 * WIDTH), BF16),
        in_specs=[VM, VM],
        out_specs=HB,
        scratch_shapes=[DMA((2,))],
        compiler_params=limit(1),
    )(*hold((first, second)))


def join(first, second):
    return pl.pallas_call(
        join_kernel,
        cost_estimate=cost(1),
        out_shape=in_vmem((((2 * ROWS, QUARTER), BF16),) * 4),
        in_specs=[VM, VM],
        out_specs=(VM,) * 4,
        compiler_params=limit(HELD_LIMIT),
    )(*hold((first, second)))


MIXES_SCRATCH = [
    pltpu.VMEM((8, EDGE, 2 * WIDTH), BF16),
    pltpu.VMEM((WIDTH, WIDTH), BF16),
    pltpu.VMEM((2, 3, ROWS, WIDTH), BF16),
    pltpu.VMEM((2, 8 * ROWS, 256), BF16),
    pltpu.VMEM((8 * ROWS, WIDTH), BF16),
    DMA((8,)),
    DMA((8,)),
    DMA((5,)),
]
X_HALF = pltpu.HBM((3, 8 * ROWS, WIDTH), BF16)


def mixes(place, blocks, vec, wa):
    return pl.pallas_call(
        mixes_kernel,
        cost_estimate=cost(15),
        out_shape=(X_HALF, X_HALF),
        in_specs=[SM] * 2 + [HB] * 4 + [VM, HB],
        out_specs=(HB, HB),
        scratch_shapes=MIXES_SCRATCH,
        compiler_params=limit(HELD_LIMIT),
    )(*place, *in_hbm(*blocks), vec, *in_hbm(wa))


def drained(layer, entry, states, firsts):
    rows, state = pltpu.HBM((ROWS, WIDTH), BF16), pltpu.HBM((SEQS, WIDTH), F32)
    return pl.pallas_call(
        drain_kernel,
        cost_estimate=cost(1),
        out_shape=(rows, rows, state, state, state, pltpu.HBM((2, SEQS, WIDTH), F32)),
        in_specs=[HB] * 4,
        out_specs=(HB,) * 6,
        scratch_shapes=[DMA((6,))],
        compiler_params=limit(1),
    )(layer, entry, states, firsts)


def weight_grads(second, place, x, blocks):
    columns = SHARES[second]
    return pl.pallas_call(
        functools.partial(weight_kernel, second),
        cost_estimate=cost(4),
        out_shape=in_vmem((((2 * ROWS, columns), BF16),) * 4),
        in_specs=[SM] * 2 + [VM] * 5,
        out_specs=(VM,) * 4,
        scratch_shapes=[
            pltpu.VMEM((8 * ROWS, QUARTER), BF16),
            pltpu.VMEM((8 * ROWS, columns), BF16),
        ],
        compiler_params=limit(HELD_LIMIT),
    )(*place, *hold((x, *blocks)))


def summed(second, shares):
    return pl.pallas_call(
        sum_kernel,
        cost_estimate=cost(1),
        out_shape=in_vmem((((64, SHARES[second]), BF16),) * 4),
        in_specs=[VM] * 4,
        out_specs=(VM,) * 4,
        compiler_params=limit(HELD_LIMIT),
    )(*hold(shares))


def gathered(second, place, parts):
    outs = in_vmem((((32, 3 * WIDTH), BF16),) * 2)
    if not second:
        outs = in_vmem((((32, 2 * WIDTH), BF16),) * 2) + (pltpu.HBM((ROWS, WIDTH), F32),)
    return pl.pallas_call(
        functools.partial(gather_kernel, second),
        cost_estimate=cost(1),
        out_shape=outs,
        in_specs=[SM] * 2 + [VM] * 4,
        out_specs=(VM,) * len(outs),
        compiler_params=limit(HELD_LIMIT),
    )(*place, *hold(parts))


def final(second, place, kept, come):
    outs = (
        array(3, 32, WIDTH, kind=F32),
        array(32, WIDTH, kind=F32),
        array(32, WIDTH, kind=F32),
        array(9, 1, 32, kind=F32),
        array(1, 32, kind=F32),
        array(1, 32, kind=F32),
    )
    if not second:
        outs = (array(32, INNER, kind=F32),)
    return pl.pallas_call(
        functools.partial(final_kernel, second),
        cost_estimate=cost(1),
        out_shape=outs,
        in_specs=[SM] * 2 + [VM] * 2,
        out_specs=(VM,) * len(outs),
        compiler_params=limit(HELD_LIMIT),
    )(*place, *hold((kept, come)))


def device(y, z, core):
    return (y * 4 + z) * 2 + core


def swapped(block):
    return lax.ppermute(block, "dp", [(d, d ^ 1) for d in range(32)])


def sent(block, distance, first_axis):
    route = []
    for y in range(4):
        for z in range(4):
            for core in range(2):
                if (core == 0) == first_axis:
                    there = device(y, (z + distance) % 4, core)
                else:
                    there = device((y + distance) % 4, z, core)
                route.append((device(y, z, core), there))
    return lax.ppermute(block, "dp", route)


def body(
    bottom_stack_feed,
    loss_sensitivity,
    resumes_segment,
    mixing_coefficients,
    fading_log,
    feature_boost,
    attention_maps,
    emission_coefficients,
    feature_addressing,
    feature_payload,
    feature_receptance,
    dividend_memory,
    divisor_memory,
    memory_power_shift,
    prior_normed_lines,
):
    sections = lax.axis_size("section")
    place = (lax.axis_index("section")[None], lax.axis_index("dp")[None])
    begins = resumes_segment
    vec = jnp.swapaxes(mixing_coefficients, 0, 1)
    small = (
        vec,
        fading_log,
        feature_boost,
        dividend_memory[0],
        divisor_memory[0],
        memory_power_shift[0],
        prior_normed_lines[0],
    )
    weights = (
        attention_maps[0],
        emission_coefficients[0],
        feature_addressing[0],
        feature_payload[0],
        feature_receptance[0],
    )
    rows, held = forward_first(
        place, begins, bottom_stack_feed.reshape(ROWS, WIDTH), small, weights
    )
    for t in range(1, sections):
        rows = lax.ppermute(rows, "section", [(t - 1, t)])
        rows, held = forward_next(t, place, begins, rows, held)
    held, edges = held[:N_BASE], held[N_BASE:]
    grad, held = backward_call(
        sections - 1, place, begins, loss_sensitivity.reshape(ROWS, WIDTH), held
    )
    grad = lax.ppermute(grad, "section", [(sections - 1, sections - 2)])
    own = join_edges(edges[0], swapped(edges[1]))
    blocks = (own,) + tuple(sent(own, k, True) for k in range(1, 4))
    for t in range(sections - 2, -1, -1):
        if t == sections - 3:
            x = mixes(place, blocks, vec, weights[2])
            begins, *x = lax.optimization_barrier((begins, *x))
        grad, held = backward_call(t, place, begins, grad, held)
        if t > 0:
            grad = lax.ppermute(grad, "section", [(t, t - 1)])
    entry_grad, *row_sets, state_grads, row_grads = held[N_BASE:]
    layer = held[N_CONSTS + N_WEIGHTS + 1]
    layer, entry_grad, *state_grads, row_grads = drained(
        layer, entry_grad, state_grads, row_grads
    )

    def half(second, after=None):
        keep, send = row_sets[2 * second : 2 * second + 2]
        if after is not None:
            send, *_ = lax.optimization_barrier((send, *after))
        pieces = join(keep, swapped(send))
        joined = pieces[0]
        pieces = (pieces[0],) + tuple(sent(pieces[k], k, True) for k in range(1, 4))
        shares = weight_grads(second, place, x[second], pieces)
        shares = (shares[0],) + tuple(sent(shares[k], k, False) for k in range(1, 4))
        parts = summed(second, shares)
        parts = (parts[0],) + tuple(sent(parts[k], k, True) for k in range(1, 4))
        kept, going, *payload = gathered(second, place, parts)
        return final(second, place, kept, swapped(going)), payload, joined

    (key,), (payload,), joined = half(False, x)
    (projection, out_weight, gate, vectors, decay, boost), _, _ = half(True, (joined, row_grads))
    return (
        layer.reshape(1, SEQS, LENGTH, WIDTH),
        entry_grad.reshape(1, SEQS, LENGTH, WIDTH),
        jnp.swapaxes(vectors, 0, 1),
        decay,
        boost,
        projection[None],
        out_weight[None],
        key[None],
        payload[None],
        gate[None],
        state_grads[0][None],
        state_grads[1][None],
        state_grads[2][None],
        row_grads[None],
    )


def solution(mesh):
    placed = (
        P("dp", None, None),
        P("dp", None, None),
        P("dp"),
        P("section", None, None),
        P("section", None),
        P("section", None),
        P("section", None, None, None),
        P("section", None, None),
        P("section", None, None),
        P("section", None, None),
        P("section", None, None),
        P("section", "dp", None),
        P("section", "dp", None),
        P("section", "dp", None),
        P("section", None, "dp", None),
    )
    return jax.shard_map(
        body,
        mesh=mesh,
        in_specs=placed,
        out_specs=(
            P("section", "dp", None, None),
            P("section", "dp", None, None),
            P("section", None, "dp"),
            P("section", "dp"),
            P("section", "dp"),
            P("section", None, "dp", None),
            P("section", "dp", None),
            P("section", "dp", None),
            P("section", "dp", None),
            P("section", "dp", None),
            P("section", "dp", None),
            P("section", "dp", None),
            P("section", "dp", None),
            P("section", None, "dp", None),
        ),
        check_vma=False,
    )
```

```python
import functools

import jax
import jax.numpy as jnp
from jax import lax
from jax.experimental import pallas as pl
from jax.experimental.pallas import tpu as pltpu
from jax.sharding import PartitionSpec as P

WIDTH = 1024
INNER = 4096
LENGTH = 64
SEQS = 2
ROWS = SEQS * LENGTH
GROUPS = WIDTH // 128
FRESH = -1e30
EPS = 1e-05
F32 = jnp.float32
BF16 = jnp.bfloat16

VM = pl.BlockSpec(memory_space=pltpu.VMEM)
HB = pl.BlockSpec(memory_space=pl.ANY)
SM = pl.BlockSpec(memory_space=pltpu.SMEM)
EDGE = ROWS + 16
QUARTER = 768
SHARES = (1024, 768)


HELD_LIMIT = 14
UNROLL = 4
WINDOW = 4
FLOPS = 10**9
BACK_COST = (14, 1, 14, 14)


def limit(mebibytes):
    return pltpu.CompilerParams(vmem_limit_bytes=mebibytes * 1024 * 1024)

EMISSION, RECEPTANCE = 3, 4
BLOCKS = (5, 4, 4)
WEIGHTS = tuple(((n, WIDTH, WIDTH), BF16) for n in BLOCKS)
CONSTS = (
    ((9, 1, WIDTH), F32),
    ((1, WIDTH), F32),
    ((1, WIDTH), F32),
    ((SEQS, WIDTH), F32),
    ((SEQS, WIDTH), F32),
    ((SEQS, WIDTH), F32),
    ((2, SEQS, WIDTH), BF16),
)
SAVED = (
    ((ROWS, WIDTH), BF16),
    ((ROWS, WIDTH), BF16),
    ((ROWS, INNER), BF16),
    ((5, ROWS, WIDTH), F32),
    ((8, ROWS * GROUPS, 128), F32),
)
EDGES = (
    ((EDGE, 2 * WIDTH), BF16),
    ((EDGE, 2 * WIDTH), BF16),
)
GRADS = (
    ((ROWS, WIDTH), BF16),
    ((4, ROWS, QUARTER), BF16),
    ((4, ROWS, QUARTER), BF16),
    ((4, ROWS, QUARTER), BF16),
    ((4, ROWS, QUARTER), BF16),
    ((3, SEQS, WIDTH), F32),
    ((2, SEQS, WIDTH), F32),
)
N_CONSTS, N_WEIGHTS, N_SAVED, N_EDGES, N_GRADS = 7, 3, 5, 2, 7
N_BASE = N_CONSTS + N_WEIGHTS + N_SAVED


def dot(left, right):
    return jnp.dot(left, right, preferred_element_type=F32)


def against(grad, weight):
    return lax.dot_general(
        grad, weight, (((1,), (1,)), ((), ())), preferred_element_type=F32
    )


def across(left, right):
    return lax.dot_general(
        left, right, (((0,), (0,)), ((), ())), preferred_element_type=F32
    )


def columns_loop(total, size):
    def run(function):
        if total // size <= UNROLL:
            for j in range(total // size):
                function(pl.ds(j * size, size))
            return

        @pl.loop(0, total // size)
        def _(j):
            function(pl.ds(pl.multiple_of(j * size, size), size))

    return run


def coordinates(section, dp):
    dp = dp[0]
    return section[0], dp >> 3, (dp >> 1) & 3, dp & 1


def row_index():
    return lax.broadcasted_iota(jnp.int32, (ROWS, WIDTH), 0)


def normed_rows(rows):
    center = jnp.mean(rows, axis=-1, keepdims=True)
    centered = rows - center
    variance = jnp.mean(centered * centered, axis=-1, keepdims=True)
    scale = lax.rsqrt(variance + EPS)
    return centered * scale, scale


def moved_down(normed, first):
    index = row_index()
    return jnp.where(
        index == 0,
        first[0],
        jnp.where(index == LENGTH, first[1], pltpu.roll(normed, 1, 0)),
    )


def moved_up(rows):
    index = row_index()
    return jnp.where(
        (index == LENGTH - 1) | (index == ROWS - 1),
        0.0,
        pltpu.roll(rows, ROWS - 1, 0),
    )


def first_rows(prior_ref, mix, marks):
    return [prior_ref[mix, s : s + 1, :].astype(F32) * marks[s] for s in range(SEQS)]


def edge_rows(first):
    index = lax.broadcasted_iota(jnp.int32, (EDGE - ROWS, WIDTH), 0)
    return jnp.where(index == 0, first[0], jnp.where(index == 1, first[1], 0.0)).astype(BF16)


def store_sets(core, keep_ref, send_ref, pieces):
    for this in range(2):

        @pl.when(core == this)
        def _(this=this):
            for which, at, value in pieces:
                (keep_ref if which == this else send_ref)[at] = value()


def to_tokens(ref, block, value):
    ref[pl.ds(block, ROWS, stride=GROUPS), :] = value


def from_tokens(ref, block):
    return ref[pl.ds(block, ROWS, stride=GROUPS), :]


def tile_of(ref, row, small):
    for g in range(GROUPS):
        small[g : g + 1, :] = ref[row : row + 1, g * 128 : (g + 1) * 128]
    return small[...]


def forward_body(
    core, marks, x_ref, consts, weights, ready, out_ref, saved, edges, scratch, square_done=None
):
    streamed = x_ref is None
    vec_ref, fade_ref, boost_ref, num_ref, den_ref, lev_ref, prior_ref = consts
    square, keys, payload = weights
    ent_ref, lay_ref, act_ref, wide_ref, scan_ref = saved
    own_ref, other_ref = edges
    sk, sv, sy, small, mix_ref, hid_ref = scratch
    low, high = slice(0, WIDTH), slice(WIDTH, 2 * WIDTH)
    top, bottom = slice(0, ROWS), slice(ROWS, EDGE)
    if x_ref is not None:
        ent_ref[...] = x_ref[...]
    rows = ent_ref[...].astype(F32)
    unit, _ = normed_rows(rows)
    normed = unit * vec_ref[0] + vec_ref[1]
    first = first_rows(prior_ref, 0, marks)
    below = moved_down(normed, first)
    for j in range(3):
        v = vec_ref[2 + j]
        mix_ref[j] = (normed * v + below * (1.0 - v)).astype(BF16)
    mix_ref[3] = normed.astype(BF16)
    first_one = first
    for target, j in ((sk, 0), (sv, 1)):
        ready(j)

        @columns_loop(WIDTH, 512)
        def _(at, j=j):
            wide_ref[3, :, at] = dot(mix_ref[j], square[j, :, at])

        for g in range(GROUPS):
            to_tokens(target, g, wide_ref[3, :, g * 128 : (g + 1) * 128])
    ready(2)

    @columns_loop(WIDTH, 512)
    def _(at):
        wide_ref[0, :, at] = jax.nn.sigmoid(dot(mix_ref[2], square[2, :, at]))

    rate = jnp.exp(tile_of(fade_ref, 0, small))
    boost = tile_of(boost_ref, 0, small)
    start = []
    for s in range(SEQS):
        level = tile_of(lev_ref, s, small)
        start.append(jnp.where(marks[s] > 0.0, level, FRESH))
        start.append(tile_of(num_ref, s, small) * marks[s])
        start.append(tile_of(den_ref, s, small) * marks[s])

    def token(t, carry):
        carry_next = []
        for s in range(SEQS):
            level, num, den = carry[3 * s : 3 * s + 3]
            at = pl.ds(pl.multiple_of((t + LENGTH * s) * GROUPS, GROUPS), GROUPS)
            key, value = sk[at, :], sv[at, :]
            boosted = boost + key
            decayed = jnp.exp(-jnp.abs(level - boosted))
            state_on_top = level > boosted
            old = jnp.where(state_on_top, 1.0, decayed)
            fresh = jnp.where(state_on_top, decayed, 1.0)
            inverse = 1.0 / (old * den + fresh)
            old = old * inverse
            fresh = fresh * inverse
            result = old * num + fresh * value
            faded = level - rate
            level = jnp.maximum(faded, key)
            decayed = jnp.exp(-jnp.abs(faded - key))
            state_on_top = faded > key
            keep = jnp.where(state_on_top, 1.0, decayed)
            new = jnp.where(state_on_top, decayed, 1.0)
            sy[at, :] = result
            scan_ref[0, at, :] = old
            scan_ref[1, at, :] = fresh
            scan_ref[2, at, :] = value - result
            scan_ref[3, at, :] = keep
            scan_ref[4, at, :] = new
            scan_ref[5, at, :] = num
            scan_ref[6, at, :] = den
            scan_ref[7, at, :] = value
            carry_next += [level, keep * num + new * value, keep * den + new]
        return tuple(carry_next)

    def tokens(block, carry):
        for j in range(8):
            carry = token(block * 8 + j, carry)
        return carry

    lax.fori_loop(0, LENGTH // 8, tokens, tuple(start))
    for g in range(GROUPS):
        at = slice(g * 128, (g + 1) * 128)
        gate = wide_ref[0, :, at]
        mixed = gate * from_tokens(sy, g)
        mix_ref[0, :, at] = mixed.astype(BF16)
        wide_ref[1, :, at] = mixed * (1.0 - gate)
    store_sets(
        core, own_ref, other_ref,
        (
            (0, (top, high), lambda: mix_ref[3]),
            (0, (bottom, high), lambda: edge_rows(first_one)),
            (1, (top, high), lambda: mix_ref[0]),
        ),
    )
    ready(3)

    @columns_loop(WIDTH, 512)
    def _(at):
        wide_ref[2, :, at] = ent_ref[:, at].astype(F32) + dot(mix_ref[0], square[EMISSION, :, at])

    unit, _ = normed_rows(wide_ref[2])
    normed = unit * vec_ref[5] + vec_ref[6]
    first = first_rows(prior_ref, 1, marks)
    below = moved_down(normed, first)
    for j in range(2):
        v = vec_ref[7 + j]
        mix_ref[1 + j] = (normed * v + below * (1.0 - v)).astype(BF16)
    for ref in edges:
        ref[top, low] = normed.astype(BF16)
        ref[bottom, low] = edge_rows(first)
    ready(4)

    @columns_loop(WIDTH, 512)
    def _(at):
        wide_ref[4, :, at] = jax.nn.sigmoid(dot(mix_ref[2], square[RECEPTANCE, :, at]))

    if square_done is not None:
        square_done()

    def hidden(j):
        at = pl.ds(pl.multiple_of(j * 512, 512), 512)
        within = pl.ds(pl.multiple_of((j & 1) * 512, 512), 512)
        active = jnp.maximum(dot(mix_ref[1], keys[j >> 1, :, within]), 0.0)
        act_ref[:, at] = active.astype(BF16)
        hid_ref[:, at] = (active * active).astype(BF16)

    def leave(at, channel):
        wide_ref[3, :, at] = channel
        lay_ref[:, at] = (wide_ref[2, :, at] + wide_ref[4, :, at] * channel).astype(BF16)

    def part(b, at):
        return dot(hid_ref[:, b * WIDTH : (b + 1) * WIDTH], payload[b, :, at])

    if not streamed:
        pl.loop(0, INNER // 512)(hidden)

        @columns_loop(WIDTH, 256)
        def _(at):
            leave(at, part(0, at) + part(1, at) + part(2, at) + part(3, at))

    else:
        for b in range(4):
            ready(5 + b)
            pl.loop(2 * b, 2 * b + 2)(hidden)
        for b in range(4):
            ready(9 + b)

            @columns_loop(WIDTH, 512)
            def _(at, b=b):
                channel = part(b, at)
                if b > 0:
                    channel = channel + wide_ref[3, :, at]
                if b < 3:
                    wide_ref[3, :, at] = channel
                else:
                    leave(at, channel)

    out_ref[...] = lay_ref[...]


def groups(refs, *sizes):
    cut, at = [], 0
    for size in sizes:
        cut.append(refs[at : at + size])
        at += size
    return cut + [refs[at:]]


def weight_pieces(maps, emission, key, payload, receptance):
    pieces = [maps.at[j] for j in range(3)] + [emission, receptance]
    for b in range(4):
        pieces.append(key.at[:, pl.ds(b * WIDTH, WIDTH)])
    for b in range(4):
        pieces.append(payload.at[pl.ds(b * WIDTH, WIDTH), :])
    return pieces


def forward_first_kernel(section, dp, begins, x_ref, *refs):
    small_in, hbm, (out_ref,), consts, kept, saved, edges, rest = groups(
        refs, N_CONSTS, 5, 1, N_CONSTS, N_WEIGHTS, N_SAVED, N_EDGES
    )
    section, _, _, core = coordinates(section, dp)
    sem, small_sem = rest[-2:]
    copies = [
        pltpu.make_async_copy(source, target, sem.at[i])
        for i, (source, target) in enumerate(
            zip(
                weight_pieces(*hbm),
                [ref.at[i] for ref, n in zip(kept, BLOCKS) for i in range(n)],
            )
        )
    ]
    arriving = [pltpu.make_async_copy(x_ref, saved[0], small_sem.at[N_CONSTS])]
    for i in range(N_CONSTS):
        arriving.append(pltpu.make_async_copy(small_in[i], consts[i], small_sem.at[i]))
    for c in arriving + copies[:WINDOW]:
        c.start()
    for c in arriving:
        c.wait()

    def ready(i):
        copies[i].wait()
        if i + WINDOW < len(copies):
            copies[i + WINDOW].start()

    @pl.when(section == 0)
    def _():
        marks = [begins[s].astype(F32) for s in range(SEQS)]
        forward_body(
            core, marks, None, consts, kept, ready, out_ref, saved, edges, rest[:-2]
        )

    @pl.when(section != 0)
    def _():
        for c in copies[WINDOW:]:
            c.start()
        for c in copies:
            c.wait()


def flip(ref):
    side = 256
    for i in range(WIDTH // side):
        for j in range(i + 1):
            one = (slice(i * side, (i + 1) * side), slice(j * side, (j + 1) * side))
            two = (one[1], one[0])
            first = ref[one].T
            if i != j:
                ref[one] = ref[two].T
            ref[two] = first


def flip_slowly(ref):
    side = 256

    @pl.loop(0, 10)
    def _(pair):
        i = jnp.int32(pair >= 1) + jnp.int32(pair >= 3) + jnp.int32(pair >= 6)
        j = pair - ((i * (i + 1)) >> 1)
        row, column = (pl.ds(pl.multiple_of(t * side, side), side) for t in (i, j))
        first, second = ref[row, column].T, ref[column, row].T
        ref[row, column] = second
        ref[column, row] = first


def forward_kernel(layer, last, section, dp, begins, x_ref, *refs):
    early, own = layer == 1, layer == last
    _, given, (out_ref,), consts, kept, saved, edges, kept_away, rest = groups(
        refs,
        N_BASE + N_EDGES,
        5 if early else 1 if own else 0,
        1, N_CONSTS, N_WEIGHTS, N_SAVED, N_EDGES,
        2 if early else 0,
    )
    scratch, sem = (rest[:-1], rest[-1]) if early or own else (rest, None)
    section, _, _, core = coordinates(section, dp)

    @pl.when(section == layer)
    def _():
        marks = [begins[s].astype(F32) for s in range(SEQS)]
        square = pltpu.make_async_copy(given[0], kept[0], sem.at[0]) if own else None
        forward_body(
            core, marks, x_ref, consts, kept, lambda i: None, out_ref, saved, edges, scratch,
            square.start if own else None,
        )
        if own:
            square.wait()

    if early:

        @pl.when(section == last)
        def _():
            for ref, n in zip(kept[:2], BLOCKS):

                @pl.loop(0, n)
                def _(i, ref=ref):
                    flip_slowly(ref.at[i])

            away = [
                pltpu.make_async_copy(kept[i], kept_away[i], sem.at[i]) for i in range(2)
            ]
            for c in away:
                c.start()
            for c in away:
                c.wait()
            targets = [ref.at[i] for ref, n in zip(kept[:2], BLOCKS) for i in range(n)]
            back = [
                pltpu.make_async_copy(source, target, sem.at[i])
                for i, (source, target) in enumerate(zip(weight_pieces(*given), targets))
            ]
            for c in back:
                c.start()
            for c in back:
                c.wait()


def norm_back(rows, gain, offset, first, parts, vec_out, prior_out, marks):
    unit, scale = normed_rows(rows)
    normed = unit * gain + offset
    change = normed - moved_down(normed, first)
    up, stay = None, None
    for grad, weight, row in parts:
        vec_out(row, jnp.sum(grad * change, axis=0, keepdims=True))
        kept = grad * weight
        passed = grad - kept
        stay = kept if stay is None else stay + kept
        up = passed if up is None else up + passed
    for s in range(SEQS):
        prior_out(s, up[s * LENGTH : s * LENGTH + 1, :] * marks[s])
    grad = stay + moved_up(up)
    return unit, scale, grad


def backward_kernel(first, layer, section, dp, begins, dy_ref, *refs):
    _, given, (out_ref,), consts, kept, saved, grads, scratch = groups(
        refs,
        N_BASE + (0 if first else N_GRADS),
        1 if first else 0,
        1, N_CONSTS, N_WEIGHTS, N_SAVED, N_GRADS,
    )
    vec_ref, fade_ref, prior_ref = consts[0], consts[1], consts[6]
    square, keys, payload = kept
    ent_ref, lay_ref, act_ref, wide_ref, scan_ref = saved
    ing_ref, keep_one, send_one, keep_two, send_two, stg_ref, rowg_ref = grads
    sg, sdk, sdv, small, wide, wide_two, wide_three, wide_four, dys_ref, dhp_ref, vecg_ref = scratch[:11]
    section, y, z, core = coordinates(section, dp)
    def vec_out(row, value):
        vecg_ref[row : row + 1, :] = value

    def store(keep_ref, send_ref, items, shared=None):
        for this in range(2):

            @pl.when(core == this)
            def _(this=this):
                @pl.loop(0, 4)
                def _(q):
                    for which, column, size, value in items:
                        ref = keep_ref if which == this else send_ref
                        distance = (q - (y if which else z)) & 3
                        ref[distance, :, column : column + size] = value(q)
                    if shared is not None:
                        ref = keep_ref if this == 1 else send_ref
                        ref[q, 0:64, 512:768] = shared

    def quarter(row):
        return lambda q: dys_ref[row, :, pl.ds(pl.multiple_of(q * 256, 256), 256)]

    def pull(grad, blocks, i, at):
        if first and blocks is payload:
            return against(grad, blocks[i, at, :])
        return dot(grad, blocks[i, :, at])

    def through_payload(grad, j):
        return pull(grad, payload, j >> 1, pl.ds(pl.multiple_of((j & 1) * 512, 512), 512))

    def through_key(grad_ref, j):
        at = pl.ds(pl.multiple_of(j * 256, 256), 256)
        total = None
        for b in range(4):
            part = pull(grad_ref[:, b * WIDTH : (b + 1) * WIDTH], keys, b, at)
            total = part if total is None else total + part
        return total

    @pl.when(section == layer)
    def _():
        marks = [begins[s].astype(F32) for s in range(SEQS)]
        if first:
            key_copy = pltpu.make_async_copy(given[0], keys, scratch[11].at[0])
            key_copy.start()
        dy = dy_ref[...].astype(F32)
        gate = wide_ref[4]
        through = dy * gate
        dys_ref[4] = through.astype(BF16)
        dys_ref[5] = (through * wide_ref[3] * (1.0 - gate)).astype(BF16)

        @pl.loop(0, INNER // 512, unroll=2)
        def _(j):
            at = pl.ds(pl.multiple_of(j * 512, 512), 512)
            part = through_payload(dys_ref[4], j)
            dhp_ref[:, at] = (2.0 * act_ref[:, at].astype(F32) * part).astype(BF16)

        def hidden(start):
            return lambda q: dhp_ref[:, pl.ds(pl.multiple_of(start + q * 512, 512), 512)]

        store(
            keep_one, send_one,
            ((0, 0, 512, hidden(0)), (1, 0, 512, hidden(2048)),
             (0, 512, 256, quarter(4)), (1, 512, 256, quarter(4))),
        )

        if first:
            key_copy.wait()

        @pl.loop(0, WIDTH // 256)
        def _(j):
            at = pl.ds(pl.multiple_of(j * 256, 256), 256)
            wide[:, at] = through_key(dhp_ref, j)
            wide_two[:, at] = pull(dys_ref[5], square, RECEPTANCE, at)

        def prior_two(s, value):
            rowg_ref[1, s : s + 1, :] = value

        gain = vec_ref[5]
        unit, scale, grad = norm_back(
            wide_ref[2], gain, vec_ref[6], first_rows(prior_ref, 1, marks),
            ((wide[...], vec_ref[7], 7), (wide_two[...], vec_ref[8], 8)),
            vec_out, prior_two, marks,
        )
        vec_out(5, jnp.sum(grad * unit, axis=0, keepdims=True))
        vec_out(6, jnp.sum(grad, axis=0, keepdims=True))
        grad = grad * gain
        mean = jnp.mean(grad, axis=-1, keepdims=True)
        along = jnp.mean(grad * unit, axis=-1, keepdims=True)
        middle = dy_ref[...].astype(F32) + scale * (grad - mean - unit * along)
        wide_three[...] = middle
        dys_ref[3] = middle.astype(BF16)

        for q in range(4):
            at = pl.ds(q * 256, 256)
            part = pull(dys_ref[3], square, EMISSION, at)
            dys_ref[2, :, at] = (part * wide_ref[1, :, at]).astype(BF16)
            wide[:, at] = part * wide_ref[0, :, at]

        for g in range(GROUPS):
            to_tokens(sg, g, wide[:, g * 128 : (g + 1) * 128])

        zero = jnp.zeros((GROUPS, 128), F32)

        def token(t, carry):
            carry_next = []
            boosted, faded = carry[4], carry[5]
            for s in range(SEQS):
                dnum, dden = carry[2 * s : 2 * s + 2]
                at = pl.ds(pl.multiple_of((t + LENGTH * s) * GROUPS, GROUPS), GROUPS)
                g = sg[at, :]
                value = scan_ref[7, at, :]
                beyond = scan_ref[2, at, :]
                keep = scan_ref[3, at, :]
                new = scan_ref[4, at, :]
                from_old = scan_ref[0, at, :] * g
                from_new = scan_ref[1, at, :] * g
                direct = from_new * beyond
                boosted = boosted + direct
                sdv[at, :] = from_new + new * dnum
                sdk[at, :] = direct + new * (dnum * value + dden)
                faded = faded - keep * (dnum * scan_ref[5, at, :] + dden * scan_ref[6, at, :])
                carry_next += [
                    from_old + keep * dnum,
                    keep * dden - from_old * (value - beyond),
                ]
            return tuple(carry_next) + (boosted, faded)

        def tokens(block, carry):
            for j in range(8):
                carry = token(LENGTH - 1 - block * 8 - j, carry)
            return carry

        ends = lax.fori_loop(0, LENGTH // 8, tokens, (zero,) * 6)

        def spread(put_piece, value):
            small[...] = value
            for g in range(GROUPS):
                put_piece(slice(g * 128, (g + 1) * 128), small[g : g + 1, :])

        for s in range(SEQS):
            dnum, dden = ends[2 * s : 2 * s + 2]
            at = pl.ds(LENGTH * s * GROUPS, GROUPS)
            moved = dnum * scan_ref[5, at, :] + dden * scan_ref[6, at, :]
            for k, value in enumerate((dnum, dden, moved)):

                def put_state(cols, piece, k=k, s=s):
                    stg_ref[k, s : s + 1, cols] = piece

                spread(put_state, value * marks[s])

        def put_decay(cols, piece):
            vecg_ref[9:10, cols] = piece

        def put_boost(cols, piece):
            vecg_ref[10:11, cols] = piece

        spread(put_decay, ends[5])
        vecg_ref[9:10, :] = vecg_ref[9:10, :] * jnp.exp(fade_ref[0:1, :])
        spread(put_boost, ends[4])

        for g in range(GROUPS):
            at = slice(g * 128, (g + 1) * 128)
            dys_ref[0, :, at] = from_tokens(sdk, g).astype(BF16)
            dys_ref[1, :, at] = from_tokens(sdv, g).astype(BF16)
        rows = ent_ref[...].astype(F32)
        pulled = (wide, wide_two, wide_four)
        for j in range(3):

            @columns_loop(WIDTH, 512)
            def _(at, j=j):
                pulled[j][:, at] = pull(dys_ref[j], square, j, at)


        def prior_one(s, value):
            rowg_ref[0, s : s + 1, :] = value

        gain = vec_ref[0]
        unit, scale, grad = norm_back(
            rows, gain, vec_ref[1], first_rows(prior_ref, 0, marks),
            [(pulled[j][...], vec_ref[2 + j], 2 + j) for j in range(3)],
            vec_out, prior_one, marks,
        )
        vec_out(0, jnp.sum(grad * unit, axis=0, keepdims=True))
        vec_out(1, jnp.sum(grad, axis=0, keepdims=True))
        packed = jnp.concatenate(
            [vecg_ref[:, b * 256 : (b + 1) * 256] for b in range(4)], axis=0
        ).astype(BF16)
        store(
            keep_two, send_two,
            ((0, 0, 256, quarter(0)), (0, 256, 256, quarter(1)), (0, 512, 256, quarter(2)),
             (1, 0, 256, quarter(5)), (1, 256, 256, quarter(3))),
            packed,
        )
        grad = grad * gain
        mean = jnp.mean(grad, axis=-1, keepdims=True)
        along = jnp.mean(grad * unit, axis=-1, keepdims=True)
        entry = (wide_three[...] + scale * (grad - mean - unit * along)).astype(BF16)
        ing_ref[...] = entry
        out_ref[...] = entry

    if first:

        @pl.when(section != layer)
        def _():
            for ref, n in zip(kept, BLOCKS):

                @pl.loop(0, n)
                def _(i, ref=ref):
                    flip(ref.at[i])


def join_edges_kernel(first, second, out, sem):
    copies = [
        pltpu.make_async_copy(ref, out.at[pl.ds(h * EDGE, EDGE), :], sem.at[h])
        for h, ref in enumerate((first, second))
    ]
    for c in copies:
        c.start()
    for c in copies:
        c.wait()


def join_kernel(first, second, *outs):
    for k in range(4):
        outs[k][:ROWS, :] = first[k]
        outs[k][ROWS:, :] = second[k]


def mixes_kernel(section, dp, own, one, two, three, vec_ref, wa, *refs):
    x_one, x_two, *scratch = refs[-10:]
    edge, wide, stage, hidden, first_mix, edge_sem, wide_sem, out_sem = scratch
    core = coordinates(section, dp)[3]

    def load(n):
        block = (own, one, two, three)[n // 2]
        return pltpu.make_async_copy(
            block.at[pl.ds(n % 2 * EDGE, EDGE), :], edge.at[n], edge_sem.at[n]
        )

    def columns(u):
        return [
            pltpu.make_async_copy(
                wa.at[:, pl.ds(pl.multiple_of((16 * u + 2 * j + core) * 128, 128), 128)],
                wide.at[:, pl.ds(j * 128, 128)],
                wide_sem.at[j],
            )
            for j in range(8)
        ]

    def out_mixes(n):
        rows = pl.ds(pl.multiple_of(n * ROWS, ROWS), ROWS)
        return pltpu.make_async_copy(
            stage.at[n & 1], x_two.at[:, rows, :], out_sem.at[n & 1]
        )

    def out_hidden(u, t):
        cols = pl.ds(pl.multiple_of(t * 256, 256), 256)
        return pltpu.make_async_copy(
            hidden.at[t & 1], x_one.at[u, :, cols], out_sem.at[2 + (t & 1)]
        )

    out_first = pltpu.make_async_copy(first_mix, x_one.at[2], out_sem.at[4])

    def mix(normed, below, j):
        v = vec_ref[j]
        return (normed * v + below * (1.0 - v)).astype(BF16)

    for n in range(8):
        load(n).start()
    for c in columns(0):
        c.start()
    for n in range(8):
        load(n).wait()

    @pl.loop(0, 8)
    def _(n):
        @pl.when(n >= 2)
        def _():
            out_mixes(n - 2).wait()

        block, here = edge.at[n], stage.at[n & 1]

        def parts(c):
            cols = slice(c * WIDTH, (c + 1) * WIDTH)
            normed = block[:ROWS, cols].astype(F32)
            first = block[ROWS:, cols].astype(F32)
            return normed, moved_down(normed, (first[0:1, :], first[1:2, :]))

        normed, below = parts(0)
        first_mix[pl.ds(pl.multiple_of(n * ROWS, ROWS), ROWS), :] = mix(normed, below, 7)

        @pl.when(core == 0)
        def _():
            normed, below = parts(1)
            for j in range(3):
                here[j] = mix(normed, below, 2 + j)

        @pl.when(core == 1)
        def _():
            here[0] = mix(normed, below, 8)
            here[1] = block[:ROWS, WIDTH:]

        out_mixes(n).start()

    out_first.start()
    for u in range(2):
        for c in columns(u):
            c.wait()

        @pl.loop(0, 4)
        def _(t, u=u):
            @pl.when(t >= 2)
            def _():
                out_hidden(u, t - 2).wait()

            cols = pl.ds(pl.multiple_of(t * 256, 256), 256)
            for r in range(4):
                rows = slice(r * 256, (r + 1) * 256)
                active = jnp.maximum(dot(first_mix[rows, :], wide[:, cols]), 0.0)
                hidden[t & 1, rows, :] = (active * active).astype(BF16)
            out_hidden(u, t).start()

        if u == 0:
            for c in columns(1):
                c.start()
        for t in (2, 3):
            out_hidden(u, t).wait()
    for n in (6, 7):
        out_mixes(n).wait()
    out_first.wait()


def drain_kernel(layer, entry, states, firsts, *refs):
    results, sem = refs[:-1], refs[-1]
    sources = (layer, entry) + tuple(states.at[k] for k in range(3)) + (firsts,)
    copies = [
        pltpu.make_async_copy(source, target, sem.at[i])
        for i, (source, target) in enumerate(zip(sources, results))
    ]
    for c in copies:
        c.start()
    for c in copies:
        c.wait()


def row_starts(y, z, core):
    starts = []
    for there in range(16):
        along_y, along_z = (there // 4 - y) & 3, (there % 4 - z) & 3
        summed = jnp.where(core == 0, along_y, along_z)
        joined = jnp.where(core == 0, along_z, along_y)
        starts.append(pl.multiple_of(summed * 256 + joined * 64, 64))
    return starts


def weight_kernel(second, section, dp, x_ref, *refs):
    blocks, outs = refs[:4], refs[4:8]
    dy, share = refs[8:]
    _, y, z, core = coordinates(section, dp)
    for k in range(4):
        dy[k * 2 * ROWS : (k + 1) * 2 * ROWS, :] = blocks[k][...]
    starts = row_starts(y, z, core)

    def unit(u, size, source, target):
        for c in range(0, WIDTH, 256):
            part = across(x_ref[u, :, c : c + 256], dy[:, source : source + size]).astype(BF16)
            for b in range(4):
                share[pl.ds(starts[c // 64 + b], 64), target : target + size] = part[
                    b * 64 : (b + 1) * 64, :
                ]

    if not second:
        unit(2, 512, 0, 0)
        for u in range(2):
            for c in range(0, WIDTH, 256):
                part = across(x_ref[u, :, c : c + 256], dy[:, 512:768]).astype(BF16)
                for b in range(2):
                    start = starts[(u * WIDTH + c) // 128 + b]
                    for half in range(2):
                        share[pl.ds(start, 64), 512 + half * 256 : 768 + half * 256] = part[
                            b * 128 + half * 64 : b * 128 + (half + 1) * 64, :
                        ]
    else:
        unit(0, 256, 0, 0)
        unit(1, 256, 256, 256)

        @pl.when(core == 0)
        def _():
            unit(2, 256, 512, 512)

        @pl.when(core == 1)
        def _():
            total = jnp.zeros((64, 256), F32)
            for d in range(8):
                total = total + dy[d * ROWS : d * ROWS + 64, 512:768].astype(F32)
            for b in range(4):
                piece = jnp.concatenate(
                    [total[b * 16 : (b + 1) * 16, :], jnp.zeros((112, 256), F32)], axis=0
                ).T.astype(BF16)
                for e in range(4):
                    at = pl.ds(starts[b * 4 + e], 64)
                    share[at, 512:640] = piece[e * 64 : (e + 1) * 64, :]
                    share[at, 640:768] = jnp.zeros((64, 128), BF16)

    for k in range(4):
        outs[k][...] = share[k * 256 : (k + 1) * 256, :]


def sum_kernel(own, one, two, three, *outs):
    for k in range(4):

        @pl.loop(0, 4)
        def _(i, k=k):
            at = pl.ds(pl.multiple_of(k * 64 + i * 16, 16), 16)
            total = own[at, :].astype(F32) + one[at, :].astype(F32) + two[at, :].astype(F32)
            total = total + three[at, :].astype(F32)
            outs[k][pl.ds(pl.multiple_of(i * 16, 16), 16), :] = total.astype(BF16)


def gather_kernel(second, section, dp, own, one, two, three, keep_ref, send_ref, *payload):
    _, y, z, core = coordinates(section, dp)
    here = jnp.where(core == 0, z, y)
    mine = pl.multiple_of(core * 32, 32)
    theirs = pl.multiple_of(32 - core * 32, 32)
    for k, ref in enumerate((own, one, two, three)):
        quarter = (here - k) & 3
        for rows, target in ((mine, keep_ref), (theirs, send_ref)):
            if not second:
                at = pl.ds(pl.multiple_of(quarter * 512, 512), 512)
                target[:, at] = ref[pl.ds(rows, 32), 0:512]
            else:
                for u in range(3):
                    at = pl.ds(pl.multiple_of(u * WIDTH + quarter * 256, 256), 256)
                    target[:, at] = ref[pl.ds(rows, 32), u * 256 : (u + 1) * 256]
        if not second:
            at = pl.ds(pl.multiple_of(quarter * 256, 256), 256)
            for half in range(2):
                payload[0][half * 64 : (half + 1) * 64, at] = ref[
                    :, 512 + half * 256 : 768 + half * 256
                ].astype(F32)


def final_kernel(second, section, dp, kept, come, *outs):
    core = coordinates(section, dp)[3]

    def write(set_zero, set_one):
        if not second:
            outs[0][:, 0:2048] = set_zero[...].astype(F32)
            outs[0][:, 2048:4096] = set_one[...].astype(F32)
            return
        proj_ref, out_ref, gate_ref, vec_ref, dec_ref, boo_ref = outs
        for u in range(3):
            proj_ref[u] = set_zero[:, u * WIDTH : (u + 1) * WIDTH].astype(F32)
        gate_ref[...] = set_one[:, 0:1024].astype(F32)
        out_ref[...] = set_one[:, 1024:2048].astype(F32)
        vectors = set_one[:, 2048:2176].astype(F32).T
        for j in range(9):
            vec_ref[j] = vectors[j : j + 1, :]
        dec_ref[...] = vectors[9:10, :]
        boo_ref[...] = vectors[10:11, :]

    @pl.when(core == 0)
    def _():
        write(kept, come)

    @pl.when(core == 1)
    def _():
        write(come, kept)


def plain(shapes):
    return tuple(jax.ShapeDtypeStruct(s, d) for s, d in shapes)


def in_vmem(shapes):
    return tuple(pltpu.VMEM(s, d) for s, d in shapes)


def hold(arrays):
    return tuple(pltpu.with_memory_space_constraint(a, pltpu.VMEM) for a in arrays)


def in_hbm(*arrays):
    return tuple(pltpu.with_memory_space_constraint(a, pltpu.HBM) for a in arrays)


def array(*shape, kind=BF16):
    return jax.ShapeDtypeStruct(shape, kind)


ROWS_OUT = array(ROWS, WIDTH)
TOKENS = pltpu.VMEM((ROWS * GROUPS, 128), F32)
SMALL = pltpu.VMEM((GROUPS, 128), F32)
WIDE = pltpu.VMEM((ROWS, WIDTH), F32)
FORWARD_SCRATCH = [
    TOKENS, TOKENS, TOKENS, SMALL,
    pltpu.VMEM((4, ROWS, WIDTH), BF16),
    pltpu.VMEM((ROWS, INNER), BF16),
]
DMA = pltpu.SemaphoreType.DMA


def forward_first(place, begins, rows, small, weights):
    shapes = CONSTS + WEIGHTS + SAVED + EDGES
    results = pl.pallas_call(
        forward_first_kernel,
        cost_estimate=cost(12),
        out_shape=(ROWS_OUT,) + in_vmem(shapes),
        in_specs=[SM] * 3 + [HB] * (1 + N_CONSTS + 5),
        out_specs=(VM,) * (1 + len(shapes)),
        scratch_shapes=FORWARD_SCRATCH + [DMA((13,)), DMA((N_CONSTS + 1,))],
        compiler_params=limit(HELD_LIMIT),
    )(*place, begins, *in_hbm(rows, *small, *weights))
    return results[0], results[1:]


def forward_next(layer, last, place, begins, rows, held, given=()):
    shapes = CONSTS + WEIGHTS + SAVED + EDGES
    away = tuple(pltpu.HBM(s, d) for s, d in WEIGHTS[:2]) if layer == 1 else ()
    results = pl.pallas_call(
        functools.partial(forward_kernel, layer, last),
        cost_estimate=cost(10),
        out_shape=(ROWS_OUT,) + plain(shapes) + away,
        in_specs=[SM] * 3 + [VM] * (1 + len(shapes)) + [HB] * len(given),
        out_specs=(VM,) * (1 + len(shapes)) + (HB,) * len(away),
        input_output_aliases={4 + i: 1 + i for i in range(len(shapes))},
        scratch_shapes=FORWARD_SCRATCH + ([DMA((9,))] if given else []),
        compiler_params=limit(HELD_LIMIT),
    )(*place, begins, *hold((rows,)), *hold(held), *in_hbm(*given))
    return results[0], results[1 : 1 + len(shapes)], results[1 + len(shapes) :]


def backward_call(layer, place, begins, grad, held, given=()):
    first = len(held) == N_BASE
    base = CONSTS + WEIGHTS + SAVED
    results = pl.pallas_call(
        functools.partial(backward_kernel, first, layer),
        cost_estimate=cost(BACK_COST[layer]),
        out_shape=(ROWS_OUT,) + plain(base) + (in_vmem(GRADS) if first else plain(GRADS)),
        in_specs=[SM] * 3 + [VM] * (1 + len(held)) + [HB] * len(given),
        out_specs=(VM,) * (1 + N_BASE + N_GRADS),
        input_output_aliases={4 + i: 1 + i for i in range(len(held))},
        scratch_shapes=[
            TOKENS, TOKENS, TOKENS, SMALL, WIDE, WIDE, WIDE, WIDE,
            pltpu.VMEM((6, ROWS, WIDTH), BF16),
            pltpu.VMEM((ROWS, INNER), BF16),
            pltpu.VMEM((16, WIDTH), F32),
        ]
        + ([DMA((1,))] if given else []),
        compiler_params=limit(HELD_LIMIT),
    )(*place, begins, *hold((grad,)), *hold(held), *in_hbm(*given))
    return results[0], results[1:]


def cost(microseconds):
    return pl.CostEstimate(
        flops=int(microseconds * FLOPS), bytes_accessed=0, transcendentals=0
    )


def join_edges(first, second):
    return pl.pallas_call(
        join_edges_kernel,
        cost_estimate=cost(3),
        out_shape=pltpu.HBM((2 * EDGE, 2 * WIDTH), BF16),
        in_specs=[VM, VM],
        out_specs=HB,
        scratch_shapes=[DMA((2,))],
        compiler_params=limit(1),
    )(*hold((first, second)))


def join(first, second):
    return pl.pallas_call(
        join_kernel,
        cost_estimate=cost(1),
        out_shape=in_vmem((((2 * ROWS, QUARTER), BF16),) * 4),
        in_specs=[VM, VM],
        out_specs=(VM,) * 4,
        compiler_params=limit(HELD_LIMIT),
    )(*hold((first, second)))


MIXES_SCRATCH = [
    pltpu.VMEM((8, EDGE, 2 * WIDTH), BF16),
    pltpu.VMEM((WIDTH, WIDTH), BF16),
    pltpu.VMEM((2, 3, ROWS, WIDTH), BF16),
    pltpu.VMEM((2, 8 * ROWS, 256), BF16),
    pltpu.VMEM((8 * ROWS, WIDTH), BF16),
    DMA((8,)),
    DMA((8,)),
    DMA((5,)),
]
X_HALF = pltpu.HBM((3, 8 * ROWS, WIDTH), BF16)


def mixes(place, blocks, vec, wa):
    return pl.pallas_call(
        mixes_kernel,
        cost_estimate=cost(15),
        out_shape=(X_HALF, X_HALF),
        in_specs=[SM] * 2 + [HB] * 4 + [VM, HB],
        out_specs=(HB, HB),
        scratch_shapes=MIXES_SCRATCH,
        compiler_params=limit(HELD_LIMIT),
    )(*place, *in_hbm(*blocks), vec, *in_hbm(wa))


def drained(layer, entry, states, firsts):
    rows, state = pltpu.HBM((ROWS, WIDTH), BF16), pltpu.HBM((SEQS, WIDTH), F32)
    return pl.pallas_call(
        drain_kernel,
        cost_estimate=cost(1),
        out_shape=(rows, rows, state, state, state, pltpu.HBM((2, SEQS, WIDTH), F32)),
        in_specs=[HB] * 4,
        out_specs=(HB,) * 6,
        scratch_shapes=[DMA((6,))],
        compiler_params=limit(1),
    )(layer, entry, states, firsts)


def weight_grads(second, place, x, blocks):
    columns = SHARES[second]
    return pl.pallas_call(
        functools.partial(weight_kernel, second),
        cost_estimate=cost(4),
        out_shape=in_vmem((((2 * ROWS, columns), BF16),) * 4),
        in_specs=[SM] * 2 + [VM] * 5,
        out_specs=(VM,) * 4,
        scratch_shapes=[
            pltpu.VMEM((8 * ROWS, QUARTER), BF16),
            pltpu.VMEM((8 * ROWS, columns), BF16),
        ],
        compiler_params=limit(HELD_LIMIT),
    )(*place, *hold((x, *blocks)))


def summed(second, shares):
    return pl.pallas_call(
        sum_kernel,
        cost_estimate=cost(1),
        out_shape=in_vmem((((64, SHARES[second]), BF16),) * 4),
        in_specs=[VM] * 4,
        out_specs=(VM,) * 4,
        compiler_params=limit(HELD_LIMIT),
    )(*hold(shares))


def gathered(second, place, parts):
    outs = in_vmem((((32, 3 * WIDTH), BF16),) * 2)
    if not second:
        outs = in_vmem((((32, 2 * WIDTH), BF16),) * 2) + (pltpu.HBM((ROWS, WIDTH), F32),)
    return pl.pallas_call(
        functools.partial(gather_kernel, second),
        cost_estimate=cost(1),
        out_shape=outs,
        in_specs=[SM] * 2 + [VM] * 4,
        out_specs=(VM,) * len(outs),
        compiler_params=limit(HELD_LIMIT),
    )(*place, *hold(parts))


def final(second, place, kept, come):
    outs = (
        array(3, 32, WIDTH, kind=F32),
        array(32, WIDTH, kind=F32),
        array(32, WIDTH, kind=F32),
        array(9, 1, 32, kind=F32),
        array(1, 32, kind=F32),
        array(1, 32, kind=F32),
    )
    if not second:
        outs = (array(32, INNER, kind=F32),)
    return pl.pallas_call(
        functools.partial(final_kernel, second),
        cost_estimate=cost(1),
        out_shape=outs,
        in_specs=[SM] * 2 + [VM] * 2,
        out_specs=(VM,) * len(outs),
        compiler_params=limit(HELD_LIMIT),
    )(*place, *hold((kept, come)))


def device(y, z, core):
    return (y * 4 + z) * 2 + core


def swapped(block):
    return lax.ppermute(block, "dp", [(d, d ^ 1) for d in range(32)])


def sent(block, distance, first_axis):
    route = []
    for y in range(4):
        for z in range(4):
            for core in range(2):
                if (core == 0) == first_axis:
                    there = device(y, (z + distance) % 4, core)
                else:
                    there = device((y + distance) % 4, z, core)
                route.append((device(y, z, core), there))
    return lax.ppermute(block, "dp", route)


def body(
    bottom_stack_feed,
    loss_sensitivity,
    resumes_segment,
    mixing_coefficients,
    fading_log,
    feature_boost,
    attention_maps,
    emission_coefficients,
    feature_addressing,
    feature_payload,
    feature_receptance,
    dividend_memory,
    divisor_memory,
    memory_power_shift,
    prior_normed_lines,
):
    sections = lax.axis_size("section")
    place = (lax.axis_index("section")[None], lax.axis_index("dp")[None])
    begins = resumes_segment
    vec = jnp.swapaxes(mixing_coefficients, 0, 1)
    small = (
        vec,
        fading_log,
        feature_boost,
        dividend_memory[0],
        divisor_memory[0],
        memory_power_shift[0],
        prior_normed_lines[0],
    )
    weights = (
        attention_maps[0],
        emission_coefficients[0],
        feature_addressing[0],
        feature_payload[0],
        feature_receptance[0],
    )
    rows, held = forward_first(
        place, begins, bottom_stack_feed.reshape(ROWS, WIDTH), small, weights
    )
    for t in range(1, sections):
        rows = lax.ppermute(rows, "section", [(t - 1, t)])
        given = weights if t == 1 else away[:1] if t == sections - 1 else ()
        rows, held, made = forward_next(t, sections - 1, place, begins, rows, held, given)
        away = made if t == 1 else away
    held, edges = held[:N_BASE], held[N_BASE:]
    grad, held = backward_call(
        sections - 1, place, begins, loss_sensitivity.reshape(ROWS, WIDTH), held, away[1:]
    )
    grad = lax.ppermute(grad, "section", [(sections - 1, sections - 2)])
    own = join_edges(edges[0], swapped(edges[1]))
    blocks = (own,) + tuple(sent(own, k, True) for k in range(1, 4))
    for t in range(sections - 2, -1, -1):
        if t == sections - 3:
            x = mixes(place, blocks, vec, weights[2])
            begins, *x = lax.optimization_barrier((begins, *x))
        grad, held = backward_call(t, place, begins, grad, held)
        if t > 0:
            grad = lax.ppermute(grad, "section", [(t, t - 1)])
    entry_grad, *row_sets, state_grads, row_grads = held[N_BASE:]
    layer = held[N_CONSTS + N_WEIGHTS + 1]
    layer, entry_grad, *state_grads, row_grads = drained(
        layer, entry_grad, state_grads, row_grads
    )

    def half(second, after=None):
        keep, send = row_sets[2 * second : 2 * second + 2]
        if after is not None:
            send, *_ = lax.optimization_barrier((send, *after))
        pieces = join(keep, swapped(send))
        joined = pieces[0]
        pieces = (pieces[0],) + tuple(sent(pieces[k], k, True) for k in range(1, 4))
        shares = weight_grads(second, place, x[second], pieces)
        shares = (shares[0],) + tuple(sent(shares[k], k, False) for k in range(1, 4))
        parts = summed(second, shares)
        parts = (parts[0],) + tuple(sent(parts[k], k, True) for k in range(1, 4))
        kept, going, *payload = gathered(second, place, parts)
        return final(second, place, kept, swapped(going)), payload, joined

    (key,), (payload,), joined = half(False, x)
    (projection, out_weight, gate, vectors, decay, boost), _, _ = half(True, (joined, row_grads))
    return (
        layer.reshape(1, SEQS, LENGTH, WIDTH),
        entry_grad.reshape(1, SEQS, LENGTH, WIDTH),
        jnp.swapaxes(vectors, 0, 1),
        decay,
        boost,
        projection[None],
        out_weight[None],
        key[None],
        payload[None],
        gate[None],
        state_grads[0][None],
        state_grads[1][None],
        state_grads[2][None],
        row_grads[None],
    )


def solution(mesh):
    placed = (
        P("dp", None, None),
        P("dp", None, None),
        P("dp"),
        P("section", None, None),
        P("section", None),
        P("section", None),
        P("section", None, None, None),
        P("section", None, None),
        P("section", None, None),
        P("section", None, None),
        P("section", None, None),
        P("section", "dp", None),
        P("section", "dp", None),
        P("section", "dp", None),
        P("section", None, "dp", None),
    )
    return jax.shard_map(
        body,
        mesh=mesh,
        in_specs=placed,
        out_specs=(
            P("section", "dp", None, None),
            P("section", "dp", None, None),
            P("section", None, "dp"),
            P("section", "dp"),
            P("section", "dp"),
            P("section", None, "dp", None),
            P("section", "dp", None),
            P("section", "dp", None),
            P("section", "dp", None),
            P("section", "dp", None),
            P("section", "dp", None),
            P("section", "dp", None),
            P("section", "dp", None),
            P("section", None, "dp", None),
        ),
        check_vma=False,
    )
```

```python
import functools

import jax
import jax.numpy as jnp
from jax import lax
from jax.experimental import pallas as pl
from jax.experimental.pallas import tpu as pltpu
from jax.sharding import PartitionSpec as P

WIDTH = 1024
INNER = 4096
LENGTH = 64
SEQS = 2
ROWS = SEQS * LENGTH
GROUPS = WIDTH // 128
FRESH = -1e30
EPS = 1e-05
F32 = jnp.float32
BF16 = jnp.bfloat16

VM = pl.BlockSpec(memory_space=pltpu.VMEM)
HB = pl.BlockSpec(memory_space=pl.ANY)
SM = pl.BlockSpec(memory_space=pltpu.SMEM)
EDGE = ROWS + 16
QUARTER = 768
SHARES = (1024, 768)


HELD_LIMIT = 14
UNROLL = 4
WINDOW = 4
FLOPS = 10**9
BACK_COST = (14, 1, 14, 14)


def limit(mebibytes):
    return pltpu.CompilerParams(vmem_limit_bytes=mebibytes * 1024 * 1024)

EMISSION, RECEPTANCE = 3, 4
BLOCKS = (5, 4, 4)
WEIGHTS = tuple(((n, WIDTH, WIDTH), BF16) for n in BLOCKS)
CONSTS = (
    ((9, 1, WIDTH), F32),
    ((1, WIDTH), F32),
    ((1, WIDTH), F32),
    ((SEQS, WIDTH), F32),
    ((SEQS, WIDTH), F32),
    ((SEQS, WIDTH), F32),
    ((2, SEQS, WIDTH), BF16),
)
SAVED = (
    ((ROWS, WIDTH), BF16),
    ((ROWS, WIDTH), BF16),
    ((ROWS, INNER), BF16),
    ((5, ROWS, WIDTH), F32),
    ((8, ROWS * GROUPS, 128), F32),
)
EDGES = (
    ((EDGE, 2 * WIDTH), BF16),
    ((EDGE, 2 * WIDTH), BF16),
)
GRADS = (
    ((ROWS, WIDTH), BF16),
    ((4, ROWS, QUARTER), BF16),
    ((4, ROWS, QUARTER), BF16),
    ((4, ROWS, QUARTER), BF16),
    ((4, ROWS, QUARTER), BF16),
    ((3, SEQS, WIDTH), F32),
    ((2, SEQS, WIDTH), F32),
)
N_CONSTS, N_WEIGHTS, N_SAVED, N_EDGES, N_GRADS = 7, 3, 5, 2, 7
N_BASE = N_CONSTS + N_WEIGHTS + N_SAVED


def dot(left, right):
    return jnp.dot(left, right, preferred_element_type=F32)


def against(grad, weight):
    return lax.dot_general(
        grad, weight, (((1,), (1,)), ((), ())), preferred_element_type=F32
    )


def across(left, right):
    return lax.dot_general(
        left, right, (((0,), (0,)), ((), ())), preferred_element_type=F32
    )


def columns_loop(total, size):
    def run(function):
        if total // size <= UNROLL:
            for j in range(total // size):
                function(pl.ds(j * size, size))
            return

        @pl.loop(0, total // size)
        def _(j):
            function(pl.ds(pl.multiple_of(j * size, size), size))

    return run


def coordinates(section, dp):
    dp = dp[0]
    return section[0], dp >> 3, (dp >> 1) & 3, dp & 1


def row_index():
    return lax.broadcasted_iota(jnp.int32, (ROWS, WIDTH), 0)


def normed_rows(rows):
    center = jnp.mean(rows, axis=-1, keepdims=True)
    centered = rows - center
    variance = jnp.mean(centered * centered, axis=-1, keepdims=True)
    scale = lax.rsqrt(variance + EPS)
    return centered * scale, scale


def moved_down(normed, first):
    index = row_index()
    return jnp.where(
        index == 0,
        first[0],
        jnp.where(index == LENGTH, first[1], pltpu.roll(normed, 1, 0)),
    )


def moved_up(rows):
    index = row_index()
    return jnp.where(
        (index == LENGTH - 1) | (index == ROWS - 1),
        0.0,
        pltpu.roll(rows, ROWS - 1, 0),
    )


def first_rows(prior_ref, mix, marks):
    return [prior_ref[mix, s : s + 1, :].astype(F32) * marks[s] for s in range(SEQS)]


def edge_rows(first):
    index = lax.broadcasted_iota(jnp.int32, (EDGE - ROWS, WIDTH), 0)
    return jnp.where(index == 0, first[0], jnp.where(index == 1, first[1], 0.0)).astype(BF16)


def store_sets(core, keep_ref, send_ref, pieces):
    for this in range(2):

        @pl.when(core == this)
        def _(this=this):
            for which, at, value in pieces:
                (keep_ref if which == this else send_ref)[at] = value()


def to_tokens(ref, block, value):
    ref[pl.ds(block, ROWS, stride=GROUPS), :] = value


def from_tokens(ref, block):
    return ref[pl.ds(block, ROWS, stride=GROUPS), :]


def tile_of(ref, row, small):
    for g in range(GROUPS):
        small[g : g + 1, :] = ref[row : row + 1, g * 128 : (g + 1) * 128]
    return small[...]


def forward_body(
    core, marks, x_ref, consts, weights, ready, out_ref, saved, edges, scratch, square_done=None
):
    streamed = x_ref is None
    vec_ref, fade_ref, boost_ref, num_ref, den_ref, lev_ref, prior_ref = consts
    square, keys, payload = weights
    ent_ref, lay_ref, act_ref, wide_ref, scan_ref = saved
    own_ref, other_ref = edges
    sk, sv, sy, small, mix_ref, hid_ref = scratch
    low, high = slice(0, WIDTH), slice(WIDTH, 2 * WIDTH)
    top, bottom = slice(0, ROWS), slice(ROWS, EDGE)
    if x_ref is not None:
        ent_ref[...] = x_ref[...]
    rows = ent_ref[...].astype(F32)
    unit, _ = normed_rows(rows)
    normed = unit * vec_ref[0] + vec_ref[1]
    first = first_rows(prior_ref, 0, marks)
    below = moved_down(normed, first)
    for j in range(3):
        v = vec_ref[2 + j]
        mix_ref[j] = (normed * v + below * (1.0 - v)).astype(BF16)
    mix_ref[3] = normed.astype(BF16)
    first_one = first
    for target, j in ((sk, 0), (sv, 1)):
        ready(j)

        @columns_loop(WIDTH, 512)
        def _(at, j=j):
            wide_ref[3, :, at] = dot(mix_ref[j], square[j, :, at])

        for g in range(GROUPS):
            to_tokens(target, g, wide_ref[3, :, g * 128 : (g + 1) * 128])
    ready(2)

    @columns_loop(WIDTH, 512)
    def _(at):
        wide_ref[0, :, at] = jax.nn.sigmoid(dot(mix_ref[2], square[2, :, at]))

    rate = jnp.exp(tile_of(fade_ref, 0, small))
    boost = tile_of(boost_ref, 0, small)
    start = []
    for s in range(SEQS):
        level = tile_of(lev_ref, s, small)
        start.append(jnp.where(marks[s] > 0.0, level, FRESH))
        start.append(tile_of(num_ref, s, small) * marks[s])
        start.append(tile_of(den_ref, s, small) * marks[s])

    def token(t, carry):
        carry_next = []
        for s in range(SEQS):
            level, num, den = carry[3 * s : 3 * s + 3]
            at = pl.ds(pl.multiple_of((t + LENGTH * s) * GROUPS, GROUPS), GROUPS)
            key, value = sk[at, :], sv[at, :]
            boosted = boost + key
            decayed = jnp.exp(-jnp.abs(level - boosted))
            state_on_top = level > boosted
            old = jnp.where(state_on_top, 1.0, decayed)
            fresh = jnp.where(state_on_top, decayed, 1.0)
            inverse = 1.0 / (old * den + fresh)
            old = old * inverse
            fresh = fresh * inverse
            result = old * num + fresh * value
            faded = level - rate
            level = jnp.maximum(faded, key)
            decayed = jnp.exp(-jnp.abs(faded - key))
            state_on_top = faded > key
            keep = jnp.where(state_on_top, 1.0, decayed)
            new = jnp.where(state_on_top, decayed, 1.0)
            sy[at, :] = result
            scan_ref[0, at, :] = old
            scan_ref[1, at, :] = fresh
            scan_ref[2, at, :] = value - result
            scan_ref[3, at, :] = keep
            scan_ref[4, at, :] = new
            scan_ref[5, at, :] = num
            scan_ref[6, at, :] = den
            scan_ref[7, at, :] = value
            carry_next += [level, keep * num + new * value, keep * den + new]
        return tuple(carry_next)

    def tokens(block, carry):
        for j in range(8):
            carry = token(block * 8 + j, carry)
        return carry

    lax.fori_loop(0, LENGTH // 8, tokens, tuple(start))
    for g in range(GROUPS):
        at = slice(g * 128, (g + 1) * 128)
        gate = wide_ref[0, :, at]
        mixed = gate * from_tokens(sy, g)
        mix_ref[0, :, at] = mixed.astype(BF16)
        wide_ref[1, :, at] = mixed * (1.0 - gate)
    store_sets(
        core, own_ref, other_ref,
        (
            (0, (top, high), lambda: mix_ref[3]),
            (0, (bottom, high), lambda: edge_rows(first_one)),
            (1, (top, high), lambda: mix_ref[0]),
        ),
    )
    ready(3)

    @columns_loop(WIDTH, 512)
    def _(at):
        wide_ref[2, :, at] = ent_ref[:, at].astype(F32) + dot(mix_ref[0], square[EMISSION, :, at])

    unit, _ = normed_rows(wide_ref[2])
    normed = unit * vec_ref[5] + vec_ref[6]
    first = first_rows(prior_ref, 1, marks)
    below = moved_down(normed, first)
    for j in range(2):
        v = vec_ref[7 + j]
        mix_ref[1 + j] = (normed * v + below * (1.0 - v)).astype(BF16)
    for ref in edges:
        ref[top, low] = normed.astype(BF16)
        ref[bottom, low] = edge_rows(first)
    ready(4)

    @columns_loop(WIDTH, 512)
    def _(at):
        wide_ref[4, :, at] = jax.nn.sigmoid(dot(mix_ref[2], square[RECEPTANCE, :, at]))

    if square_done is not None:
        square_done()

    def hidden(j):
        at = pl.ds(pl.multiple_of(j * 512, 512), 512)
        within = pl.ds(pl.multiple_of((j & 1) * 512, 512), 512)
        active = jnp.maximum(dot(mix_ref[1], keys[j >> 1, :, within]), 0.0)
        act_ref[:, at] = active.astype(BF16)
        hid_ref[:, at] = (active * active).astype(BF16)

    def leave(at, channel):
        wide_ref[3, :, at] = channel
        lay_ref[:, at] = (wide_ref[2, :, at] + wide_ref[4, :, at] * channel).astype(BF16)

    def part(b, at):
        return dot(hid_ref[:, b * WIDTH : (b + 1) * WIDTH], payload[b, :, at])

    if not streamed:
        pl.loop(0, INNER // 512)(hidden)

        @columns_loop(WIDTH, 256)
        def _(at):
            leave(at, part(0, at) + part(1, at) + part(2, at) + part(3, at))

    else:
        for b in range(4):
            ready(5 + b)
            pl.loop(2 * b, 2 * b + 2)(hidden)
        for b in range(4):
            ready(9 + b)

            @columns_loop(WIDTH, 512)
            def _(at, b=b):
                channel = part(b, at)
                if b > 0:
                    channel = channel + wide_ref[3, :, at]
                if b < 3:
                    wide_ref[3, :, at] = channel
                else:
                    leave(at, channel)

    out_ref[...] = lay_ref[...]


def groups(refs, *sizes):
    cut, at = [], 0
    for size in sizes:
        cut.append(refs[at : at + size])
        at += size
    return cut + [refs[at:]]


def weight_pieces(maps, emission, key, payload, receptance):
    pieces = [maps.at[j] for j in range(3)] + [emission, receptance]
    for b in range(4):
        pieces.append(key.at[:, pl.ds(b * WIDTH, WIDTH)])
    for b in range(4):
        pieces.append(payload.at[pl.ds(b * WIDTH, WIDTH), :])
    return pieces


def forward_first_kernel(section, dp, begins, x_ref, *refs):
    small_in, hbm, (out_ref,), consts, kept, saved, edges, rest = groups(
        refs, N_CONSTS, 5, 1, N_CONSTS, N_WEIGHTS, N_SAVED, N_EDGES
    )
    section, _, _, core = coordinates(section, dp)
    sem, small_sem = rest[-2:]
    copies = [
        pltpu.make_async_copy(source, target, sem.at[i])
        for i, (source, target) in enumerate(
            zip(
                weight_pieces(*hbm),
                [ref.at[i] for ref, n in zip(kept, BLOCKS) for i in range(n)],
            )
        )
    ]
    arriving = [pltpu.make_async_copy(x_ref, saved[0], small_sem.at[N_CONSTS])]
    for i in range(N_CONSTS):
        arriving.append(pltpu.make_async_copy(small_in[i], consts[i], small_sem.at[i]))
    for c in arriving + copies[:WINDOW]:
        c.start()
    for c in arriving:
        c.wait()

    def ready(i):
        copies[i].wait()
        if i + WINDOW < len(copies):
            copies[i + WINDOW].start()

    @pl.when(section == 0)
    def _():
        marks = [begins[s].astype(F32) for s in range(SEQS)]
        forward_body(
            core, marks, None, consts, kept, ready, out_ref, saved, edges, rest[:-2]
        )

    @pl.when(section != 0)
    def _():
        for c in copies[WINDOW:]:
            c.start()
        for c in copies:
            c.wait()


def flip(ref):
    side = 256
    for i in range(WIDTH // side):
        for j in range(i + 1):
            one = (slice(i * side, (i + 1) * side), slice(j * side, (j + 1) * side))
            two = (one[1], one[0])
            first = ref[one].T
            if i != j:
                ref[one] = ref[two].T
            ref[two] = first


def flip_slowly(ref):
    side = 256

    @pl.loop(0, 10)
    def _(pair):
        i = jnp.int32(pair >= 1) + jnp.int32(pair >= 3) + jnp.int32(pair >= 6)
        j = pair - ((i * (i + 1)) >> 1)
        row, column = (pl.ds(pl.multiple_of(t * side, side), side) for t in (i, j))
        first, second = ref[row, column].T, ref[column, row].T
        ref[row, column] = second
        ref[column, row] = first


def forward_kernel(layer, last, section, dp, begins, x_ref, *refs):
    early, own = layer == 1, layer == last
    _, given, (out_ref,), consts, kept, saved, edges, kept_away, rest = groups(
        refs,
        N_BASE + N_EDGES,
        5 if early else 1 if own else 0,
        1, N_CONSTS, N_WEIGHTS, N_SAVED, N_EDGES,
        2 if early else 0,
    )
    scratch, sem = (rest[:-1], rest[-1]) if early or own else (rest, None)
    section, _, _, core = coordinates(section, dp)

    @pl.when(section == layer)
    def _():
        marks = [begins[s].astype(F32) for s in range(SEQS)]
        square = pltpu.make_async_copy(given[0], kept[0], sem.at[0]) if own else None
        forward_body(
            core, marks, x_ref, consts, kept, lambda i: None, out_ref, saved, edges, scratch,
            square.start if own else None,
        )
        if own:
            square.wait()

    if early:

        @pl.when(section == last)
        def _():
            for ref, n in zip(kept[:2], BLOCKS):

                @pl.loop(0, n)
                def _(i, ref=ref):
                    flip_slowly(ref.at[i])

            away = [
                pltpu.make_async_copy(kept[i], kept_away[i], sem.at[i]) for i in range(2)
            ]
            for c in away:
                c.start()
            for c in away:
                c.wait()
            targets = [ref.at[i] for ref, n in zip(kept[:2], BLOCKS) for i in range(n)]
            back = [
                pltpu.make_async_copy(source, target, sem.at[i])
                for i, (source, target) in enumerate(zip(weight_pieces(*given), targets))
            ]
            for c in back:
                c.start()
            for c in back:
                c.wait()


def norm_back(rows, gain, offset, first, parts, vec_out, prior_out, marks):
    unit, scale = normed_rows(rows)
    normed = unit * gain + offset
    change = normed - moved_down(normed, first)
    up, stay = None, None
    for grad, weight, row in parts:
        vec_out(row, jnp.sum(grad * change, axis=0, keepdims=True))
        kept = grad * weight
        passed = grad - kept
        stay = kept if stay is None else stay + kept
        up = passed if up is None else up + passed
    for s in range(SEQS):
        prior_out(s, up[s * LENGTH : s * LENGTH + 1, :] * marks[s])
    grad = stay + moved_up(up)
    return unit, scale, grad


def backward_kernel(first, layer, section, dp, begins, dy_ref, *refs):
    _, given, (out_ref,), consts, kept, saved, grads, scratch = groups(
        refs,
        N_BASE + (0 if first else N_GRADS),
        1 if first else 0,
        1, N_CONSTS, N_WEIGHTS, N_SAVED, N_GRADS,
    )
    vec_ref, fade_ref, prior_ref = consts[0], consts[1], consts[6]
    square, keys, payload = kept
    ent_ref, lay_ref, act_ref, wide_ref, scan_ref = saved
    ing_ref, keep_one, send_one, keep_two, send_two, stg_ref, rowg_ref = grads
    sg, sdk, sdv, small, wide, wide_two, wide_three, wide_four, dys_ref, dhp_ref, vecg_ref = scratch[:11]
    section, y, z, core = coordinates(section, dp)
    def vec_out(row, value):
        vecg_ref[row : row + 1, :] = value

    def store(keep_ref, send_ref, items, shared=None):
        for this in range(2):

            @pl.when(core == this)
            def _(this=this):
                @pl.loop(0, 4)
                def _(q):
                    for which, column, size, value in items:
                        ref = keep_ref if which == this else send_ref
                        distance = (q - (y if which else z)) & 3
                        ref[distance, :, column : column + size] = value(q)
                    if shared is not None:
                        ref = keep_ref if this == 1 else send_ref
                        ref[q, 0:64, 512:768] = shared

    def quarter(row):
        return lambda q: dys_ref[row, :, pl.ds(pl.multiple_of(q * 256, 256), 256)]

    def pull(grad, blocks, i, at):
        if first and blocks is payload:
            return against(grad, blocks[i, at, :])
        return dot(grad, blocks[i, :, at])

    def through_payload(grad, j):
        return pull(grad, payload, j >> 1, pl.ds(pl.multiple_of((j & 1) * 512, 512), 512))

    def through_key(grad_ref, j):
        at = pl.ds(pl.multiple_of(j * 256, 256), 256)
        total = None
        for b in range(4):
            part = pull(grad_ref[:, b * WIDTH : (b + 1) * WIDTH], keys, b, at)
            total = part if total is None else total + part
        return total

    @pl.when(section == layer)
    def _():
        marks = [begins[s].astype(F32) for s in range(SEQS)]
        if first:
            key_copy = pltpu.make_async_copy(given[0], keys, scratch[11].at[0])
            key_copy.start()
        dy = dy_ref[...].astype(F32)
        gate = wide_ref[4]
        through = dy * gate
        dys_ref[4] = through.astype(BF16)
        dys_ref[5] = (through * wide_ref[3] * (1.0 - gate)).astype(BF16)

        @pl.loop(0, INNER // 512, unroll=2)
        def _(j):
            at = pl.ds(pl.multiple_of(j * 512, 512), 512)
            part = through_payload(dys_ref[4], j)
            dhp_ref[:, at] = (2.0 * act_ref[:, at].astype(F32) * part).astype(BF16)

        def hidden(start):
            return lambda q: dhp_ref[:, pl.ds(pl.multiple_of(start + q * 512, 512), 512)]

        store(
            keep_one, send_one,
            ((0, 0, 512, hidden(0)), (1, 0, 512, hidden(2048)),
             (0, 512, 256, quarter(4)), (1, 512, 256, quarter(4))),
        )

        if first:
            key_copy.wait()

        @pl.loop(0, WIDTH // 256)
        def _(j):
            at = pl.ds(pl.multiple_of(j * 256, 256), 256)
            wide[:, at] = through_key(dhp_ref, j)
            wide_two[:, at] = pull(dys_ref[5], square, RECEPTANCE, at)

        def prior_two(s, value):
            rowg_ref[1, s : s + 1, :] = value

        gain = vec_ref[5]
        unit, scale, grad = norm_back(
            wide_ref[2], gain, vec_ref[6], first_rows(prior_ref, 1, marks),
            ((wide[...], vec_ref[7], 7), (wide_two[...], vec_ref[8], 8)),
            vec_out, prior_two, marks,
        )
        vec_out(5, jnp.sum(grad * unit, axis=0, keepdims=True))
        vec_out(6, jnp.sum(grad, axis=0, keepdims=True))
        grad = grad * gain
        mean = jnp.mean(grad, axis=-1, keepdims=True)
        along = jnp.mean(grad * unit, axis=-1, keepdims=True)
        middle = dy_ref[...].astype(F32) + scale * (grad - mean - unit * along)
        wide_three[...] = middle
        dys_ref[3] = middle.astype(BF16)

        for q in range(4):
            at = pl.ds(q * 256, 256)
            part = pull(dys_ref[3], square, EMISSION, at)
            dys_ref[2, :, at] = (part * wide_ref[1, :, at]).astype(BF16)
            wide[:, at] = part * wide_ref[0, :, at]

        for g in range(GROUPS):
            to_tokens(sg, g, wide[:, g * 128 : (g + 1) * 128])

        zero = jnp.zeros((GROUPS, 128), F32)

        def token(t, carry):
            carry_next = []
            boosted, faded = carry[4], carry[5]
            for s in range(SEQS):
                dnum, dden = carry[2 * s : 2 * s + 2]
                at = pl.ds(pl.multiple_of((t + LENGTH * s) * GROUPS, GROUPS), GROUPS)
                g = sg[at, :]
                value = scan_ref[7, at, :]
                beyond = scan_ref[2, at, :]
                keep = scan_ref[3, at, :]
                new = scan_ref[4, at, :]
                from_old = scan_ref[0, at, :] * g
                from_new = scan_ref[1, at, :] * g
                direct = from_new * beyond
                boosted = boosted + direct
                sdv[at, :] = from_new + new * dnum
                sdk[at, :] = direct + new * (dnum * value + dden)
                faded = faded - keep * (dnum * scan_ref[5, at, :] + dden * scan_ref[6, at, :])
                carry_next += [
                    from_old + keep * dnum,
                    keep * dden - from_old * (value - beyond),
                ]
            return tuple(carry_next) + (boosted, faded)

        def tokens(block, carry):
            for j in range(8):
                carry = token(LENGTH - 1 - block * 8 - j, carry)
            return carry

        ends = lax.fori_loop(0, LENGTH // 8, tokens, (zero,) * 6)

        def spread(put_piece, value):
            small[...] = value
            for g in range(GROUPS):
                put_piece(slice(g * 128, (g + 1) * 128), small[g : g + 1, :])

        for s in range(SEQS):
            dnum, dden = ends[2 * s : 2 * s + 2]
            at = pl.ds(LENGTH * s * GROUPS, GROUPS)
            moved = dnum * scan_ref[5, at, :] + dden * scan_ref[6, at, :]
            for k, value in enumerate((dnum, dden, moved)):

                def put_state(cols, piece, k=k, s=s):
                    stg_ref[k, s : s + 1, cols] = piece

                spread(put_state, value * marks[s])

        def put_decay(cols, piece):
            vecg_ref[9:10, cols] = piece

        def put_boost(cols, piece):
            vecg_ref[10:11, cols] = piece

        spread(put_decay, ends[5])
        vecg_ref[9:10, :] = vecg_ref[9:10, :] * jnp.exp(fade_ref[0:1, :])
        spread(put_boost, ends[4])

        for g in range(GROUPS):
            at = slice(g * 128, (g + 1) * 128)
            dys_ref[0, :, at] = from_tokens(sdk, g).astype(BF16)
            dys_ref[1, :, at] = from_tokens(sdv, g).astype(BF16)
        rows = ent_ref[...].astype(F32)
        pulled = (wide, wide_two, wide_four)
        for j in range(3):

            @columns_loop(WIDTH, 512)
            def _(at, j=j):
                pulled[j][:, at] = pull(dys_ref[j], square, j, at)


        def prior_one(s, value):
            rowg_ref[0, s : s + 1, :] = value

        gain = vec_ref[0]
        unit, scale, grad = norm_back(
            rows, gain, vec_ref[1], first_rows(prior_ref, 0, marks),
            [(pulled[j][...], vec_ref[2 + j], 2 + j) for j in range(3)],
            vec_out, prior_one, marks,
        )
        vec_out(0, jnp.sum(grad * unit, axis=0, keepdims=True))
        vec_out(1, jnp.sum(grad, axis=0, keepdims=True))
        packed = jnp.concatenate(
            [vecg_ref[:, b * 256 : (b + 1) * 256] for b in range(4)], axis=0
        ).astype(BF16)
        store(
            keep_two, send_two,
            ((0, 0, 256, quarter(0)), (0, 256, 256, quarter(1)), (0, 512, 256, quarter(2)),
             (1, 0, 256, quarter(5)), (1, 256, 256, quarter(3))),
            packed,
        )
        grad = grad * gain
        mean = jnp.mean(grad, axis=-1, keepdims=True)
        along = jnp.mean(grad * unit, axis=-1, keepdims=True)
        entry = (wide_three[...] + scale * (grad - mean - unit * along)).astype(BF16)
        ing_ref[...] = entry
        out_ref[...] = entry


def transpose_kernel(last, section, dp, *refs):
    @pl.when(section[0] != last)
    def _():
        for ref, n in zip(refs[N_WEIGHTS:], BLOCKS):

            @pl.loop(0, n, unroll=4 if n == 4 else 1)
            def _(i, ref=ref):
                flip(ref.at[i])


def join_edges_kernel(first, second, out, sem):
    copies = [
        pltpu.make_async_copy(ref, out.at[pl.ds(h * EDGE, EDGE), :], sem.at[h])
        for h, ref in enumerate((first, second))
    ]
    for c in copies:
        c.start()
    for c in copies:
        c.wait()


def join_kernel(first, second, *outs):
    for k in range(4):
        outs[k][:ROWS, :] = first[k]
        outs[k][ROWS:, :] = second[k]


def mixes_kernel(section, dp, own, one, two, three, vec_ref, wa, *refs):
    x_one, x_two, edge, wide, stage, hidden, first_mix, edge_sem, wide_sem, out_sem = refs
    core = coordinates(section, dp)[3]
    blocks = (own, one, two, three)
    pair = 2 * ROWS

    def load(k):
        for i, block in enumerate(blocks):

            @pl.when(k == i)
            def _(block=block):
                pltpu.make_async_copy(block, edge.at[k & 1], edge_sem.at[k & 1]).start()

    columns = [
        pltpu.make_async_copy(
            wa.at[:, pl.ds(pl.multiple_of((2 * j + core) * 128, 128), 128)],
            wide.at[:, pl.ds(j * 128, 128)],
            wide_sem.at[j],
        )
        for j in range(16)
    ]

    def outs(k):
        rows = pl.ds(pl.multiple_of(k * pair, pair), pair)
        slot = k & 1
        return (
            pltpu.make_async_copy(first_mix.at[slot], x_one.at[2, rows, :], out_sem.at[slot, 0]),
            pltpu.make_async_copy(stage.at[slot], x_two.at[:, rows, :], out_sem.at[slot, 1]),
        )

    def out_hidden(k, u):
        rows = pl.ds(pl.multiple_of(k * pair, pair), pair)
        return pltpu.make_async_copy(hidden.at[u], x_one.at[u, rows, :], out_sem.at[u, 2])

    def mix(normed, below, j):
        v = vec_ref[j]
        return (normed * v + below * (1.0 - v)).astype(BF16)

    load(jnp.int32(0))
    for c in columns:
        c.start()

    @pl.loop(0, 4)
    def _(k):
        slot = k & 1

        @pl.when(k < 3)
        def _():
            load(k + 1)

        pltpu.make_async_copy(own, edge.at[slot], edge_sem.at[slot]).wait()

        @pl.when(k >= 2)
        def _():
            for c in outs(k - 2):
                c.wait()

        @pl.loop(0, 2)
        def _(h):
            start = pl.multiple_of(h * EDGE, 16)
            at = pl.ds(pl.multiple_of(h * ROWS, ROWS), ROWS)

            def parts(c):
                cols = slice(c * WIDTH, (c + 1) * WIDTH)
                normed = edge[slot, pl.ds(start, ROWS), cols].astype(F32)
                first = edge[slot, pl.ds(pl.multiple_of(start + ROWS, 16), 16), cols].astype(F32)
                return normed, moved_down(normed, (first[0:1, :], first[1:2, :]))

            normed, below = parts(0)
            first_mix[slot, at, :] = mix(normed, below, 7)

            @pl.when(core == 0)
            def _():
                normed, below = parts(1)
                for j in range(3):
                    stage[slot, j, at, :] = mix(normed, below, 2 + j)

            @pl.when(core == 1)
            def _():
                stage[slot, 0, at, :] = mix(normed, below, 8)
                stage[slot, 1, at, :] = edge[slot, pl.ds(start, ROWS), WIDTH:]

        for c in outs(k):
            c.start()

        @pl.when(k == 0)
        def _():
            for c in columns:
                c.wait()

        for u in range(2):

            @pl.when(k >= 1)
            def _(u=u):
                out_hidden(k - 1, u).wait()

            @pl.loop(0, 2)
            def _(j, u=u):
                for half in range(2):
                    at = pl.ds(pl.multiple_of(j * 512 + half * 256, 256), 256)
                    wide_at = pl.ds(pl.multiple_of(u * WIDTH + j * 512 + half * 256, 256), 256)
                    active = jnp.maximum(dot(first_mix[slot], wide[:, wide_at]), 0.0)
                    hidden[u, :, at] = (active * active).astype(BF16)

            out_hidden(k, u).start()

    for k in (2, 3):
        for c in outs(k):
            c.wait()
    for u in range(2):
        out_hidden(3, u).wait()


def drain_kernel(layer, entry, states, firsts, *refs):
    results, sem = refs[:-1], refs[-1]
    sources = (layer, entry) + tuple(states.at[k] for k in range(3)) + (firsts,)
    copies = [
        pltpu.make_async_copy(source, target, sem.at[i])
        for i, (source, target) in enumerate(zip(sources, results))
    ]
    for c in copies:
        c.start()
    for c in copies:
        c.wait()


def row_starts(y, z, core):
    starts = []
    for there in range(16):
        along_y, along_z = (there // 4 - y) & 3, (there % 4 - z) & 3
        summed = jnp.where(core == 0, along_y, along_z)
        joined = jnp.where(core == 0, along_z, along_y)
        starts.append(pl.multiple_of(summed * 256 + joined * 64, 64))
    return starts


def weight_kernel(second, section, dp, x_ref, *refs):
    blocks, outs = refs[:4], refs[4:8]
    dy, share = refs[8:]
    _, y, z, core = coordinates(section, dp)
    for k in range(4):
        dy[k * 2 * ROWS : (k + 1) * 2 * ROWS, :] = blocks[k][...]
    starts = row_starts(y, z, core)

    def unit(u, size, source, target):
        for c in range(0, WIDTH, 256):
            part = across(x_ref[u, :, c : c + 256], dy[:, source : source + size]).astype(BF16)
            for b in range(4):
                share[pl.ds(starts[c // 64 + b], 64), target : target + size] = part[
                    b * 64 : (b + 1) * 64, :
                ]

    if not second:
        unit(2, 512, 0, 0)
        for u in range(2):
            for c in range(0, WIDTH, 256):
                part = across(x_ref[u, :, c : c + 256], dy[:, 512:768]).astype(BF16)
                for b in range(2):
                    start = starts[(u * WIDTH + c) // 128 + b]
                    for half in range(2):
                        share[pl.ds(start, 64), 512 + half * 256 : 768 + half * 256] = part[
                            b * 128 + half * 64 : b * 128 + (half + 1) * 64, :
                        ]
    else:
        unit(0, 256, 0, 0)
        unit(1, 256, 256, 256)

        @pl.when(core == 0)
        def _():
            unit(2, 256, 512, 512)

        @pl.when(core == 1)
        def _():
            total = jnp.zeros((64, 256), F32)
            for d in range(8):
                total = total + dy[d * ROWS : d * ROWS + 64, 512:768].astype(F32)
            for b in range(4):
                piece = jnp.concatenate(
                    [total[b * 16 : (b + 1) * 16, :], jnp.zeros((112, 256), F32)], axis=0
                ).T.astype(BF16)
                for e in range(4):
                    at = pl.ds(starts[b * 4 + e], 64)
                    share[at, 512:640] = piece[e * 64 : (e + 1) * 64, :]
                    share[at, 640:768] = jnp.zeros((64, 128), BF16)

    for k in range(4):
        outs[k][...] = share[k * 256 : (k + 1) * 256, :]


def sum_kernel(own, one, two, three, *outs):
    for k in range(4):

        @pl.loop(0, 4)
        def _(i, k=k):
            at = pl.ds(pl.multiple_of(k * 64 + i * 16, 16), 16)
            total = own[at, :].astype(F32) + one[at, :].astype(F32) + two[at, :].astype(F32)
            total = total + three[at, :].astype(F32)
            outs[k][pl.ds(pl.multiple_of(i * 16, 16), 16), :] = total.astype(BF16)


def gather_kernel(second, section, dp, own, one, two, three, keep_ref, send_ref, *payload):
    _, y, z, core = coordinates(section, dp)
    here = jnp.where(core == 0, z, y)
    mine = pl.multiple_of(core * 32, 32)
    theirs = pl.multiple_of(32 - core * 32, 32)
    for k, ref in enumerate((own, one, two, three)):
        quarter = (here - k) & 3
        for rows, target in ((mine, keep_ref), (theirs, send_ref)):
            if not second:
                at = pl.ds(pl.multiple_of(quarter * 512, 512), 512)
                target[:, at] = ref[pl.ds(rows, 32), 0:512]
            else:
                for u in range(3):
                    at = pl.ds(pl.multiple_of(u * WIDTH + quarter * 256, 256), 256)
                    target[:, at] = ref[pl.ds(rows, 32), u * 256 : (u + 1) * 256]
        if not second:
            at = pl.ds(pl.multiple_of(quarter * 256, 256), 256)
            for half in range(2):
                payload[0][half * 64 : (half + 1) * 64, at] = ref[
                    :, 512 + half * 256 : 768 + half * 256
                ].astype(F32)


def final_kernel(second, section, dp, kept, come, *outs):
    core = coordinates(section, dp)[3]

    def write(set_zero, set_one):
        if not second:
            outs[0][:, 0:2048] = set_zero[...].astype(F32)
            outs[0][:, 2048:4096] = set_one[...].astype(F32)
            return
        proj_ref, out_ref, gate_ref, vec_ref, dec_ref, boo_ref = outs
        for u in range(3):
            proj_ref[u] = set_zero[:, u * WIDTH : (u + 1) * WIDTH].astype(F32)
        gate_ref[...] = set_one[:, 0:1024].astype(F32)
        out_ref[...] = set_one[:, 1024:2048].astype(F32)
        vectors = set_one[:, 2048:2176].astype(F32).T
        for j in range(9):
            vec_ref[j] = vectors[j : j + 1, :]
        dec_ref[...] = vectors[9:10, :]
        boo_ref[...] = vectors[10:11, :]

    @pl.when(core == 0)
    def _():
        write(kept, come)

    @pl.when(core == 1)
    def _():
        write(come, kept)


def plain(shapes):
    return tuple(jax.ShapeDtypeStruct(s, d) for s, d in shapes)


def in_vmem(shapes):
    return tuple(pltpu.VMEM(s, d) for s, d in shapes)


def hold(arrays):
    return tuple(pltpu.with_memory_space_constraint(a, pltpu.VMEM) for a in arrays)


def in_hbm(*arrays):
    return tuple(pltpu.with_memory_space_constraint(a, pltpu.HBM) for a in arrays)


def array(*shape, kind=BF16):
    return jax.ShapeDtypeStruct(shape, kind)


ROWS_OUT = array(ROWS, WIDTH)
TOKENS = pltpu.VMEM((ROWS * GROUPS, 128), F32)
SMALL = pltpu.VMEM((GROUPS, 128), F32)
WIDE = pltpu.VMEM((ROWS, WIDTH), F32)
FORWARD_SCRATCH = [
    TOKENS, TOKENS, TOKENS, SMALL,
    pltpu.VMEM((4, ROWS, WIDTH), BF16),
    pltpu.VMEM((ROWS, INNER), BF16),
]
DMA = pltpu.SemaphoreType.DMA


def forward_first(place, begins, rows, small, weights):
    shapes = CONSTS + WEIGHTS + SAVED + EDGES
    results = pl.pallas_call(
        forward_first_kernel,
        cost_estimate=cost(12),
        out_shape=(ROWS_OUT,) + in_vmem(shapes),
        in_specs=[SM] * 3 + [HB] * (1 + N_CONSTS + 5),
        out_specs=(VM,) * (1 + len(shapes)),
        scratch_shapes=FORWARD_SCRATCH + [DMA((13,)), DMA((N_CONSTS + 1,))],
        compiler_params=limit(HELD_LIMIT),
    )(*place, *in_hbm(begins, rows, *small, *weights))
    return results[0], results[1:]


def forward_next(layer, last, place, begins, rows, held, given=()):
    shapes = CONSTS + WEIGHTS + SAVED + EDGES
    away = tuple(pltpu.HBM(s, d) for s, d in WEIGHTS[:2]) if layer == 1 else ()
    results = pl.pallas_call(
        functools.partial(forward_kernel, layer, last),
        cost_estimate=cost(10),
        out_shape=(ROWS_OUT,) + plain(shapes) + away,
        in_specs=[SM] * 3 + [VM] * (1 + len(shapes)) + [HB] * len(given),
        out_specs=(VM,) * (1 + len(shapes)) + (HB,) * len(away),
        input_output_aliases={4 + i: 1 + i for i in range(len(shapes))},
        scratch_shapes=FORWARD_SCRATCH + ([DMA((9,))] if given else []),
        compiler_params=limit(HELD_LIMIT),
    )(*place, begins, *hold((rows,)), *hold(held), *in_hbm(*given))
    return results[0], results[1 : 1 + len(shapes)], results[1 + len(shapes) :]


def backward_call(layer, place, begins, grad, held, given=()):
    first = len(held) == N_BASE
    base = CONSTS + WEIGHTS + SAVED
    results = pl.pallas_call(
        functools.partial(backward_kernel, first, layer),
        cost_estimate=cost(BACK_COST[layer]),
        out_shape=(ROWS_OUT,) + plain(base) + (in_vmem(GRADS) if first else plain(GRADS)),
        in_specs=[SM] * 3 + [VM] * (1 + len(held)) + [HB] * len(given),
        out_specs=(VM,) * (1 + N_BASE + N_GRADS),
        input_output_aliases={4 + i: 1 + i for i in range(len(held))},
        scratch_shapes=[
            TOKENS, TOKENS, TOKENS, SMALL, WIDE, WIDE, WIDE, WIDE,
            pltpu.VMEM((6, ROWS, WIDTH), BF16),
            pltpu.VMEM((ROWS, INNER), BF16),
            pltpu.VMEM((16, WIDTH), F32),
        ]
        + ([DMA((1,))] if given else []),
        compiler_params=limit(HELD_LIMIT),
    )(*place, begins, *hold((grad,)), *hold(held), *in_hbm(*given))
    return results[0], results[1:]


def cost(microseconds):
    return pl.CostEstimate(
        flops=int(microseconds * FLOPS), bytes_accessed=0, transcendentals=0
    )


def transposed(last, place, held):
    first, end = N_CONSTS, N_CONSTS + N_WEIGHTS
    weights = pl.pallas_call(
        functools.partial(transpose_kernel, last),
        cost_estimate=cost(9),
        out_shape=plain(WEIGHTS),
        in_specs=[SM] * 2 + [VM] * N_WEIGHTS,
        out_specs=(VM,) * N_WEIGHTS,
        input_output_aliases={2 + i: i for i in range(N_WEIGHTS)},
        compiler_params=limit(HELD_LIMIT),
    )(*place, *hold(held[first:end]))
    return tuple(held[:first]) + tuple(weights) + tuple(held[end:])


def join_edges(first, second):
    return pl.pallas_call(
        join_edges_kernel,
        cost_estimate=cost(3),
        out_shape=pltpu.HBM((2 * EDGE, 2 * WIDTH), BF16),
        in_specs=[VM, VM],
        out_specs=HB,
        scratch_shapes=[DMA((2,))],
        compiler_params=limit(1),
    )(*hold((first, second)))


def join(first, second):
    return pl.pallas_call(
        join_kernel,
        cost_estimate=cost(1),
        out_shape=in_vmem((((2 * ROWS, QUARTER), BF16),) * 4),
        in_specs=[VM, VM],
        out_specs=(VM,) * 4,
        compiler_params=limit(HELD_LIMIT),
    )(*hold((first, second)))


MIXES_SCRATCH = [
    pltpu.VMEM((2, 2 * EDGE, 2 * WIDTH), BF16),
    pltpu.VMEM((WIDTH, 2 * WIDTH), BF16),
    pltpu.VMEM((2, 3, 2 * ROWS, WIDTH), BF16),
    pltpu.VMEM((2, 2 * ROWS, WIDTH), BF16),
    pltpu.VMEM((2, 2 * ROWS, WIDTH), BF16),
    DMA((2,)),
    DMA((16,)),
    DMA((2, 3)),
]
X_HALF = pltpu.HBM((3, 8 * ROWS, WIDTH), BF16)


def mixes(place, blocks, vec, wa):
    return pl.pallas_call(
        mixes_kernel,
        cost_estimate=cost(15),
        out_shape=(X_HALF, X_HALF),
        in_specs=[SM] * 2 + [HB] * 4 + [VM, HB],
        out_specs=(HB, HB),
        scratch_shapes=MIXES_SCRATCH,
        compiler_params=limit(HELD_LIMIT),
    )(*place, *in_hbm(*blocks), vec, *in_hbm(wa))


def drained(layer, entry, states, firsts):
    rows, state = pltpu.HBM((ROWS, WIDTH), BF16), pltpu.HBM((SEQS, WIDTH), F32)
    return pl.pallas_call(
        drain_kernel,
        cost_estimate=cost(1),
        out_shape=(rows, rows, state, state, state, pltpu.HBM((2, SEQS, WIDTH), F32)),
        in_specs=[HB] * 4,
        out_specs=(HB,) * 6,
        scratch_shapes=[DMA((6,))],
        compiler_params=limit(1),
    )(layer, entry, states, firsts)


def weight_grads(second, place, x, blocks):
    columns = SHARES[second]
    return pl.pallas_call(
        functools.partial(weight_kernel, second),
        cost_estimate=cost(4),
        out_shape=in_vmem((((2 * ROWS, columns), BF16),) * 4),
        in_specs=[SM] * 2 + [VM] * 5,
        out_specs=(VM,) * 4,
        scratch_shapes=[
            pltpu.VMEM((8 * ROWS, QUARTER), BF16),
            pltpu.VMEM((8 * ROWS, columns), BF16),
        ],
        compiler_params=limit(HELD_LIMIT),
    )(*place, *hold((x, *blocks)))


def summed(second, shares):
    return pl.pallas_call(
        sum_kernel,
        cost_estimate=cost(1),
        out_shape=in_vmem((((64, SHARES[second]), BF16),) * 4),
        in_specs=[VM] * 4,
        out_specs=(VM,) * 4,
        compiler_params=limit(HELD_LIMIT),
    )(*hold(shares))


def gathered(second, place, parts):
    outs = in_vmem((((32, 3 * WIDTH), BF16),) * 2)
    if not second:
        outs = in_vmem((((32, 2 * WIDTH), BF16),) * 2) + (pltpu.HBM((ROWS, WIDTH), F32),)
    return pl.pallas_call(
        functools.partial(gather_kernel, second),
        cost_estimate=cost(1),
        out_shape=outs,
        in_specs=[SM] * 2 + [VM] * 4,
        out_specs=(VM,) * len(outs),
        compiler_params=limit(HELD_LIMIT),
    )(*place, *hold(parts))


def final(second, place, kept, come):
    outs = (
        array(3, 32, WIDTH, kind=F32),
        array(32, WIDTH, kind=F32),
        array(32, WIDTH, kind=F32),
        array(9, 1, 32, kind=F32),
        array(1, 32, kind=F32),
        array(1, 32, kind=F32),
    )
    if not second:
        outs = (array(32, INNER, kind=F32),)
    return pl.pallas_call(
        functools.partial(final_kernel, second),
        cost_estimate=cost(1),
        out_shape=outs,
        in_specs=[SM] * 2 + [VM] * 2,
        out_specs=(VM,) * len(outs),
        compiler_params=limit(HELD_LIMIT),
    )(*place, *hold((kept, come)))


def device(y, z, core):
    return (y * 4 + z) * 2 + core


def swapped(block):
    return lax.ppermute(block, "dp", [(d, d ^ 1) for d in range(32)])


def sent(block, distance, first_axis):
    route = []
    for y in range(4):
        for z in range(4):
            for core in range(2):
                if (core == 0) == first_axis:
                    there = device(y, (z + distance) % 4, core)
                else:
                    there = device((y + distance) % 4, z, core)
                route.append((device(y, z, core), there))
    return lax.ppermute(block, "dp", route)


def body(
    bottom_stack_feed,
    loss_sensitivity,
    resumes_segment,
    mixing_coefficients,
    fading_log,
    feature_boost,
    attention_maps,
    emission_coefficients,
    feature_addressing,
    feature_payload,
    feature_receptance,
    dividend_memory,
    divisor_memory,
    memory_power_shift,
    prior_normed_lines,
):
    sections = lax.axis_size("section")
    place = (lax.axis_index("section")[None], lax.axis_index("dp")[None])
    begins = resumes_segment
    vec = jnp.swapaxes(mixing_coefficients, 0, 1)
    small = (
        vec,
        fading_log,
        feature_boost,
        dividend_memory[0],
        divisor_memory[0],
        memory_power_shift[0],
        prior_normed_lines[0],
    )
    weights = (
        attention_maps[0],
        emission_coefficients[0],
        feature_addressing[0],
        feature_payload[0],
        feature_receptance[0],
    )
    rows, held = forward_first(
        place, begins, bottom_stack_feed.reshape(ROWS, WIDTH), small, weights
    )
    for t in range(1, sections):
        rows = lax.ppermute(rows, "section", [(t - 1, t)])
        given = weights if t == 1 else away[:1] if t == sections - 1 else ()
        rows, held, made = forward_next(t, sections - 1, place, begins, rows, held, given)
        away = made if t == 1 else away
    held, edges = held[:N_BASE], held[N_BASE:]
    grad, held = backward_call(
        sections - 1, place, begins, loss_sensitivity.reshape(ROWS, WIDTH), held, away[1:]
    )
    grad = lax.ppermute(grad, "section", [(sections - 1, sections - 2)])
    own = join_edges(edges[0], swapped(edges[1]))
    section, own = lax.optimization_barrier((place[0], own))
    held = transposed(sections - 1, (section, place[1]), held)
    blocks = (own,) + tuple(sent(own, k, True) for k in range(1, 4))
    for t in range(sections - 2, -1, -1):
        if t == sections - 3:
            x = mixes(place, blocks, vec, weights[2])
            begins, *x = lax.optimization_barrier((begins, *x))
        grad, held = backward_call(t, place, begins, grad, held)
        if t > 0:
            grad = lax.ppermute(grad, "section", [(t, t - 1)])
    entry_grad, *row_sets, state_grads, row_grads = held[N_BASE:]
    layer = held[N_CONSTS + N_WEIGHTS + 1]
    layer, entry_grad, *state_grads, row_grads = drained(
        layer, entry_grad, state_grads, row_grads
    )

    def half(second, after=None):
        keep, send = row_sets[2 * second : 2 * second + 2]
        if after is not None:
            send, *_ = lax.optimization_barrier((send, *after))
        pieces = join(keep, swapped(send))
        joined = pieces[0]
        pieces = (pieces[0],) + tuple(sent(pieces[k], k, True) for k in range(1, 4))
        shares = weight_grads(second, place, x[second], pieces)
        shares = (shares[0],) + tuple(sent(shares[k], k, False) for k in range(1, 4))
        parts = summed(second, shares)
        parts = (parts[0],) + tuple(sent(parts[k], k, True) for k in range(1, 4))
        kept, going, *payload = gathered(second, place, parts)
        return final(second, place, kept, swapped(going)), payload, joined

    (key,), (payload,), joined = half(False, x)
    (projection, out_weight, gate, vectors, decay, boost), _, _ = half(True, (joined, row_grads))
    return (
        layer.reshape(1, SEQS, LENGTH, WIDTH),
        entry_grad.reshape(1, SEQS, LENGTH, WIDTH),
        jnp.swapaxes(vectors, 0, 1),
        decay,
        boost,
        projection[None],
        out_weight[None],
        key[None],
        payload[None],
        gate[None],
        state_grads[0][None],
        state_grads[1][None],
        state_grads[2][None],
        row_grads[None],
    )


def solution(mesh):
    placed = (
        P("dp", None, None),
        P("dp", None, None),
        P("dp"),
        P("section", None, None),
        P("section", None),
        P("section", None),
        P("section", None, None, None),
        P("section", None, None),
        P("section", None, None),
        P("section", None, None),
        P("section", None, None),
        P("section", "dp", None),
        P("section", "dp", None),
        P("section", "dp", None),
        P("section", None, "dp", None),
    )
    return jax.shard_map(
        body,
        mesh=mesh,
        in_specs=placed,
        out_specs=(
            P("section", "dp", None, None),
            P("section", "dp", None, None),
            P("section", None, "dp"),
            P("section", "dp"),
            P("section", "dp"),
            P("section", None, "dp", None),
            P("section", "dp", None),
            P("section", "dp", None),
            P("section", "dp", None),
            P("section", "dp", None),
            P("section", "dp", None),
            P("section", "dp", None),
            P("section", "dp", None),
            P("section", None, "dp", None),
        ),
        check_vma=False,
    )
```

```python
import functools

import jax
import jax.numpy as jnp
from jax import lax
from jax.experimental import pallas as pl
from jax.experimental.pallas import tpu as pltpu
from jax.sharding import PartitionSpec as P

WIDTH = 1024
INNER = 4096
LENGTH = 64
SEQS = 2
ROWS = SEQS * LENGTH
GROUPS = WIDTH // 128
FRESH = -1e30
EPS = 1e-05
F32 = jnp.float32
BF16 = jnp.bfloat16

VM = pl.BlockSpec(memory_space=pltpu.VMEM)
HB = pl.BlockSpec(memory_space=pl.ANY)
SM = pl.BlockSpec(memory_space=pltpu.SMEM)
EDGE = ROWS + 16
QUARTER = 768
SHARES = (1024, 768)


HELD_LIMIT = 14
UNROLL = 4
WINDOW = 4
FLOPS = 10**9
BACK_COST = (14, 1, 14, 14)


def limit(mebibytes):
    return pltpu.CompilerParams(vmem_limit_bytes=mebibytes * 1024 * 1024)

EMISSION, RECEPTANCE = 3, 4
BLOCKS = (5, 4, 4)
WEIGHTS = tuple(((n, WIDTH, WIDTH), BF16) for n in BLOCKS)
CONSTS = (
    ((9, 1, WIDTH), F32),
    ((1, WIDTH), F32),
    ((1, WIDTH), F32),
    ((SEQS, WIDTH), F32),
    ((SEQS, WIDTH), F32),
    ((SEQS, WIDTH), F32),
    ((2, SEQS, WIDTH), BF16),
)
SAVED = (
    ((ROWS, WIDTH), BF16),
    ((ROWS, WIDTH), BF16),
    ((ROWS, INNER), BF16),
    ((5, ROWS, WIDTH), F32),
    ((8, ROWS * GROUPS, 128), F32),
)
EDGES = (
    ((EDGE, 2 * WIDTH), BF16),
    ((EDGE, 2 * WIDTH), BF16),
)
GRADS = (
    ((ROWS, WIDTH), BF16),
    ((4, ROWS, QUARTER), BF16),
    ((4, ROWS, QUARTER), BF16),
    ((4, ROWS, QUARTER), BF16),
    ((4, ROWS, QUARTER), BF16),
    ((3, SEQS, WIDTH), F32),
    ((2, SEQS, WIDTH), F32),
)
N_CONSTS, N_WEIGHTS, N_SAVED, N_EDGES, N_GRADS = 7, 3, 5, 2, 7
N_BASE = N_CONSTS + N_WEIGHTS + N_SAVED


def dot(left, right):
    return jnp.dot(left, right, preferred_element_type=F32)


def against(grad, weight):
    return lax.dot_general(
        grad, weight, (((1,), (1,)), ((), ())), preferred_element_type=F32
    )


def across(left, right):
    return lax.dot_general(
        left, right, (((0,), (0,)), ((), ())), preferred_element_type=F32
    )


def columns_loop(total, size):
    def run(function):
        if total // size <= UNROLL:
            for j in range(total // size):
                function(pl.ds(j * size, size))
            return

        @pl.loop(0, total // size)
        def _(j):
            function(pl.ds(pl.multiple_of(j * size, size), size))

    return run


def coordinates(section, dp):
    dp = dp[0]
    return section[0], dp >> 3, (dp >> 1) & 3, dp & 1


def row_index():
    return lax.broadcasted_iota(jnp.int32, (ROWS, WIDTH), 0)


def normed_rows(rows):
    center = jnp.mean(rows, axis=-1, keepdims=True)
    centered = rows - center
    variance = jnp.mean(centered * centered, axis=-1, keepdims=True)
    scale = lax.rsqrt(variance + EPS)
    return centered * scale, scale


def moved_down(normed, first):
    index = row_index()
    return jnp.where(
        index == 0,
        first[0],
        jnp.where(index == LENGTH, first[1], pltpu.roll(normed, 1, 0)),
    )


def moved_up(rows):
    index = row_index()
    return jnp.where(
        (index == LENGTH - 1) | (index == ROWS - 1),
        0.0,
        pltpu.roll(rows, ROWS - 1, 0),
    )


def first_rows(prior_ref, mix, marks):
    return [prior_ref[mix, s : s + 1, :].astype(F32) * marks[s] for s in range(SEQS)]


def edge_rows(first):
    index = lax.broadcasted_iota(jnp.int32, (EDGE - ROWS, WIDTH), 0)
    return jnp.where(index == 0, first[0], jnp.where(index == 1, first[1], 0.0)).astype(BF16)


def store_sets(core, keep_ref, send_ref, pieces):
    for this in range(2):

        @pl.when(core == this)
        def _(this=this):
            for which, at, value in pieces:
                (keep_ref if which == this else send_ref)[at] = value()


def to_tokens(ref, block, value):
    ref[pl.ds(block, ROWS, stride=GROUPS), :] = value


def from_tokens(ref, block):
    return ref[pl.ds(block, ROWS, stride=GROUPS), :]


def tile_of(ref, row, small):
    for g in range(GROUPS):
        small[g : g + 1, :] = ref[row : row + 1, g * 128 : (g + 1) * 128]
    return small[...]


def forward_body(
    core, marks, x_ref, consts, weights, ready, out_ref, saved, edges, scratch, square_done=None
):
    streamed = x_ref is None
    vec_ref, fade_ref, boost_ref, num_ref, den_ref, lev_ref, prior_ref = consts
    square, keys, payload = weights
    ent_ref, lay_ref, act_ref, wide_ref, scan_ref = saved
    own_ref, other_ref = edges
    sk, sv, sy, small, mix_ref, hid_ref = scratch
    low, high = slice(0, WIDTH), slice(WIDTH, 2 * WIDTH)
    top, bottom = slice(0, ROWS), slice(ROWS, EDGE)
    if x_ref is not None:
        ent_ref[...] = x_ref[...]
    rows = ent_ref[...].astype(F32)
    unit, _ = normed_rows(rows)
    normed = unit * vec_ref[0] + vec_ref[1]
    first = first_rows(prior_ref, 0, marks)
    below = moved_down(normed, first)
    for j in range(3):
        v = vec_ref[2 + j]
        mix_ref[j] = (normed * v + below * (1.0 - v)).astype(BF16)
    mix_ref[3] = normed.astype(BF16)
    first_one = first
    for target, j in ((sk, 0), (sv, 1)):
        ready(j)

        @columns_loop(WIDTH, 512)
        def _(at, j=j):
            wide_ref[3, :, at] = dot(mix_ref[j], square[j, :, at])

        for g in range(GROUPS):
            to_tokens(target, g, wide_ref[3, :, g * 128 : (g + 1) * 128])
    ready(2)

    @columns_loop(WIDTH, 512)
    def _(at):
        wide_ref[0, :, at] = jax.nn.sigmoid(dot(mix_ref[2], square[2, :, at]))

    rate = jnp.exp(tile_of(fade_ref, 0, small))
    boost = tile_of(boost_ref, 0, small)
    start = []
    for s in range(SEQS):
        level = tile_of(lev_ref, s, small)
        start.append(jnp.where(marks[s] > 0.0, level, FRESH))
        start.append(tile_of(num_ref, s, small) * marks[s])
        start.append(tile_of(den_ref, s, small) * marks[s])

    def token(t, carry):
        carry_next = []
        for s in range(SEQS):
            level, num, den = carry[3 * s : 3 * s + 3]
            at = pl.ds(pl.multiple_of((t + LENGTH * s) * GROUPS, GROUPS), GROUPS)
            key, value = sk[at, :], sv[at, :]
            boosted = boost + key
            decayed = jnp.exp(-jnp.abs(level - boosted))
            state_on_top = level > boosted
            old = jnp.where(state_on_top, 1.0, decayed)
            fresh = jnp.where(state_on_top, decayed, 1.0)
            inverse = 1.0 / (old * den + fresh)
            old = old * inverse
            fresh = fresh * inverse
            result = old * num + fresh * value
            faded = level - rate
            level = jnp.maximum(faded, key)
            decayed = jnp.exp(-jnp.abs(faded - key))
            state_on_top = faded > key
            keep = jnp.where(state_on_top, 1.0, decayed)
            new = jnp.where(state_on_top, decayed, 1.0)
            sy[at, :] = result
            scan_ref[0, at, :] = old
            scan_ref[1, at, :] = fresh
            scan_ref[2, at, :] = value - result
            scan_ref[3, at, :] = keep
            scan_ref[4, at, :] = new
            scan_ref[5, at, :] = num
            scan_ref[6, at, :] = den
            scan_ref[7, at, :] = value
            carry_next += [level, keep * num + new * value, keep * den + new]
        return tuple(carry_next)

    def tokens(block, carry):
        for j in range(8):
            carry = token(block * 8 + j, carry)
        return carry

    lax.fori_loop(0, LENGTH // 8, tokens, tuple(start))
    for g in range(GROUPS):
        at = slice(g * 128, (g + 1) * 128)
        gate = wide_ref[0, :, at]
        mixed = gate * from_tokens(sy, g)
        mix_ref[0, :, at] = mixed.astype(BF16)
        wide_ref[1, :, at] = mixed * (1.0 - gate)
    store_sets(
        core, own_ref, other_ref,
        (
            (0, (top, high), lambda: mix_ref[3]),
            (0, (bottom, high), lambda: edge_rows(first_one)),
            (1, (top, high), lambda: mix_ref[0]),
        ),
    )
    ready(3)

    @columns_loop(WIDTH, 512)
    def _(at):
        wide_ref[2, :, at] = ent_ref[:, at].astype(F32) + dot(mix_ref[0], square[EMISSION, :, at])

    unit, _ = normed_rows(wide_ref[2])
    normed = unit * vec_ref[5] + vec_ref[6]
    first = first_rows(prior_ref, 1, marks)
    below = moved_down(normed, first)
    for j in range(2):
        v = vec_ref[7 + j]
        mix_ref[1 + j] = (normed * v + below * (1.0 - v)).astype(BF16)
    for ref in edges:
        ref[top, low] = normed.astype(BF16)
        ref[bottom, low] = edge_rows(first)
    ready(4)

    @columns_loop(WIDTH, 512)
    def _(at):
        wide_ref[4, :, at] = jax.nn.sigmoid(dot(mix_ref[2], square[RECEPTANCE, :, at]))

    if square_done is not None:
        square_done()

    def hidden(j):
        at = pl.ds(pl.multiple_of(j * 512, 512), 512)
        within = pl.ds(pl.multiple_of((j & 1) * 512, 512), 512)
        active = jnp.maximum(dot(mix_ref[1], keys[j >> 1, :, within]), 0.0)
        act_ref[:, at] = active.astype(BF16)
        hid_ref[:, at] = (active * active).astype(BF16)

    def leave(at, channel):
        wide_ref[3, :, at] = channel
        lay_ref[:, at] = (wide_ref[2, :, at] + wide_ref[4, :, at] * channel).astype(BF16)

    def part(b, at):
        return dot(hid_ref[:, b * WIDTH : (b + 1) * WIDTH], payload[b, :, at])

    if not streamed:
        pl.loop(0, INNER // 512)(hidden)

        @columns_loop(WIDTH, 256)
        def _(at):
            leave(at, part(0, at) + part(1, at) + part(2, at) + part(3, at))

    else:
        for b in range(4):
            ready(5 + b)
            pl.loop(2 * b, 2 * b + 2)(hidden)
        for b in range(4):
            ready(9 + b)

            @columns_loop(WIDTH, 512)
            def _(at, b=b):
                channel = part(b, at)
                if b > 0:
                    channel = channel + wide_ref[3, :, at]
                if b < 3:
                    wide_ref[3, :, at] = channel
                else:
                    leave(at, channel)

    out_ref[...] = lay_ref[...]


def groups(refs, *sizes):
    cut, at = [], 0
    for size in sizes:
        cut.append(refs[at : at + size])
        at += size
    return cut + [refs[at:]]


def weight_pieces(maps, emission, key, payload, receptance):
    pieces = [maps.at[j] for j in range(3)] + [emission, receptance]
    for b in range(4):
        pieces.append(key.at[:, pl.ds(b * WIDTH, WIDTH)])
    for b in range(4):
        pieces.append(payload.at[pl.ds(b * WIDTH, WIDTH), :])
    return pieces


def forward_first_kernel(section, dp, begins, x_ref, *refs):
    small_in, hbm, (out_ref,), consts, kept, saved, edges, rest = groups(
        refs, N_CONSTS, 5, 1, N_CONSTS, N_WEIGHTS, N_SAVED, N_EDGES
    )
    section, _, _, core = coordinates(section, dp)
    sem, small_sem = rest[-2:]
    copies = [
        pltpu.make_async_copy(source, target, sem.at[i])
        for i, (source, target) in enumerate(
            zip(
                weight_pieces(*hbm),
                [ref.at[i] for ref, n in zip(kept, BLOCKS) for i in range(n)],
            )
        )
    ]
    arriving = [pltpu.make_async_copy(x_ref, saved[0], small_sem.at[N_CONSTS])]
    for i in range(N_CONSTS):
        arriving.append(pltpu.make_async_copy(small_in[i], consts[i], small_sem.at[i]))
    for c in arriving + copies[:WINDOW]:
        c.start()
    for c in arriving:
        c.wait()

    def ready(i):
        copies[i].wait()
        if i + WINDOW < len(copies):
            copies[i + WINDOW].start()

    @pl.when(section == 0)
    def _():
        marks = [begins[s].astype(F32) for s in range(SEQS)]
        forward_body(
            core, marks, None, consts, kept, ready, out_ref, saved, edges, rest[:-2]
        )

    @pl.when(section != 0)
    def _():
        for c in copies[WINDOW:]:
            c.start()
        for c in copies:
            c.wait()


def flip(ref):
    side = 256
    for i in range(WIDTH // side):
        for j in range(i + 1):
            one = (slice(i * side, (i + 1) * side), slice(j * side, (j + 1) * side))
            two = (one[1], one[0])
            first = ref[one].T
            if i != j:
                ref[one] = ref[two].T
            ref[two] = first


def flip_slowly(ref):
    side = 256

    @pl.loop(0, 10)
    def _(pair):
        i = jnp.int32(pair >= 1) + jnp.int32(pair >= 3) + jnp.int32(pair >= 6)
        j = pair - ((i * (i + 1)) >> 1)
        row, column = (pl.ds(pl.multiple_of(t * side, side), side) for t in (i, j))
        first, second = ref[row, column].T, ref[column, row].T
        ref[row, column] = second
        ref[column, row] = first


def forward_kernel(layer, last, section, dp, begins, x_ref, *refs):
    early, own = layer == 1, layer == last
    _, given, (out_ref,), consts, kept, saved, edges, kept_away, rest = groups(
        refs,
        N_BASE + N_EDGES,
        5 if early else 1 if own else 0,
        1, N_CONSTS, N_WEIGHTS, N_SAVED, N_EDGES,
        2 if early else 0,
    )
    scratch, sem = (rest[:-1], rest[-1]) if early or own else (rest, None)
    section, _, _, core = coordinates(section, dp)

    @pl.when(section == layer)
    def _():
        marks = [begins[s].astype(F32) for s in range(SEQS)]
        square = pltpu.make_async_copy(given[0], kept[0], sem.at[0]) if own else None
        forward_body(
            core, marks, x_ref, consts, kept, lambda i: None, out_ref, saved, edges, scratch,
            square.start if own else None,
        )
        if own:
            square.wait()

    if early:

        @pl.when(section == last)
        def _():
            for ref, n in zip(kept[:2], BLOCKS):

                @pl.loop(0, n)
                def _(i, ref=ref):
                    flip_slowly(ref.at[i])

            away = [
                pltpu.make_async_copy(kept[i], kept_away[i], sem.at[i]) for i in range(2)
            ]
            for c in away:
                c.start()
            for c in away:
                c.wait()
            targets = [ref.at[i] for ref, n in zip(kept[:2], BLOCKS) for i in range(n)]
            back = [
                pltpu.make_async_copy(source, target, sem.at[i])
                for i, (source, target) in enumerate(zip(weight_pieces(*given), targets))
            ]
            for c in back:
                c.start()
            for c in back:
                c.wait()


def norm_back(rows, gain, offset, first, parts, vec_out, prior_out, marks):
    unit, scale = normed_rows(rows)
    normed = unit * gain + offset
    change = normed - moved_down(normed, first)
    up, stay = None, None
    for grad, weight, row in parts:
        vec_out(row, jnp.sum(grad * change, axis=0, keepdims=True))
        kept = grad * weight
        passed = grad - kept
        stay = kept if stay is None else stay + kept
        up = passed if up is None else up + passed
    for s in range(SEQS):
        prior_out(s, up[s * LENGTH : s * LENGTH + 1, :] * marks[s])
    grad = stay + moved_up(up)
    return unit, scale, grad


def backward_kernel(first, layer, section, dp, begins, dy_ref, *refs):
    _, given, (out_ref,), consts, kept, saved, grads, scratch = groups(
        refs,
        N_BASE + (0 if first else N_GRADS),
        1 if first else 0,
        1, N_CONSTS, N_WEIGHTS, N_SAVED, N_GRADS,
    )
    vec_ref, fade_ref, prior_ref = consts[0], consts[1], consts[6]
    square, keys, payload = kept
    ent_ref, lay_ref, act_ref, wide_ref, scan_ref = saved
    ing_ref, keep_one, send_one, keep_two, send_two, stg_ref, rowg_ref = grads
    sg, sdk, sdv, small, wide, wide_two, wide_three, wide_four, dys_ref, dhp_ref, vecg_ref = scratch[:11]
    section, y, z, core = coordinates(section, dp)
    def vec_out(row, value):
        vecg_ref[row : row + 1, :] = value

    def store(keep_ref, send_ref, items, shared=None):
        for this in range(2):

            @pl.when(core == this)
            def _(this=this):
                @pl.loop(0, 4)
                def _(q):
                    for which, column, size, value in items:
                        ref = keep_ref if which == this else send_ref
                        distance = (q - (y if which else z)) & 3
                        ref[distance, :, column : column + size] = value(q)
                    if shared is not None:
                        ref = keep_ref if this == 1 else send_ref
                        ref[q, 0:64, 512:768] = shared

    def quarter(row):
        return lambda q: dys_ref[row, :, pl.ds(pl.multiple_of(q * 256, 256), 256)]

    def pull(grad, blocks, i, at):
        if first and blocks is payload:
            return against(grad, blocks[i, at, :])
        return dot(grad, blocks[i, :, at])

    def through_payload(grad, j):
        return pull(grad, payload, j >> 1, pl.ds(pl.multiple_of((j & 1) * 512, 512), 512))

    def through_key(grad_ref, j):
        at = pl.ds(pl.multiple_of(j * 256, 256), 256)
        total = None
        for b in range(4):
            part = pull(grad_ref[:, b * WIDTH : (b + 1) * WIDTH], keys, b, at)
            total = part if total is None else total + part
        return total

    @pl.when(section == layer)
    def _():
        marks = [begins[s].astype(F32) for s in range(SEQS)]
        if first:
            key_copy = pltpu.make_async_copy(given[0], keys, scratch[11].at[0])
            key_copy.start()
        dy = dy_ref[...].astype(F32)
        gate = wide_ref[4]
        through = dy * gate
        dys_ref[4] = through.astype(BF16)
        dys_ref[5] = (through * wide_ref[3] * (1.0 - gate)).astype(BF16)

        @pl.loop(0, INNER // 512, unroll=4)
        def _(j):
            at = pl.ds(pl.multiple_of(j * 512, 512), 512)
            part = through_payload(dys_ref[4], j)
            dhp_ref[:, at] = (2.0 * act_ref[:, at].astype(F32) * part).astype(BF16)

        def hidden(start):
            return lambda q: dhp_ref[:, pl.ds(pl.multiple_of(start + q * 512, 512), 512)]

        store(
            keep_one, send_one,
            ((0, 0, 512, hidden(0)), (1, 0, 512, hidden(2048)),
             (0, 512, 256, quarter(4)), (1, 512, 256, quarter(4))),
        )

        if first:
            key_copy.wait()

        @pl.loop(0, WIDTH // 256, unroll=2)
        def _(j):
            at = pl.ds(pl.multiple_of(j * 256, 256), 256)
            wide[:, at] = through_key(dhp_ref, j)
            wide_two[:, at] = pull(dys_ref[5], square, RECEPTANCE, at)

        def prior_two(s, value):
            rowg_ref[1, s : s + 1, :] = value

        gain = vec_ref[5]
        unit, scale, grad = norm_back(
            wide_ref[2], gain, vec_ref[6], first_rows(prior_ref, 1, marks),
            ((wide[...], vec_ref[7], 7), (wide_two[...], vec_ref[8], 8)),
            vec_out, prior_two, marks,
        )
        vec_out(5, jnp.sum(grad * unit, axis=0, keepdims=True))
        vec_out(6, jnp.sum(grad, axis=0, keepdims=True))
        grad = grad * gain
        mean = jnp.mean(grad, axis=-1, keepdims=True)
        along = jnp.mean(grad * unit, axis=-1, keepdims=True)
        middle = dy_ref[...].astype(F32) + scale * (grad - mean - unit * along)
        wide_three[...] = middle
        dys_ref[3] = middle.astype(BF16)

        for q in range(4):
            at = pl.ds(q * 256, 256)
            part = pull(dys_ref[3], square, EMISSION, at)
            dys_ref[2, :, at] = (part * wide_ref[1, :, at]).astype(BF16)
            wide[:, at] = part * wide_ref[0, :, at]

        for g in range(GROUPS):
            to_tokens(sg, g, wide[:, g * 128 : (g + 1) * 128])

        zero = jnp.zeros((GROUPS, 128), F32)

        def token(t, carry):
            carry_next = []
            boosted, faded = carry[4], carry[5]
            for s in range(SEQS):
                dnum, dden = carry[2 * s : 2 * s + 2]
                at = pl.ds(pl.multiple_of((t + LENGTH * s) * GROUPS, GROUPS), GROUPS)
                g = sg[at, :]
                value = scan_ref[7, at, :]
                beyond = scan_ref[2, at, :]
                keep = scan_ref[3, at, :]
                new = scan_ref[4, at, :]
                from_old = scan_ref[0, at, :] * g
                from_new = scan_ref[1, at, :] * g
                direct = from_new * beyond
                boosted = boosted + direct
                sdv[at, :] = from_new + new * dnum
                sdk[at, :] = direct + new * (dnum * value + dden)
                faded = faded - keep * (dnum * scan_ref[5, at, :] + dden * scan_ref[6, at, :])
                carry_next += [
                    from_old + keep * dnum,
                    keep * dden - from_old * (value - beyond),
                ]
            return tuple(carry_next) + (boosted, faded)

        def tokens(block, carry):
            for j in range(8):
                carry = token(LENGTH - 1 - block * 8 - j, carry)
            return carry

        ends = lax.fori_loop(0, LENGTH // 8, tokens, (zero,) * 6)

        def spread(put_piece, value):
            small[...] = value
            for g in range(GROUPS):
                put_piece(slice(g * 128, (g + 1) * 128), small[g : g + 1, :])

        for s in range(SEQS):
            dnum, dden = ends[2 * s : 2 * s + 2]
            at = pl.ds(LENGTH * s * GROUPS, GROUPS)
            moved = dnum * scan_ref[5, at, :] + dden * scan_ref[6, at, :]
            for k, value in enumerate((dnum, dden, moved)):

                def put_state(cols, piece, k=k, s=s):
                    stg_ref[k, s : s + 1, cols] = piece

                spread(put_state, value * marks[s])

        def put_decay(cols, piece):
            vecg_ref[9:10, cols] = piece

        def put_boost(cols, piece):
            vecg_ref[10:11, cols] = piece

        spread(put_decay, ends[5])
        vecg_ref[9:10, :] = vecg_ref[9:10, :] * jnp.exp(fade_ref[0:1, :])
        spread(put_boost, ends[4])

        for g in range(GROUPS):
            at = slice(g * 128, (g + 1) * 128)
            dys_ref[0, :, at] = from_tokens(sdk, g).astype(BF16)
            dys_ref[1, :, at] = from_tokens(sdv, g).astype(BF16)
        rows = ent_ref[...].astype(F32)
        pulled = (wide, wide_two, wide_four)
        for j in range(3):

            @columns_loop(WIDTH, 512)
            def _(at, j=j):
                pulled[j][:, at] = pull(dys_ref[j], square, j, at)


        def prior_one(s, value):
            rowg_ref[0, s : s + 1, :] = value

        gain = vec_ref[0]
        unit, scale, grad = norm_back(
            rows, gain, vec_ref[1], first_rows(prior_ref, 0, marks),
            [(pulled[j][...], vec_ref[2 + j], 2 + j) for j in range(3)],
            vec_out, prior_one, marks,
        )
        vec_out(0, jnp.sum(grad * unit, axis=0, keepdims=True))
        vec_out(1, jnp.sum(grad, axis=0, keepdims=True))
        packed = jnp.concatenate(
            [vecg_ref[:, b * 256 : (b + 1) * 256] for b in range(4)], axis=0
        ).astype(BF16)
        store(
            keep_two, send_two,
            ((0, 0, 256, quarter(0)), (0, 256, 256, quarter(1)), (0, 512, 256, quarter(2)),
             (1, 0, 256, quarter(5)), (1, 256, 256, quarter(3))),
            packed,
        )
        grad = grad * gain
        mean = jnp.mean(grad, axis=-1, keepdims=True)
        along = jnp.mean(grad * unit, axis=-1, keepdims=True)
        entry = (wide_three[...] + scale * (grad - mean - unit * along)).astype(BF16)
        ing_ref[...] = entry
        out_ref[...] = entry


def transpose_kernel(last, section, dp, *refs):
    @pl.when(section[0] != last)
    def _():
        for ref, n in zip(refs[N_WEIGHTS:], BLOCKS):

            @pl.loop(0, n, unroll=4 if n == 4 else 1)
            def _(i, ref=ref):
                flip(ref.at[i])


def join_edges_kernel(first, second, out, sem):
    copies = [
        pltpu.make_async_copy(ref, out.at[pl.ds(h * EDGE, EDGE), :], sem.at[h])
        for h, ref in enumerate((first, second))
    ]
    for c in copies:
        c.start()
    for c in copies:
        c.wait()


def join_kernel(first, second, *outs):
    for k in range(4):
        outs[k][:ROWS, :] = first[k]
        outs[k][ROWS:, :] = second[k]


def mixes_kernel(section, dp, own, one, two, three, vec_ref, wa, *refs):
    x_one, x_two, edge, wide, stage, hidden, first_mix, edge_sem, wide_sem, out_sem = refs
    core = coordinates(section, dp)[3]
    blocks = (own, one, two, three)
    pair = 2 * ROWS

    def load(k):
        for i, block in enumerate(blocks):

            @pl.when(k == i)
            def _(block=block):
                pltpu.make_async_copy(block, edge.at[k & 1], edge_sem.at[k & 1]).start()

    columns = [
        pltpu.make_async_copy(
            wa.at[:, pl.ds(pl.multiple_of((2 * j + core) * 128, 128), 128)],
            wide.at[:, pl.ds(j * 128, 128)],
            wide_sem.at[j],
        )
        for j in range(16)
    ]

    def outs(k):
        rows = pl.ds(pl.multiple_of(k * pair, pair), pair)
        slot = k & 1
        return (
            pltpu.make_async_copy(first_mix.at[slot], x_one.at[2, rows, :], out_sem.at[slot, 0]),
            pltpu.make_async_copy(stage.at[slot], x_two.at[:, rows, :], out_sem.at[slot, 1]),
        )

    def out_hidden(k, u):
        rows = pl.ds(pl.multiple_of(k * pair, pair), pair)
        return pltpu.make_async_copy(hidden.at[u], x_one.at[u, rows, :], out_sem.at[u, 2])

    def mix(normed, below, j):
        v = vec_ref[j]
        return (normed * v + below * (1.0 - v)).astype(BF16)

    load(jnp.int32(0))
    for c in columns:
        c.start()

    @pl.loop(0, 4)
    def _(k):
        slot = k & 1

        @pl.when(k < 3)
        def _():
            load(k + 1)

        pltpu.make_async_copy(own, edge.at[slot], edge_sem.at[slot]).wait()

        @pl.when(k >= 2)
        def _():
            for c in outs(k - 2):
                c.wait()

        @pl.loop(0, 2)
        def _(h):
            start = pl.multiple_of(h * EDGE, 16)
            at = pl.ds(pl.multiple_of(h * ROWS, ROWS), ROWS)

            def parts(c):
                cols = slice(c * WIDTH, (c + 1) * WIDTH)
                normed = edge[slot, pl.ds(start, ROWS), cols].astype(F32)
                first = edge[slot, pl.ds(pl.multiple_of(start + ROWS, 16), 16), cols].astype(F32)
                return normed, moved_down(normed, (first[0:1, :], first[1:2, :]))

            normed, below = parts(0)
            first_mix[slot, at, :] = mix(normed, below, 7)

            @pl.when(core == 0)
            def _():
                normed, below = parts(1)
                for j in range(3):
                    stage[slot, j, at, :] = mix(normed, below, 2 + j)

            @pl.when(core == 1)
            def _():
                stage[slot, 0, at, :] = mix(normed, below, 8)
                stage[slot, 1, at, :] = edge[slot, pl.ds(start, ROWS), WIDTH:]

        for c in outs(k):
            c.start()

        @pl.when(k == 0)
        def _():
            for c in columns:
                c.wait()

        for u in range(2):

            @pl.when(k >= 1)
            def _(u=u):
                out_hidden(k - 1, u).wait()

            @pl.loop(0, 2)
            def _(j, u=u):
                for half in range(2):
                    at = pl.ds(pl.multiple_of(j * 512 + half * 256, 256), 256)
                    wide_at = pl.ds(pl.multiple_of(u * WIDTH + j * 512 + half * 256, 256), 256)
                    active = jnp.maximum(dot(first_mix[slot], wide[:, wide_at]), 0.0)
                    hidden[u, :, at] = (active * active).astype(BF16)

            out_hidden(k, u).start()

    for k in (2, 3):
        for c in outs(k):
            c.wait()
    for u in range(2):
        out_hidden(3, u).wait()


def drain_kernel(layer, entry, states, firsts, *refs):
    results, sem = refs[:-1], refs[-1]
    sources = (layer, entry) + tuple(states.at[k] for k in range(3)) + (firsts,)
    copies = [
        pltpu.make_async_copy(source, target, sem.at[i])
        for i, (source, target) in enumerate(zip(sources, results))
    ]
    for c in copies:
        c.start()
    for c in copies:
        c.wait()


def row_starts(y, z, core):
    starts = []
    for there in range(16):
        along_y, along_z = (there // 4 - y) & 3, (there % 4 - z) & 3
        summed = jnp.where(core == 0, along_y, along_z)
        joined = jnp.where(core == 0, along_z, along_y)
        starts.append(pl.multiple_of(summed * 256 + joined * 64, 64))
    return starts


def weight_kernel(second, section, dp, x_ref, *refs):
    blocks, outs = refs[:4], refs[4:8]
    dy, share = refs[8:]
    _, y, z, core = coordinates(section, dp)
    for k in range(4):
        dy[k * 2 * ROWS : (k + 1) * 2 * ROWS, :] = blocks[k][...]
    starts = row_starts(y, z, core)

    def unit(u, size, source, target):
        for c in range(0, WIDTH, 256):
            part = across(x_ref[u, :, c : c + 256], dy[:, source : source + size]).astype(BF16)
            for b in range(4):
                share[pl.ds(starts[c // 64 + b], 64), target : target + size] = part[
                    b * 64 : (b + 1) * 64, :
                ]

    if not second:
        unit(2, 512, 0, 0)
        for u in range(2):
            for c in range(0, WIDTH, 256):
                part = across(x_ref[u, :, c : c + 256], dy[:, 512:768]).astype(BF16)
                for b in range(2):
                    start = starts[(u * WIDTH + c) // 128 + b]
                    for half in range(2):
                        share[pl.ds(start, 64), 512 + half * 256 : 768 + half * 256] = part[
                            b * 128 + half * 64 : b * 128 + (half + 1) * 64, :
                        ]
    else:
        unit(0, 256, 0, 0)
        unit(1, 256, 256, 256)

        @pl.when(core == 0)
        def _():
            unit(2, 256, 512, 512)

        @pl.when(core == 1)
        def _():
            total = jnp.zeros((64, 256), F32)
            for d in range(8):
                total = total + dy[d * ROWS : d * ROWS + 64, 512:768].astype(F32)
            for b in range(4):
                piece = jnp.concatenate(
                    [total[b * 16 : (b + 1) * 16, :], jnp.zeros((112, 256), F32)], axis=0
                ).T.astype(BF16)
                for e in range(4):
                    at = pl.ds(starts[b * 4 + e], 64)
                    share[at, 512:640] = piece[e * 64 : (e + 1) * 64, :]
                    share[at, 640:768] = jnp.zeros((64, 128), BF16)

    for k in range(4):
        outs[k][...] = share[k * 256 : (k + 1) * 256, :]


def sum_kernel(own, one, two, three, *outs):
    for k in range(4):

        @pl.loop(0, 4)
        def _(i, k=k):
            at = pl.ds(pl.multiple_of(k * 64 + i * 16, 16), 16)
            total = own[at, :].astype(F32) + one[at, :].astype(F32) + two[at, :].astype(F32)
            total = total + three[at, :].astype(F32)
            outs[k][pl.ds(pl.multiple_of(i * 16, 16), 16), :] = total.astype(BF16)


def gather_kernel(second, section, dp, own, one, two, three, keep_ref, send_ref, *payload):
    _, y, z, core = coordinates(section, dp)
    here = jnp.where(core == 0, z, y)
    mine = pl.multiple_of(core * 32, 32)
    theirs = pl.multiple_of(32 - core * 32, 32)
    for k, ref in enumerate((own, one, two, three)):
        quarter = (here - k) & 3
        for rows, target in ((mine, keep_ref), (theirs, send_ref)):
            if not second:
                at = pl.ds(pl.multiple_of(quarter * 512, 512), 512)
                target[:, at] = ref[pl.ds(rows, 32), 0:512]
            else:
                for u in range(3):
                    at = pl.ds(pl.multiple_of(u * WIDTH + quarter * 256, 256), 256)
                    target[:, at] = ref[pl.ds(rows, 32), u * 256 : (u + 1) * 256]
        if not second:
            at = pl.ds(pl.multiple_of(quarter * 256, 256), 256)
            for half in range(2):
                payload[0][half * 64 : (half + 1) * 64, at] = ref[
                    :, 512 + half * 256 : 768 + half * 256
                ].astype(F32)


def final_kernel(second, section, dp, kept, come, *outs):
    core = coordinates(section, dp)[3]

    def write(set_zero, set_one):
        if not second:
            outs[0][:, 0:2048] = set_zero[...].astype(F32)
            outs[0][:, 2048:4096] = set_one[...].astype(F32)
            return
        proj_ref, out_ref, gate_ref, vec_ref, dec_ref, boo_ref = outs
        for u in range(3):
            proj_ref[u] = set_zero[:, u * WIDTH : (u + 1) * WIDTH].astype(F32)
        gate_ref[...] = set_one[:, 0:1024].astype(F32)
        out_ref[...] = set_one[:, 1024:2048].astype(F32)
        vectors = set_one[:, 2048:2176].astype(F32).T
        for j in range(9):
            vec_ref[j] = vectors[j : j + 1, :]
        dec_ref[...] = vectors[9:10, :]
        boo_ref[...] = vectors[10:11, :]

    @pl.when(core == 0)
    def _():
        write(kept, come)

    @pl.when(core == 1)
    def _():
        write(come, kept)


def plain(shapes):
    return tuple(jax.ShapeDtypeStruct(s, d) for s, d in shapes)


def in_vmem(shapes):
    return tuple(pltpu.VMEM(s, d) for s, d in shapes)


def hold(arrays):
    return tuple(pltpu.with_memory_space_constraint(a, pltpu.VMEM) for a in arrays)


def in_hbm(*arrays):
    return tuple(pltpu.with_memory_space_constraint(a, pltpu.HBM) for a in arrays)


def array(*shape, kind=BF16):
    return jax.ShapeDtypeStruct(shape, kind)


ROWS_OUT = array(ROWS, WIDTH)
TOKENS = pltpu.VMEM((ROWS * GROUPS, 128), F32)
SMALL = pltpu.VMEM((GROUPS, 128), F32)
WIDE = pltpu.VMEM((ROWS, WIDTH), F32)
FORWARD_SCRATCH = [
    TOKENS, TOKENS, TOKENS, SMALL,
    pltpu.VMEM((4, ROWS, WIDTH), BF16),
    pltpu.VMEM((ROWS, INNER), BF16),
]
DMA = pltpu.SemaphoreType.DMA


def forward_first(place, begins, rows, small, weights):
    shapes = CONSTS + WEIGHTS + SAVED + EDGES
    results = pl.pallas_call(
        forward_first_kernel,
        cost_estimate=cost(12),
        out_shape=(ROWS_OUT,) + in_vmem(shapes),
        in_specs=[SM] * 3 + [HB] * (1 + N_CONSTS + 5),
        out_specs=(VM,) * (1 + len(shapes)),
        scratch_shapes=FORWARD_SCRATCH + [DMA((13,)), DMA((N_CONSTS + 1,))],
        compiler_params=limit(HELD_LIMIT),
    )(*place, *in_hbm(begins, rows, *small, *weights))
    return results[0], results[1:]


def forward_next(layer, last, place, begins, rows, held, given=()):
    shapes = CONSTS + WEIGHTS + SAVED + EDGES
    away = tuple(pltpu.HBM(s, d) for s, d in WEIGHTS[:2]) if layer == 1 else ()
    results = pl.pallas_call(
        functools.partial(forward_kernel, layer, last),
        cost_estimate=cost(10),
        out_shape=(ROWS_OUT,) + plain(shapes) + away,
        in_specs=[SM] * 3 + [VM] * (1 + len(shapes)) + [HB] * len(given),
        out_specs=(VM,) * (1 + len(shapes)) + (HB,) * len(away),
        input_output_aliases={4 + i: 1 + i for i in range(len(shapes))},
        scratch_shapes=FORWARD_SCRATCH + ([DMA((9,))] if given else []),
        compiler_params=limit(HELD_LIMIT),
    )(*place, begins, *hold((rows,)), *hold(held), *in_hbm(*given))
    return results[0], results[1 : 1 + len(shapes)], results[1 + len(shapes) :]


def backward_call(layer, place, begins, grad, held, given=()):
    first = len(held) == N_BASE
    base = CONSTS + WEIGHTS + SAVED
    results = pl.pallas_call(
        functools.partial(backward_kernel, first, layer),
        cost_estimate=cost(BACK_COST[layer]),
        out_shape=(ROWS_OUT,) + plain(base) + (in_vmem(GRADS) if first else plain(GRADS)),
        in_specs=[SM] * 3 + [VM] * (1 + len(held)) + [HB] * len(given),
        out_specs=(VM,) * (1 + N_BASE + N_GRADS),
        input_output_aliases={4 + i: 1 + i for i in range(len(held))},
        scratch_shapes=[
            TOKENS, TOKENS, TOKENS, SMALL, WIDE, WIDE, WIDE, WIDE,
            pltpu.VMEM((6, ROWS, WIDTH), BF16),
            pltpu.VMEM((ROWS, INNER), BF16),
            pltpu.VMEM((16, WIDTH), F32),
        ]
        + ([DMA((1,))] if given else []),
        compiler_params=limit(HELD_LIMIT),
    )(*place, begins, *hold((grad,)), *hold(held), *in_hbm(*given))
    return results[0], results[1:]


def cost(microseconds):
    return pl.CostEstimate(
        flops=int(microseconds * FLOPS), bytes_accessed=0, transcendentals=0
    )


def transposed(last, place, held):
    first, end = N_CONSTS, N_CONSTS + N_WEIGHTS
    weights = pl.pallas_call(
        functools.partial(transpose_kernel, last),
        cost_estimate=cost(9),
        out_shape=plain(WEIGHTS),
        in_specs=[SM] * 2 + [VM] * N_WEIGHTS,
        out_specs=(VM,) * N_WEIGHTS,
        input_output_aliases={2 + i: i for i in range(N_WEIGHTS)},
        compiler_params=limit(HELD_LIMIT),
    )(*place, *hold(held[first:end]))
    return tuple(held[:first]) + tuple(weights) + tuple(held[end:])


def join_edges(first, second):
    return pl.pallas_call(
        join_edges_kernel,
        cost_estimate=cost(3),
        out_shape=pltpu.HBM((2 * EDGE, 2 * WIDTH), BF16),
        in_specs=[VM, VM],
        out_specs=HB,
        scratch_shapes=[DMA((2,))],
        compiler_params=limit(1),
    )(*hold((first, second)))


def join(first, second):
    return pl.pallas_call(
        join_kernel,
        cost_estimate=cost(1),
        out_shape=in_vmem((((2 * ROWS, QUARTER), BF16),) * 4),
        in_specs=[VM, VM],
        out_specs=(VM,) * 4,
        compiler_params=limit(HELD_LIMIT),
    )(*hold((first, second)))


MIXES_SCRATCH = [
    pltpu.VMEM((2, 2 * EDGE, 2 * WIDTH), BF16),
    pltpu.VMEM((WIDTH, 2 * WIDTH), BF16),
    pltpu.VMEM((2, 3, 2 * ROWS, WIDTH), BF16),
    pltpu.VMEM((2, 2 * ROWS, WIDTH), BF16),
    pltpu.VMEM((2, 2 * ROWS, WIDTH), BF16),
    DMA((2,)),
    DMA((16,)),
    DMA((2, 3)),
]
X_HALF = pltpu.HBM((3, 8 * ROWS, WIDTH), BF16)


def mixes(place, blocks, vec, wa):
    return pl.pallas_call(
        mixes_kernel,
        cost_estimate=cost(15),
        out_shape=(X_HALF, X_HALF),
        in_specs=[SM] * 2 + [HB] * 4 + [VM, HB],
        out_specs=(HB, HB),
        scratch_shapes=MIXES_SCRATCH,
        compiler_params=limit(HELD_LIMIT),
    )(*place, *in_hbm(*blocks), vec, *in_hbm(wa))


def drained(layer, entry, states, firsts):
    rows, state = pltpu.HBM((ROWS, WIDTH), BF16), pltpu.HBM((SEQS, WIDTH), F32)
    return pl.pallas_call(
        drain_kernel,
        cost_estimate=cost(1),
        out_shape=(rows, rows, state, state, state, pltpu.HBM((2, SEQS, WIDTH), F32)),
        in_specs=[HB] * 4,
        out_specs=(HB,) * 6,
        scratch_shapes=[DMA((6,))],
        compiler_params=limit(1),
    )(layer, entry, states, firsts)


def weight_grads(second, place, x, blocks):
    columns = SHARES[second]
    return pl.pallas_call(
        functools.partial(weight_kernel, second),
        cost_estimate=cost(4),
        out_shape=in_vmem((((2 * ROWS, columns), BF16),) * 4),
        in_specs=[SM] * 2 + [VM] * 5,
        out_specs=(VM,) * 4,
        scratch_shapes=[
            pltpu.VMEM((8 * ROWS, QUARTER), BF16),
            pltpu.VMEM((8 * ROWS, columns), BF16),
        ],
        compiler_params=limit(HELD_LIMIT),
    )(*place, *hold((x, *blocks)))


def summed(second, shares):
    return pl.pallas_call(
        sum_kernel,
        cost_estimate=cost(1),
        out_shape=in_vmem((((64, SHARES[second]), BF16),) * 4),
        in_specs=[VM] * 4,
        out_specs=(VM,) * 4,
        compiler_params=limit(HELD_LIMIT),
    )(*hold(shares))


def gathered(second, place, parts):
    outs = in_vmem((((32, 3 * WIDTH), BF16),) * 2)
    if not second:
        outs = in_vmem((((32, 2 * WIDTH), BF16),) * 2) + (pltpu.HBM((ROWS, WIDTH), F32),)
    return pl.pallas_call(
        functools.partial(gather_kernel, second),
        cost_estimate=cost(1),
        out_shape=outs,
        in_specs=[SM] * 2 + [VM] * 4,
        out_specs=(VM,) * len(outs),
        compiler_params=limit(HELD_LIMIT),
    )(*place, *hold(parts))


def final(second, place, kept, come):
    outs = (
        array(3, 32, WIDTH, kind=F32),
        array(32, WIDTH, kind=F32),
        array(32, WIDTH, kind=F32),
        array(9, 1, 32, kind=F32),
        array(1, 32, kind=F32),
        array(1, 32, kind=F32),
    )
    if not second:
        outs = (array(32, INNER, kind=F32),)
    return pl.pallas_call(
        functools.partial(final_kernel, second),
        cost_estimate=cost(1),
        out_shape=outs,
        in_specs=[SM] * 2 + [VM] * 2,
        out_specs=(VM,) * len(outs),
        compiler_params=limit(HELD_LIMIT),
    )(*place, *hold((kept, come)))


def device(y, z, core):
    return (y * 4 + z) * 2 + core


def swapped(block):
    return lax.ppermute(block, "dp", [(d, d ^ 1) for d in range(32)])


def sent(block, distance, first_axis):
    route = []
    for y in range(4):
        for z in range(4):
            for core in range(2):
                if (core == 0) == first_axis:
                    there = device(y, (z + distance) % 4, core)
                else:
                    there = device((y + distance) % 4, z, core)
                route.append((device(y, z, core), there))
    return lax.ppermute(block, "dp", route)


def body(
    bottom_stack_feed,
    loss_sensitivity,
    resumes_segment,
    mixing_coefficients,
    fading_log,
    feature_boost,
    attention_maps,
    emission_coefficients,
    feature_addressing,
    feature_payload,
    feature_receptance,
    dividend_memory,
    divisor_memory,
    memory_power_shift,
    prior_normed_lines,
):
    sections = lax.axis_size("section")
    place = (lax.axis_index("section")[None], lax.axis_index("dp")[None])
    begins = resumes_segment
    vec = jnp.swapaxes(mixing_coefficients, 0, 1)
    small = (
        vec,
        fading_log,
        feature_boost,
        dividend_memory[0],
        divisor_memory[0],
        memory_power_shift[0],
        prior_normed_lines[0],
    )
    weights = (
        attention_maps[0],
        emission_coefficients[0],
        feature_addressing[0],
        feature_payload[0],
        feature_receptance[0],
    )
    rows, held = forward_first(
        place, begins, bottom_stack_feed.reshape(ROWS, WIDTH), small, weights
    )
    for t in range(1, sections):
        rows = lax.ppermute(rows, "section", [(t - 1, t)])
        given = weights if t == 1 else away[:1] if t == sections - 1 else ()
        rows, held, made = forward_next(t, sections - 1, place, begins, rows, held, given)
        away = made if t == 1 else away
    held, edges = held[:N_BASE], held[N_BASE:]
    grad, held = backward_call(
        sections - 1, place, begins, loss_sensitivity.reshape(ROWS, WIDTH), held, away[1:]
    )
    grad = lax.ppermute(grad, "section", [(sections - 1, sections - 2)])
    own = join_edges(edges[0], swapped(edges[1]))
    section, own = lax.optimization_barrier((place[0], own))
    held = transposed(sections - 1, (section, place[1]), held)
    blocks = (own,) + tuple(sent(own, k, True) for k in range(1, 4))
    for t in range(sections - 2, -1, -1):
        if t == sections - 3:
            x = mixes(place, blocks, vec, weights[2])
            begins, *x = lax.optimization_barrier((begins, *x))
        grad, held = backward_call(t, place, begins, grad, held)
        if t > 0:
            grad = lax.ppermute(grad, "section", [(t, t - 1)])
    entry_grad, *row_sets, state_grads, row_grads = held[N_BASE:]
    layer = held[N_CONSTS + N_WEIGHTS + 1]
    layer, entry_grad, *state_grads, row_grads = drained(
        layer, entry_grad, state_grads, row_grads
    )

    def half(second, after=None):
        keep, send = row_sets[2 * second : 2 * second + 2]
        if after is not None:
            send, *_ = lax.optimization_barrier((send, *after))
        pieces = join(keep, swapped(send))
        joined = pieces[0]
        pieces = (pieces[0],) + tuple(sent(pieces[k], k, True) for k in range(1, 4))
        shares = weight_grads(second, place, x[second], pieces)
        shares = (shares[0],) + tuple(sent(shares[k], k, False) for k in range(1, 4))
        parts = summed(second, shares)
        parts = (parts[0],) + tuple(sent(parts[k], k, True) for k in range(1, 4))
        kept, going, *payload = gathered(second, place, parts)
        return final(second, place, kept, swapped(going)), payload, joined

    (key,), (payload,), joined = half(False, x)
    (projection, out_weight, gate, vectors, decay, boost), _, _ = half(True, (joined, row_grads))
    return (
        layer.reshape(1, SEQS, LENGTH, WIDTH),
        entry_grad.reshape(1, SEQS, LENGTH, WIDTH),
        jnp.swapaxes(vectors, 0, 1),
        decay,
        boost,
        projection[None],
        out_weight[None],
        key[None],
        payload[None],
        gate[None],
        state_grads[0][None],
        state_grads[1][None],
        state_grads[2][None],
        row_grads[None],
    )


def solution(mesh):
    placed = (
        P("dp", None, None),
        P("dp", None, None),
        P("dp"),
        P("section", None, None),
        P("section", None),
        P("section", None),
        P("section", None, None, None),
        P("section", None, None),
        P("section", None, None),
        P("section", None, None),
        P("section", None, None),
        P("section", "dp", None),
        P("section", "dp", None),
        P("section", "dp", None),
        P("section", None, "dp", None),
    )
    return jax.shard_map(
        body,
        mesh=mesh,
        in_specs=placed,
        out_specs=(
            P("section", "dp", None, None),
            P("section", "dp", None, None),
            P("section", None, "dp"),
            P("section", "dp"),
            P("section", "dp"),
            P("section", None, "dp", None),
            P("section", "dp", None),
            P("section", "dp", None),
            P("section", "dp", None),
            P("section", "dp", None),
            P("section", "dp", None),
            P("section", "dp", None),
            P("section", "dp", None),
            P("section", None, "dp", None),
        ),
        check_vma=False,
    )
```
